256 devices in a mesh: gx: 16 (over y, x), gy: 16 (over z, core).
Axes of the slice: x: 4, y: 4, z: 8, core: 2. Of those that a mesh axis runs over, the one named last changes fastest.
Arguments:
- drawdown: float32 [16, 2048, 2048], P(None, 'gx', 'gy'), may hold values from -6 to 6
- step_ratio: float32 [16, 2048, 2048], P(None, 'gx', 'gy'), may hold values from 3000 to 30000
- layer_class: int32 [16, 2048, 2048], P(None, 'gx', 'gy'), may hold values from 0 to 7
- class_conductance: float32 [8], replicated, may hold values from 3 to 30
- leakance: float32 [15], replicated, may hold values from 0.0005 to 0.02
- well_mask: int32 [16, 2048, 2048], P(None, 'gx', 'gy'), may hold values from 0 to 1, as said below
- rate_index: int32 [2048, 2048], P('gx', 'gy'), may hold values from 0 to 15
- rate_table: float32 [16], replicated, may hold values from 1 to 10
- pit_mask: int32 [16, 2048, 2048], P(None, 'gx', 'gy'), may hold values from 0 to 1, as said below
- pit_level: float32 [16], replicated, may hold values from 1 to 3
Outputs:
- new_drawdown: float32 [16, 2048, 2048], P(None, 'gx', 'gy')
The draws below stay inside these ranges and needn't reach their ends.
Inputs may be any that keep to these rules, and one draw needn't show every extreme that they name: `pit_mask`: the pit is one box of cells: a rectangle in x and y over the layers from the top down to some depth above the bottom layer. `well_mask`: each well is a column of cells screened over one run of consecutive layers.
All inputs are finite; a program needn't handle non-finite values.
Results may differ from the reference program's by a relative error of at most 0.0023.
Values sent between devices are 32-bit elements; how exact they have to be, the bound alone decides.
A program may use at most 128 MiB of HBM per device.

```python
import math
import jax
import jax.numpy as jnp
from jax import lax

LAYERS = 16
CLASSES = 8
RATES = 16
NX = 2048
NY = 2048


def draw_drawdown(key, part):
    key = jax.random.fold_in(key, 11)
    shape = (LAYERS, NX, NY)
    return jnp.clip(jax.random.normal(key, shape, jnp.float32), -6.0, 6.0)


def draw_pit_mask(key, part):
    key = jax.random.fold_in(key, 23)
    keys = jax.random.split(key, 5)
    shape = (LAYERS, NX, NY)
    half_x = jax.random.randint(keys[0], (), max(NX // 32, 1), max(NX // 8, 2) + 1)
    half_y = jax.random.randint(keys[1], (), max(NY // 32, 1), max(NY // 8, 2) + 1)
    centre_x = jax.random.randint(keys[2], (), 0, NX)
    centre_y = jax.random.randint(keys[3], (), 0, NY)
    depth = jax.random.randint(keys[4], (), 1, LAYERS // 2 + 1)
    layer_ids = lax.broadcasted_iota(jnp.int32, shape, 0)
    cell_x = lax.broadcasted_iota(jnp.int32, shape, 1)
    cell_y = lax.broadcasted_iota(jnp.int32, shape, 2)
    inside = (jnp.abs(cell_x - centre_x) <= half_x) & (jnp.abs(cell_y - centre_y) <= half_y) & (layer_ids < depth)
    return inside.astype(jnp.int32)


def draw_well_mask(key, part):
    key = jax.random.fold_in(key, 37)
    keys = jax.random.split(key, 5)
    shape = (LAYERS, NX, NY)
    chosen = jax.random.randint(keys[0], (NX, NY), 0, 16) == 0
    forced_x = jax.random.randint(keys[1], (), 0, NX)
    forced_y = jax.random.randint(keys[2], (), 0, NY)
    plane_x = lax.broadcasted_iota(jnp.int32, (NX, NY), 0)
    plane_y = lax.broadcasted_iota(jnp.int32, (NX, NY), 1)
    column = chosen | (plane_x == forced_x) & (plane_y == forced_y)
    screen_top = jax.random.randint(keys[3], (NX, NY), 0, LAYERS // 2)
    screen_span = jax.random.randint(keys[4], (NX, NY), 1, LAYERS // 2 + 1)
    layer_ids = lax.broadcasted_iota(jnp.int32, shape, 0)
    screened = column[None] & (layer_ids >= screen_top[None]) & (layer_ids < screen_top[None] + screen_span[None])
    return screened.astype(jnp.int32)


def place_ends(entries, key, smallest, largest):
    longest = entries.shape.index(max(entries.shape))
    spots = []
    for shift in (0, 1):
        where = [jax.random.randint(jax.random.fold_in(key, axis), (), 0, length) for axis, length in enumerate(entries.shape)]
        where[longest] = (where[longest] + shift) % entries.shape[longest]
        spots.append(tuple(where))
    return entries.at[spots[0]].set(smallest).at[spots[1]].set(largest)


def shard_levels(stream_key, dims, cuts, least, high):
    gain = 1.0
    for axis_at, blocks in cuts:
        steps = jax.random.uniform(jax.random.fold_in(jax.random.fold_in(stream_key, 6), axis_at), (blocks,), jnp.float32, least / len(cuts), high / len(cuts))
        gain = gain * jnp.repeat(jnp.exp(steps), dims[axis_at] // blocks).reshape((-1,) + (1,) * (len(dims) - 1 - axis_at))
    return gain


def setup_inputs(seed: int = 0) -> dict:
    key_list = jax.random.split(jax.random.key(seed), 11)
    return {
        "drawdown": draw_drawdown(jax.random.fold_in(key_list[10], 71), 0),
        "step_ratio": jnp.clip(jnp.exp(math.log(30000.0) - 2.3025851 * jax.random.uniform(key_list[1], (LAYERS, NX, NY), jnp.float32) ** shard_levels(key_list[1], (LAYERS, NX, NY), ((1, 16), (2, 16)), -0.2, 0.2)), 3000.0, 30000.0),
        "layer_class": place_ends(jax.random.randint(key_list[2], (LAYERS, NX, NY), 0, CLASSES), jax.random.fold_in(key_list[2], 1), 0, CLASSES - 1).astype(jnp.int32),
        "class_conductance": jnp.clip(jnp.exp(jax.random.uniform(key_list[3], (CLASSES,), jnp.float32, math.log(3.0), math.log(30.0))), 3.0, 30.0),
        "leakance": jnp.clip(jnp.exp(jax.random.uniform(key_list[4], (LAYERS - 1,), jnp.float32, math.log(0.0005), math.log(0.02))), 0.0005, 0.02),
        "well_mask": draw_well_mask(jax.random.fold_in(key_list[10], 71), 0),
        "rate_index": place_ends(jax.random.randint(key_list[6], (NX, NY), 0, RATES), jax.random.fold_in(key_list[6], 1), 0, RATES - 1).astype(jnp.int32),
        "rate_table": jnp.clip(jnp.exp(jax.random.uniform(key_list[7], (RATES,), jnp.float32, math.log(1.0), math.log(10.0))), 1.0, 10.0),
        "pit_mask": draw_pit_mask(jax.random.fold_in(key_list[10], 71), 0),
        "pit_level": jnp.clip(jax.random.uniform(key_list[9], (LAYERS,), jnp.float32, 1.0, 3.0), 1.0, 3.0),
    }


def harmonic(first_val, second_val):
    return 2.0 * first_val * second_val / (first_val + second_val)


def shifted_pair(field, axis_idx):
    widths = [(0, 0)] * field.ndim
    widths[axis_idx] = (1, 1)
    padded = jnp.pad(field, widths)
    length = field.shape[axis_idx]
    below = lax.slice_in_dim(padded, 0, length, axis=axis_idx)
    above = lax.slice_in_dim(padded, 2, length + 2, axis=axis_idx)
    return below, above


def face_pair(conduct, below, above):
    face_below = harmonic(conduct, jnp.where(below > 0, below, conduct))
    face_above = harmonic(conduct, jnp.where(above > 0, above, conduct))
    return face_below, face_above


def band_rows(step_ratio, face_below, face_above, pit_cells):
    lower_band = jnp.where(pit_cells, 0.0, -step_ratio * face_below)
    upper_band = jnp.where(pit_cells, 0.0, -step_ratio * face_above)
    diag_band = jnp.where(pit_cells, 1.0, 1.0 + step_ratio * (face_below + face_above))
    return lower_band, diag_band, upper_band


def thomas_lines(lower_band, diag_band, upper_band, right_side):
    def forward(carried, row_items):
        ratio_prev, value_prev = carried
        low_c, diag_c, up_c, rhs_c = row_items
        pivot_val = diag_c - low_c * ratio_prev
        ratio_next = up_c / pivot_val
        value_next = (rhs_c - low_c * value_prev) / pivot_val
        return (ratio_next, value_next), (ratio_next, value_next)

    zero_row = jnp.zeros_like(diag_band[0])
    unused, (ratios, values) = lax.scan(forward, (zero_row, zero_row), (lower_band, diag_band, upper_band, right_side))

    def backward(carried, row_items):
        ratio_c, value_c = row_items
        solved = value_c - ratio_c * carried
        return solved, solved

    unused, solved_all = lax.scan(backward, zero_row, (ratios, values), reverse=True)
    return solved_all


def sweep_axis(bands, right_side, axis_idx):
    moved = [jnp.moveaxis(band, axis_idx, 0) for band in bands]
    solved = thomas_lines(moved[0], moved[1], moved[2], jnp.moveaxis(right_side, axis_idx, 0))
    return jnp.moveaxis(solved, 0, axis_idx)


def vertical_thomas(lower_band, diag_band, upper_band, right_side):
    ratio_prev = jnp.zeros_like(diag_band[0])
    value_prev = jnp.zeros_like(diag_band[0])
    ratio_list = []
    value_list = []
    for layer_idx in range(diag_band.shape[0]):
        pivot_val = diag_band[layer_idx] - lower_band[layer_idx] * ratio_prev
        ratio_prev = upper_band[layer_idx] / pivot_val
        value_prev = (right_side[layer_idx] - lower_band[layer_idx] * value_prev) / pivot_val
        ratio_list.append(ratio_prev)
        value_list.append(value_prev)
    solved = value_list[-1]
    result_list = [solved]
    for layer_idx in range(diag_band.shape[0] - 2, -1, -1):
        solved = value_list[layer_idx] - ratio_list[layer_idx] * solved
        result_list.append(solved)
    return jnp.stack(result_list[::-1])


def reference(drawdown, step_ratio, layer_class, class_conductance, leakance, well_mask, rate_index, rate_table, pit_mask, pit_level):
    conduct = class_conductance[layer_class]
    pumping_rate = rate_table[rate_index]
    x_low_s, x_up_s = shifted_pair(drawdown, 1)
    y_low_s, y_up_s = shifted_pair(drawdown, 2)
    x_low_k, x_up_k = shifted_pair(conduct, 1)
    y_low_k, y_up_k = shifted_pair(conduct, 2)
    fx_below, fx_above = face_pair(conduct, x_low_k, x_up_k)
    fy_below, fy_above = face_pair(conduct, y_low_k, y_up_k)
    across_y = fy_above * (y_up_s - drawdown) - fy_below * (drawdown - y_low_s)
    vertical_g = leakance[:, None, None] * harmonic(conduct[:-1], conduct[1:])
    zero_layer = jnp.zeros_like(drawdown[:1])
    fz_below = jnp.concatenate([zero_layer, vertical_g], axis=0)
    fz_above = jnp.concatenate([vertical_g, zero_layer], axis=0)
    z_low_s = jnp.concatenate([zero_layer, drawdown[:-1]], axis=0)
    z_up_s = jnp.concatenate([drawdown[1:], zero_layer], axis=0)
    across_z = fz_above * (z_up_s - drawdown) - fz_below * (drawdown - z_low_s)
    pit_cells = pit_mask == 1
    pit_field = jnp.broadcast_to(pit_level[:, None, None], drawdown.shape)
    pumping = well_mask.astype(jnp.float32) * pumping_rate[None]
    first_rhs = drawdown + step_ratio * (across_y + across_z + pumping)
    x_bands = band_rows(step_ratio, fx_below, fx_above, pit_cells)
    section_x = sweep_axis(x_bands, jnp.where(pit_cells, pit_field, first_rhs), 1)
    y_bands = band_rows(step_ratio, fy_below, fy_above, pit_cells)
    section_y = sweep_axis(y_bands, jnp.where(pit_cells, pit_field, section_x - step_ratio * across_y), 2)
    z_bands = band_rows(step_ratio, fz_below, fz_above, pit_cells)
    third_rhs = jnp.where(pit_cells, pit_field, section_y - step_ratio * across_z)
    return vertical_thomas(z_bands[0], z_bands[1], z_bands[2], third_rhs)
```

```python
import jax
import jax.numpy as jnp
from jax import lax
from jax.experimental import pallas as pl
from jax.experimental.pallas import tpu as pltpu
from jax.sharding import PartitionSpec as P

MESH = pl.DeviceIdType.MESH
HELD = 2.0**100
CELLS = 16
RUNS = 8


def inverse(x):
    return pl.reciprocal(x, approx=True)


def order(count):
    steps = []
    stride = 1
    while stride < count:
        for node in range(stride - 1, count - 1, 2 * stride):
            steps.append((node, node - stride, node + stride))
        stride *= 2
    return steps


def plus(total, term):
    return term if total is None else total + term


def reduce_matrix(c, w):
    c, w, w_left, kept = list(c), list(w), None, {}
    for k, left, right in order(len(c)):
        inv = inverse(w[k] + (c[k] + c[right]))
        tl, tr = c[k] * inv, c[right] * inv
        c[right] = c[k] * tr
        if left < 0:
            w_left = plus(w_left, w[k] * tl)
        else:
            w[left] = w[left] + w[k] * tl
        w[right] = w[right] + w[k] * tr
        kept[k] = (inv, tl, tr)
    return c[-1], w[-1], w_left, kept


def reduce_rhs(b, kept):
    b, b_left, base = list(b), None, {}
    for k, left, right in order(len(b)):
        inv, tl, tr = kept(k)
        if left < 0:
            b_left = plus(b_left, b[k] * tl)
        else:
            b[left] = b[left] + b[k] * tl
        b[right] = b[right] + b[k] * tr
        base[k] = b[k] * inv
    return b[-1], b_left, base


def expand(count, base, tl, tr, s_left, s_last):
    s = {-1: s_left, count - 1: s_last}
    for k, left, right in reversed(order(count)):
        s[k] = base(k) + tl(k) * s[left] + tr(k) * s[right]
    return s


def up(x, by):
    return pltpu.roll(x, RUNS - by, 0)


def down(x, by):
    return pltpu.roll(x, by, 0)


def chain_matrix(c_e, w_e, c_o, w_o, sub):
    inv = inverse(w_e + (c_e + c_o))
    tl, tr = c_e * inv, c_o * inv
    c = c_e * tr
    w = w_o + w_e * tr + jnp.where(sub < RUNS - 1, up(w_e * tl, 1), 0.0)
    kept = [(inv, tl, tr)]
    for by in (1, 2, 4):
        right = jnp.where(sub < RUNS - by, up(c, by), 0.0)
        inv = inverse(w + (c + right))
        tl, tr = c * inv, right * inv
        kept.append((inv, tl, tr))
        w = (
            w
            + jnp.where(sub >= by, down(w * tr, by), 0.0)
            + jnp.where(sub < RUNS - by, up(w * tl, by), 0.0)
        )
        c = jnp.where(sub >= by, down(c * tr, by), c)
    kept.append(inverse(w + c))
    return kept


def chain_rhs(kept, b_e, b_o, sub):
    inv_e, tl_e, tr_e = kept[0]
    b = b_o + b_e * tr_e + jnp.where(sub < RUNS - 1, up(b_e * tl_e, 1), 0.0)
    for by, (inv, tl, tr) in zip((1, 2, 4), kept[1:4]):
        b = (
            b
            + jnp.where(sub >= by, down(b * tr, by), 0.0)
            + jnp.where(sub < RUNS - by, up(b * tl, by), 0.0)
        )
    s_o = b * kept[4]
    s_low = jnp.where(sub >= 1, down(s_o, 1), 0.0)
    s_e = b_e * inv_e + tl_e * s_low + tr_e * s_o
    return s_low, s_e, s_o


def kernel(
    s_in,
    r_in,
    cls_in,
    k_tab,
    leak,
    well_in,
    rate_in,
    rate_tab,
    pit_in,
    level,
    out,
    s_v,
    w_v,
    cls_v,
    well_v,
    rate_v,
    pit_v,
    ra_v,
    rat_v,
    st_v,
    wt_v,
    q_v,
    tmp_v,
    ly_v,
    lz_v,
    fy_v,
    xh_v,
    xl_v,
    xr_v,
    yi_v,
    yl_v,
    yr_v,
    zt_v,
    zi_v,
    ez_v,
    lo_send,
    hi_send,
    x_send,
    lo_recv,
    hi_recv,
    x_recv,
    node_w,
    node_c,
    node_e,
    node_b,
    node_g,
    xa_send,
    xa_recv,
    xb_send,
    xb_recv,
    ym_send,
    ym_recv,
    ya_send,
    ya_recv,
    yb_send,
    yb_recv,
    in_sem,
    out_sem,
    halo_sem,
    a2a_sem,
):
    layers = s_in.shape[0]
    ix, iy = lax.axis_index("gx"), lax.axis_index("gy")
    nx, ny = lax.axis_size("gx"), lax.axis_size("gy")
    rows = RUNS * layers

    loads = [
        pltpu.make_async_copy(src, dst, in_sem.at[n])
        for n, (src, dst) in enumerate(
            [
                (cls_in, cls_v),
                (s_in, s_v),
                (r_in, w_v),
                (pit_in, pit_v),
                (rate_in, rate_v),
                (well_in, well_v),
            ]
        )
    ]
    for load in loads:
        load.start()

    barrier = pltpu.get_barrier_semaphore()

    def greet(k, _):
        pl.semaphore_signal(
            barrier, inc=1, device_id={"gx": lax.rem(ix + k, nx)}, device_id_type=MESH
        )
        return 0

    def greet_y(k, _):
        pl.semaphore_signal(
            barrier, inc=1, device_id={"gy": lax.rem(iy + k, ny)}, device_id_type=MESH
        )
        return 0

    lax.fori_loop(1, nx, greet, 0)
    lax.fori_loop(1, ny, greet_y, 0)

    sub = lax.broadcasted_iota(jnp.int32, (RUNS, 128), 0)
    first, final = sub == 0, sub == RUNS - 1
    ra_tab = [0.5 / jnp.full((RUNS, 128), k_tab[n], jnp.float32) for n in range(8)]
    ra_tab = [jnp.broadcast_to(t[:1], (128, 128)) for t in ra_tab]

    def strided(ref, l):
        return [ref[l, pl.ds(n, RUNS, stride=CELLS), :] for n in range(CELLS)]

    loads[0].wait()
    loads[1].wait()

    def look(l, _):
        cls = cls_v[l]
        odd, two, four = (cls & 1) != 0, (cls & 2) != 0, cls >= 4
        pairs = [jnp.where(odd, ra_tab[n + 1], ra_tab[n]) for n in (0, 2, 4, 6)]
        ra = jnp.where(
            four, jnp.where(two, pairs[3], pairs[2]), jnp.where(two, pairs[1], pairs[0])
        )
        ra_v[l] = ra
        rat_v[l] = ra.T
        st_v[l] = s_v[l].T
        return 0

    lax.fori_loop(0, layers, look, 0)
    lo_send[0] = st_v[:, 0, :]
    lo_send[1] = rat_v[:, 0, :]
    hi_send[0] = st_v[:, 127, :]
    hi_send[1] = rat_v[:, 127, :]
    x_send[...] = ra_v[:, 127, :]

    pl.semaphore_wait(barrier, nx + ny - 2)

    halos = [
        pltpu.make_async_remote_copy(
            src_ref=src,
            dst_ref=dst,
            send_sem=halo_sem.at[2 * n],
            recv_sem=halo_sem.at[2 * n + 1],
            device_id=where,
            device_id_type=MESH,
        )
        for n, (src, dst, where) in enumerate(
            [
                (lo_send, hi_recv, {"gy": lax.rem(iy + ny - 1, ny)}),
                (hi_send, lo_recv, {"gy": lax.rem(iy + 1, ny)}),
                (x_send, x_recv, {"gx": lax.rem(ix + 1, nx)}),
            ]
        )
    ]
    for halo in halos:
        halo.start()

    loads[2].wait()
    loads[3].wait()

    def weigh(l, _):
        pit = pit_v[l] == 1
        w = jnp.where(pit, HELD, inverse(w_v[l]))
        w_v[l] = w
        s_v[l] = w * jnp.where(pit, level[l], s_v[l])
        wt_v[l] = w.T
        return 0

    lax.fori_loop(0, layers, weigh, 0)

    loads[4].wait()
    loads[5].wait()
    rate = rate_v[...]
    pump = jnp.full(rate.shape, rate_tab[0], jnp.float32)
    for n in range(1, 16):
        pump = jnp.where(rate == n, rate_tab[n], pump)
    tmp_v[0] = pump

    for halo in halos:
        halo.wait_recv()
    at_lo, at_hi = iy == 0, iy == ny - 1
    lo_recv[0] = jnp.where(at_lo, 0.0, lo_recv[0])
    lo_recv[1] = jnp.where(at_lo, lo_send[1], lo_recv[1])
    hi_recv[0] = jnp.where(at_hi, 0.0, hi_recv[0])
    hi_recv[1] = jnp.where(at_hi, hi_send[1], hi_recv[1])
    x_recv[...] = jnp.where(ix == 0, ra_v[:, 0, :], x_recv[...])

    ez_v[...] = jnp.zeros_like(ez_v)

    def across(l, _):
        above = jnp.minimum(l + 1, layers - 1)
        below = jnp.maximum(l - 1, 0)
        leak_l = jnp.where(l < layers - 1, leak[jnp.minimum(l, layers - 2)], 0.0)
        leak_b = jnp.where(l > 0, leak[below], 0.0)
        ra, s = strided(rat_v, l), strided(st_v, l)
        ra_left = jnp.where(first, lo_recv[1, pl.ds(l, 1), :], down(ra[15], 1))
        s_left = jnp.where(first, lo_recv[0, pl.ds(l, 1), :], down(s[15], 1))
        face = inverse(ra_left + ra[0])
        fy_v[l, 0] = face
        flux_left = face * (s[0] - s_left)
        face_end = inverse(ra[15] + hi_recv[1, pl.ds(l, 1), :])
        flux_end = face_end * (hi_recv[0, pl.ds(l, 1), :] - s[15])
        flux_end = jnp.where(final, flux_end, up(flux_left, 1))
        flux = flux_left
        for n in range(CELLS):
            if n < CELLS - 1:
                face = inverse(ra[n] + ra[n + 1])
                fy_v[l, n + 1] = face
                flux_next = face * (s[n + 1] - s[n])
            else:
                flux_next = flux_end
            ly = flux_next - flux
            flux = flux_next
            run = pl.ds(n, RUNS, stride=CELLS)
            face_z = leak_l * inverse(ra[n] + rat_v[above, run, :])
            face_b = leak_b * inverse(ra[n] + rat_v[below, run, :])
            lz = face_z * (st_v[above, run, :] - s[n]) - face_b * (s[n] - st_v[below, run, :])
            ly_v[l, n] = ly
            lz_v[l, n] = lz
            tmp_v[1, run, :] = ly + lz
            e = wt_v[l, run, :] + ez_v[n]
            inv = inverse(e + face_z)
            t = face_z * inv
            zt_v[l, n] = t
            zi_v[l, n] = inv
            ez_v[n] = e * t
        q_v[l] = tmp_v[1].T
        return 0

    lax.fori_loop(0, layers, across, 0)

    def whole(ref):
        return ref.at[pl.ds(0, rows - RUNS)]

    def block(ref, n):
        return ref.at[pl.ds(pl.multiple_of(n * RUNS, RUNS), RUNS)]

    def spread(src, dst, pair, axis, me, count):
        def send(k, _):
            other = lax.rem(me + k, count)
            pltpu.make_async_remote_copy(
                src_ref=block(src, other),
                dst_ref=block(dst, me),
                send_sem=a2a_sem.at[2 * pair],
                recv_sem=a2a_sem.at[2 * pair + 1],
                device_id={axis: other},
                device_id_type=MESH,
            ).start()
            return 0

        lax.fori_loop(1, count, send, 0)
        own = pl.ds(pl.multiple_of(me * RUNS, RUNS), RUNS)
        dst[own, :] = src[own, :]

    def arrived(dst, pair):
        pltpu.make_async_copy(whole(dst), whole(dst), a2a_sem.at[2 * pair + 1]).wait()

    def left(src, pair):
        pltpu.make_async_copy(whole(src), whole(src), a2a_sem.at[2 * pair]).wait()

    def nodes(ref, h):
        return [ref[pl.ds(n + 64 * h, 8, stride=RUNS), :] for n in range(RUNS)]

    def put(ref, n, h, x):
        ref[pl.ds(n + 64 * h, 8, stride=RUNS), :] = x

    def join(w, extra):
        return [w[n] + extra[n + 1] for n in range(RUNS - 1)] + [w[RUNS - 1]]

    def runs_x(l, _):
        ra, w = strided(ra_v, l), strided(w_v, l)
        ra_left = jnp.where(first, x_recv[pl.ds(l, 1), :], down(ra[15], 1))
        c = [inverse(ra_left + ra[0])]
        c += [inverse(ra[n] + ra[n + 1]) for n in range(CELLS - 1)]
        b = []
        for n in range(CELLS):
            run = pl.ds(n, RUNS, stride=CELLS)
            pumped = well_v[l, run, :].astype(jnp.float32) * tmp_v[0, run, :]
            b.append(s_v[l, run, :] + (q_v[l, run, :] + pumped))
        c, w, e, kept = reduce_matrix(c, w)
        b, g, base = reduce_rhs(b, lambda k: kept[k])
        for k in base:
            xh_v[l, k] = base[k]
            xl_v[l, k] = kept[k][1]
            xr_v[l, k] = kept[k][2]
        at = pl.ds(pl.multiple_of(l * RUNS, RUNS), RUNS)
        for ref, x in ((node_w, w), (node_c, c), (node_e, e), (node_b, b), (node_g, g)):
            ref[at, :] = x
        return 0

    lax.fori_loop(0, layers, runs_x, 0)

    x_runs = []
    for h in range(2):
        w_extra, b_extra = nodes(node_e, h), nodes(node_g, h)
        c, w, e, kept = reduce_matrix(nodes(node_c, h), join(nodes(node_w, h), w_extra))
        b, g, base = reduce_rhs(join(nodes(node_b, h), b_extra), lambda k: kept[k])
        edge = inverse(2.0 * x_send[pl.ds(8 * h, 8), :])
        w = w + jnp.where(ix == nx - 1, edge, 0.0)
        for n, x in enumerate((c, w, e + w_extra[0], b, g + b_extra[0])):
            put(xa_send, n, h, x)
        x_runs.append((base, kept))
    spread(xa_send, xa_recv, 0, "gx", ix, nx)

    def runs_y(l, _):
        c = [fy_v[l, n] for n in range(CELLS)]
        c, w, e, kept = reduce_matrix(c, strided(wt_v, l))
        for k in kept:
            yi_v[l, k], yl_v[l, k], yr_v[l, k] = kept[k]
        at = pl.ds(pl.multiple_of(l * RUNS, RUNS), RUNS)
        for ref, x in ((node_w, w), (node_c, c), (node_e, e)):
            ref[at, :] = x
        return 0

    lax.fori_loop(0, layers, runs_y, 0)

    y_runs = []
    for h in range(2):
        w_extra = nodes(node_e, h)
        c, w, e, kept = reduce_matrix(nodes(node_c, h), join(nodes(node_w, h), w_extra))
        edge = inverse(2.0 * hi_send[1, pl.ds(8 * h, 8), :])
        w = w + jnp.where(iy == ny - 1, edge, 0.0)
        for n, x in enumerate((c, w, e + w_extra[0])):
            put(ym_send, n, h, x)
        y_runs.append(kept)
    spread(ym_send, ym_recv, 2, "gy", iy, ny)

    def take(ref, n):
        even = ref[pl.ds(n, 8, stride=2 * RUNS), :]
        odd = ref[pl.ds(RUNS + n, 8, stride=2 * RUNS), :]
        return even, odd

    def beyond(odd_w, extra_e):
        return odd_w + jnp.where(final, 0.0, up(extra_e, 1))

    def give(ref, s_low, s_e, s_o):
        ref[pl.ds(0, 8, stride=2 * RUNS), :] = s_low
        ref[pl.ds(1, 8, stride=2 * RUNS), :] = s_e
        ref[pl.ds(RUNS, 8, stride=2 * RUNS), :] = s_e
        ref[pl.ds(RUNS + 1, 8, stride=2 * RUNS), :] = s_o

    arrived(xa_recv, 0)
    c, w, e, b, g = [take(xa_recv, n) for n in range(5)]
    kept = chain_matrix(c[0], w[0] + e[1], c[1], beyond(w[1], e[0]), sub)
    give(xb_send, *chain_rhs(kept, b[0] + g[1], beyond(b[1], g[0]), sub))
    spread(xb_send, xb_recv, 1, "gx", ix, nx)

    arrived(ym_recv, 2)
    c, w, e = [take(ym_recv, n) for n in range(3)]
    y_chain = chain_matrix(c[0], w[0] + e[1], c[1], beyond(w[1], e[0]), sub)

    arrived(xb_recv, 1)

    def ends(ref, h, base, kept):
        s_left = ref[pl.ds(64 * h, 8, stride=RUNS), :]
        s_last = ref[pl.ds(64 * h + 1, 8, stride=RUNS), :]
        s = expand(
            RUNS, lambda k: base[k], lambda k: kept[k][1], lambda k: kept[k][2], s_left, s_last
        )
        for n in range(RUNS):
            put(node_w, n, h, s[n])
            put(node_c, n, h, s[n - 1])

    for h in range(2):
        ends(xb_recv, h, *x_runs[h])

    def fill_x(l, _):
        at = pl.ds(pl.multiple_of(l * RUNS, RUNS), RUNS)
        s = expand(
            CELLS,
            lambda k: xh_v[l, k],
            lambda k: xl_v[l, k],
            lambda k: xr_v[l, k],
            node_c[at, :],
            node_w[at, :],
        )
        for n in range(CELLS):
            tmp_v[1, pl.ds(n, RUNS, stride=CELLS), :] = s[n]
        q_v[l] = tmp_v[1].T
        b = []
        for n in range(CELLS):
            run = pl.ds(n, RUNS, stride=CELLS)
            b.append(wt_v[l, run, :] * q_v[l, run, :] - ly_v[l, n])
        b, g, base = reduce_rhs(b, lambda k: (yi_v[l, k], yl_v[l, k], yr_v[l, k]))
        for k in base:
            xh_v[l, k] = base[k]
        node_b[at, :] = b
        node_g[at, :] = g
        return 0

    lax.fori_loop(0, layers, fill_x, 0)

    y_base = []
    for h in range(2):
        b_extra = nodes(node_g, h)
        b, g, base = reduce_rhs(join(nodes(node_b, h), b_extra), lambda k: y_runs[h][k])
        put(ya_send, 0, h, b)
        put(ya_send, 1, h, g + b_extra[0])
        y_base.append(base)
    spread(ya_send, ya_recv, 3, "gy", iy, ny)
    arrived(ya_recv, 3)
    b, g = take(ya_recv, 0), take(ya_recv, 1)
    give(yb_send, *chain_rhs(y_chain, b[0] + g[1], beyond(b[1], g[0]), sub))
    spread(yb_send, yb_recv, 4, "gy", iy, ny)
    arrived(yb_recv, 4)
    for h in range(2):
        ends(yb_recv, h, y_base[h], y_runs[h])

    ez_v[...] = jnp.zeros_like(ez_v)

    def fill_y(l, _):
        at = pl.ds(pl.multiple_of(l * RUNS, RUNS), RUNS)
        s = expand(
            CELLS,
            lambda k: xh_v[l, k],
            lambda k: yl_v[l, k],
            lambda k: yr_v[l, k],
            node_c[at, :],
            node_w[at, :],
        )
        for n in range(CELLS):
            b = wt_v[l, pl.ds(n, RUNS, stride=CELLS), :] * s[n] - lz_v[l, n] + ez_v[n]
            ez_v[n] = b * zt_v[l, n]
            zi_v[l, n] = b * zi_v[l, n]
        return 0

    lax.fori_loop(0, layers, fill_y, 0)

    ez_v[...] = jnp.zeros_like(ez_v)

    def write(l, _):
        return pltpu.make_async_copy(q_v.at[l], out.at[l], out_sem)

    def fill_z(step, _):
        l = layers - 1 - step
        for n in range(CELLS):
            s = zi_v[l, n] + zt_v[l, n] * ez_v[n]
            ez_v[n] = s
            tmp_v[1, pl.ds(n, RUNS, stride=CELLS), :] = s
        q_v[l] = tmp_v[1].T
        return 0

    lax.fori_loop(0, layers, fill_z, 0)
    final_copy = pltpu.make_async_copy(q_v, out, out_sem)
    final_copy.start()
    for halo in halos:
        halo.wait_send()
    left(xa_send, 0)
    left(xb_send, 1)
    left(ym_send, 2)
    left(ya_send, 3)
    left(yb_send, 4)
    final_copy.wait()


def body(*args):
    layers, cells_x, cells_y = args[0].shape
    field = pltpu.VMEM((layers, cells_x, cells_y), jnp.float32)
    index = pltpu.VMEM((layers, cells_x, cells_y), jnp.int32)
    runs = pltpu.VMEM((layers, CELLS, RUNS, 128), jnp.float32)
    rows = pltpu.VMEM((RUNS * layers, 128), jnp.float32)
    halo = pltpu.VMEM((2, layers, 128), jnp.float32)
    edge = pltpu.VMEM((layers, 128), jnp.float32)
    hbm = pl.BlockSpec(memory_space=pl.ANY)
    smem = pl.BlockSpec(memory_space=pltpu.SMEM)
    return pl.pallas_call(
        kernel,
        out_shape=jax.ShapeDtypeStruct(args[0].shape, jnp.float32),
        in_specs=[hbm, hbm, hbm, smem, smem, hbm, hbm, smem, hbm, smem],
        out_specs=hbm,
        scratch_shapes=[
            field,
            field,
            index,
            index,
            pltpu.VMEM((cells_x, cells_y), jnp.int32),
            index,
            field,
            field,
            field,
            field,
            field,
            pltpu.VMEM((2, cells_x, cells_y), jnp.float32),
            runs,
            runs,
            runs,
            runs,
            runs,
            runs,
            runs,
            runs,
            runs,
            runs,
            runs,
            pltpu.VMEM((CELLS, RUNS, 128), jnp.float32),
            halo,
            halo,
            edge,
            halo,
            halo,
            edge,
        ]
        + [rows] * 15
        + [
            pltpu.SemaphoreType.DMA((6,)),
            pltpu.SemaphoreType.DMA,
            pltpu.SemaphoreType.DMA((6,)),
            pltpu.SemaphoreType.DMA((10,)),
        ],
        compiler_params=pltpu.CompilerParams(
            collective_id=0, has_side_effects=True, vmem_limit_bytes=56 * 1024 * 1024
        ),
        cost_estimate=pl.CostEstimate(
            flops=100 * args[0].size, bytes_accessed=24 * args[0].size, transcendentals=0
        ),
        name="drawdown_step",
    )(*args)


def solution(mesh):
    field = P(None, "gx", "gy")
    in_specs = (field, field, field, P(), P(), field, P("gx", "gy"), P(), field, P())
    return jax.shard_map(body, mesh=mesh, in_specs=in_specs, out_specs=field, check_vma=False)
```

```python
import jax
import jax.numpy as jnp
from jax import lax
from jax.experimental import pallas as pl
from jax.experimental.pallas import tpu as pltpu
from jax.sharding import PartitionSpec as P

MESH = pl.DeviceIdType.MESH
HELD = 2.0**100
CELLS = 16
RUNS = 8
TILE = CELLS * RUNS


def inverse(x):
    return pltpu.reciprocal(x, approx=True)


def order(count):
    steps = []
    stride = 1
    while stride < count:
        for node in range(stride - 1, count - 1, 2 * stride):
            steps.append((node, node - stride, node + stride))
        stride *= 2
    return steps


def plus(total, term):
    return term if total is None else total + term


def reduce_matrix(c, w):
    c, w, w_left, kept = list(c), list(w), None, {}
    for k, left, right in order(len(c)):
        inv = inverse(w[k] + (c[k] + c[right]))
        tl, tr = c[k] * inv, c[right] * inv
        c[right] = c[k] * tr
        if left < 0:
            w_left = plus(w_left, w[k] * tl)
        else:
            w[left] = w[left] + w[k] * tl
        w[right] = w[right] + w[k] * tr
        kept[k] = (inv, tl, tr)
    return c[-1], w[-1], w_left, kept


def reduce_rhs(b, kept):
    b, b_left, base = list(b), None, {}
    for k, left, right in order(len(b)):
        inv, tl, tr = kept(k)
        if left < 0:
            b_left = plus(b_left, b[k] * tl)
        else:
            b[left] = b[left] + b[k] * tl
        b[right] = b[right] + b[k] * tr
        base[k] = b[k] * inv
    return b[-1], b_left, base


def expand(count, base, tl, tr, s_left, s_last):
    s = {-1: s_left, count - 1: s_last}
    for k, left, right in reversed(order(count)):
        s[k] = base(k) + tl(k) * s[left] + tr(k) * s[right]
    return s


def take_out(c_left, c_right, w):
    inv = inverse(w + (c_left + c_right))
    tl, tr = c_left * inv, c_right * inv
    return c_left * tr, w * tl, w * tr, (inv, tl, tr)


def down(x):
    return pltpu.roll(x, 1, 0)


def up(x):
    return pltpu.roll(x, RUNS - 1, 0)


def looped(count, unroll, step):
    def body(i, _):
        step([i * unroll + u for u in range(unroll)])
        return 0

    lax.fori_loop(0, count // unroll, body, 0)


def runs_kernel(
    s_in,
    r_in,
    cls_in,
    k_tab,
    leak,
    well_in,
    rate_in,
    rate_tab,
    pit_in,
    level,
    zi_out,
    zt_out,
    s_v,
    w_v,
    cls_v,
    well_v,
    rate_v,
    pit_v,
    ra_v,
    xi_v,
    xl_v,
    xr_v,
    rat_v,
    st_v,
    wt_v,
    q_v,
    wr_v,
    ly_v,
    lz_v,
    fy_v,
    yi_v,
    yl_v,
    yr_v,
    zt_v,
    zi_v,
    pump_v,
    ez_v,
    flux_v,
    ra_c,
    s_c,
    lo_send,
    hi_send,
    lo_recv,
    hi_recv,
    node_w,
    node_c,
    node_e,
    node_b,
    node_g,
    xm_send,
    xm_recv,
    xr_send,
    xr_recv,
    xs_v,
    pm_send,
    pm_recv,
    ym_send,
    ym_recv,
    pr_send,
    pr_recv,
    yr_send,
    yr_recv,
    ys_v,
    pb_send,
    pb_recv,
    yl_end,
    yr_end,
    in_sem,
    out_sem,
    send_sem,
    recv_sem,
):
    layers = s_in.shape[0]
    ix, iy = lax.axis_index("gx"), lax.axis_index("gy")
    nx, ny = lax.axis_size("gx"), lax.axis_size("gy")
    core, chip = lax.rem(iy, 2), iy // 2
    mate = {"gy": iy + 1 - 2 * core}
    halves = range(layers // 8)

    fields = [(cls_in, cls_v), (s_in, s_v), (r_in, w_v), (pit_in, pit_v), (well_in, well_v)]
    for n, (src, dst) in enumerate(fields):
        for q in range(RUNS):
            pltpu.make_async_copy(
                src.at[:, pl.ds(CELLS * q, CELLS), :], dst.at[:, :, q, :], in_sem.at[n]
            ).start()
    for q in range(RUNS):
        pltpu.make_async_copy(
            rate_in.at[pl.ds(CELLS * q, CELLS), :], rate_v.at[:, q, :], in_sem.at[5]
        ).start()

    def loaded(n):
        ref = fields[n][1] if n < 5 else rate_v
        pltpu.make_async_copy(ref, ref, in_sem.at[n]).wait()

    barrier = pltpu.get_barrier_semaphore()

    def greet(where):
        pl.semaphore_signal(barrier, inc=1, device_id=where, device_id_type=MESH)

    def greet_x(k, _):
        greet({"gx": lax.rem(ix + k, nx)})
        return 0

    def greet_y(k, _):
        greet({"gy": lax.rem(iy + 2 * k, ny)})
        return 0

    lax.fori_loop(1, nx, greet_x, 0)
    lax.fori_loop(1, ny // 2, greet_y, 0)
    greet({"gy": lax.rem(iy + 1, ny)})
    greet({"gy": lax.rem(iy + ny - 1, ny)})

    def remote(src, dst, n, where):
        return pltpu.make_async_remote_copy(
            src_ref=src,
            dst_ref=dst,
            send_sem=send_sem.at[n],
            recv_sem=recv_sem.at[n],
            device_id=where,
            device_id_type=MESH,
        )

    sub = lax.broadcasted_iota(jnp.int32, (RUNS, 128), 0)
    first, final = sub == 0, sub == RUNS - 1

    def at(l):
        return pl.ds(pl.multiple_of(l * RUNS, RUNS), RUNS)

    def turned(x):
        return x.reshape(TILE, 128).T

    def strided(ref, l):
        return [ref[l, pl.ds(n, RUNS, stride=CELLS), :] for n in range(CELLS)]

    ra_tab = [0.5 / jnp.full((RUNS, 128), k_tab[n], jnp.float32) for n in range(8)]
    ra_tab = [jnp.broadcast_to(t[:1], (TILE, 128)).reshape(CELLS, RUNS, 128) for t in ra_tab]
    loaded(0)
    loaded(1)

    def look(ls):
        ras = []
        for l in ls:
            cls = cls_v[l]
            odd, two, four = (cls & 1) != 0, (cls & 2) != 0, cls >= 4
            pairs = [jnp.where(odd, ra_tab[n + 1], ra_tab[n]) for n in (0, 2, 4, 6)]
            ras.append(
                jnp.where(
                    four,
                    jnp.where(two, pairs[3], pairs[2]),
                    jnp.where(two, pairs[1], pairs[0]),
                )
            )
        ss = [s_v[l] for l in ls]
        turned_ra = [turned(x) for x in ras]
        turned_s = [turned(x) for x in ss]
        for u, l in enumerate(ls):
            ra_v[l] = ras[u]
            rat_v[l] = turned_ra[u]
            st_v[l] = turned_s[u]

    looped(layers, 4, look)
    lo_send[0] = st_v[:, 0, :]
    lo_send[1] = rat_v[:, 0, :]
    hi_send[0] = st_v[:, TILE - 1, :]
    hi_send[1] = rat_v[:, TILE - 1, :]

    pl.semaphore_wait(barrier, nx + ny // 2)
    halos = [
        remote(lo_send, hi_recv, 0, {"gy": lax.rem(iy + ny - 1, ny)}),
        remote(hi_send, lo_recv, 1, {"gy": lax.rem(iy + 1, ny)}),
    ]
    for halo in halos:
        halo.start()

    loaded(2)
    loaded(3)
    own_x = jnp.where(ix == 0, 1.0, 0.0)

    def weigh(ls):
        ws = []
        for l in ls:
            pit = pit_v[l] == 1
            w = jnp.where(pit, HELD, inverse(w_v[l]))
            ws.append(w)
            s_v[l] = w * jnp.where(pit, level[l], s_v[l])
        wts = [turned(w) for w in ws]
        for u, l in enumerate(ls):
            wt_v[l] = wts[u]
        for u, l in enumerate(ls):
            ra, w = [ra_v[l, n] for n in range(CELLS)], [ws[u][n] for n in range(CELLS)]
            w_v[l] = ws[u]
            c = [inverse(ra[0] + jnp.where(first, own_x * ra[0], down(ra[15])))]
            c += [inverse(ra[n] + ra[n + 1]) for n in range(CELLS - 1)]
            c, w, e, kept = reduce_matrix(c, w)
            for k in kept:
                xi_v[l, k], xl_v[l, k], xr_v[l, k] = kept[k]
            node_w[at(l), :], node_c[at(l), :], node_e[at(l), :] = w, c, e

    looped(layers, 2, weigh)

    def nodes(ref, h):
        return [ref[pl.ds(n + 64 * h, 8, stride=RUNS), :] for n in range(RUNS)]

    def put(ref, n, h, x):
        ref[pl.ds(n + 64 * h, 8, stride=RUNS), :] = x

    def join(w, extra):
        return [w[n] + extra[n + 1] for n in range(RUNS - 1)] + [w[RUNS - 1]]

    def segment(h, c_end):
        extra = nodes(node_e, h)
        c, w, e, kept = reduce_matrix(nodes(node_c, h), join(nodes(node_w, h), extra))
        c, w_left, w_right, last = take_out(c, c_end, w)
        kept[RUNS - 1] = last
        return (c, extra[0] + e + w_left, w_right), kept

    def segment_rhs(h, kept):
        extra = nodes(node_g, h)
        b, g, base = reduce_rhs(join(nodes(node_b, h), extra), lambda k: kept[k])
        inv, tl, tr = kept[RUNS - 1]
        base[RUNS - 1] = b * inv
        return (extra[0] + g + b * tl, b * tr), base

    x_kept = []
    end_x = jnp.where(ix == nx - 1, 2.0, 1.0)
    for h in halves:
        values, kept = segment(h, inverse(end_x * ra_v[pl.ds(8 * h, 8), CELLS - 1, RUNS - 1, :]))
        for n, x in enumerate(values):
            xm_send[pl.ds(layers * n + 8 * h, 8), :] = x
        x_kept.append(kept)

    def gather_x(src, dst, n):
        def send(k, _):
            other = lax.rem(ix + k, nx)
            remote(src, dst.at[ix], n, {"gx": other}).start()
            return 0

        lax.fori_loop(1, nx, send, 0)
        dst[ix] = src[...]

    def gather_y(src, dst, n):
        def send(k, _):
            other = lax.rem(iy + 2 * k, ny)
            remote(src, dst.at[chip], n, {"gy": other}).start()
            return 0

        lax.fori_loop(1, ny // 2, send, 0)
        dst[chip] = src[...]

    def arrived(dst, n, count):
        ref = dst.at[pl.ds(0, count)]
        pltpu.make_async_copy(ref, ref, recv_sem.at[n]).wait()

    gather_x(xm_send, xm_recv, 2)

    ez_v[...] = jnp.zeros_like(ez_v)
    flux_v[...] = jnp.zeros_like(flux_v)
    own_y = jnp.where(iy == 0, 1.0, 0.0)
    for n in range(CELLS):
        ra_c[n] = rat_v[0, pl.ds(n, RUNS, stride=CELLS), :]
        s_c[n] = st_v[0, pl.ds(n, RUNS, stride=CELLS), :]

    def across(ls):
        ra = [ra_c[n] for n in range(CELLS)]
        s = [s_c[n] for n in range(CELLS)]
        for l in ls:
            above = jnp.minimum(l + 1, layers - 1)
            leak_l = jnp.where(l < layers - 1, leak[jnp.minimum(l, layers - 2)], 0.0)
            ra_up, s_up = strided(rat_v, above), strided(st_v, above)
            wt = strided(wt_v, l)
            ra_before = down(ra[15])
            face = inverse(ra[0] + jnp.where(first, own_y * ra[0], ra_before))
            fy_v[l, 0] = face
            flux_left = jnp.where(first, 0.0, face * (s[0] - down(s[15])))
            flux = flux_left
            for n in range(CELLS):
                if n < CELLS - 1:
                    face = inverse(ra[n] + ra[n + 1])
                    fy_v[l, n + 1] = face
                    flux_next = face * (s[n + 1] - s[n])
                else:
                    flux_next = up(flux_left)
                ly = flux_next - flux
                flux = flux_next
                face_z = leak_l * inverse(ra[n] + ra_up[n])
                flux_z = face_z * (s_up[n] - s[n])
                lz = flux_z - flux_v[n]
                flux_v[n] = flux_z
                ly_v[l, n] = ly
                lz_v[l, n] = lz
                q_v[l, pl.ds(n, RUNS, stride=CELLS), :] = ly + lz
                wr_v[l, n] = wt[n]
                e = wt[n] + ez_v[n]
                inv = inverse(e + face_z)
                t = face_z * inv
                zt_v[l, n] = t
                zi_v[l, n] = inv
                ez_v[n] = e * t
            ra, s = ra_up, s_up
        for n in range(CELLS):
            ra_c[n], s_c[n] = ra[n], s[n]

    looped(layers, 2, across)
    zt_copy = pltpu.make_async_copy(zt_v, zt_out, out_sem.at[0])
    zt_copy.start()

    loaded(4)
    loaded(5)
    rate = rate_v[...]
    pump = jnp.full(rate.shape, rate_tab[0], jnp.float32)
    for n in range(1, 16):
        pump = jnp.where(rate == n, rate_tab[n], pump)
    pump_v[...] = pump

    for halo in halos:
        halo.wait_recv()
    at_lo, at_hi = iy == 0, iy == ny - 1
    s_lo = jnp.where(at_lo, 0.0, lo_recv[0])
    ra_lo = jnp.where(at_lo, lo_send[1], lo_recv[1])
    s_hi = jnp.where(at_hi, 0.0, hi_recv[0])
    ra_hi = jnp.where(at_hi, hi_send[1], hi_recv[1])
    flux_lo = inverse(ra_lo + lo_send[1]) * (lo_send[0] - s_lo)
    flux_hi = inverse(ra_hi + hi_send[1]) * (s_hi - hi_send[0])
    q_v[:, 0, :] = q_v[:, 0, :] - flux_lo
    q_v[:, TILE - 1, :] = q_v[:, TILE - 1, :] + flux_hi
    ly_v[:, 0, 0, :] = ly_v[:, 0, 0, :] - flux_lo
    ly_v[:, CELLS - 1, RUNS - 1, :] = ly_v[:, CELLS - 1, RUNS - 1, :] + flux_hi

    def runs_x(ls):
        qs = [q_v[l].T.reshape(CELLS, RUNS, 128) for l in ls]
        bs = []
        for u, l in enumerate(ls):
            pumped = well_v[l].astype(jnp.float32) * pump_v[...]
            bs.append(s_v[l] + (qs[u] + pumped))
        for u, l in enumerate(ls):
            b, g, base = reduce_rhs(
                [bs[u][n] for n in range(CELLS)], lambda k: (xi_v[l, k], xl_v[l, k], xr_v[l, k])
            )
            for k in base:
                xi_v[l, k] = base[k]
            node_b[at(l), :], node_g[at(l), :] = b, g

    looped(layers, 4, runs_x)

    x_base = []
    for h in halves:
        values, base = segment_rhs(h, x_kept[h])
        for n, x in enumerate(values):
            xr_send[pl.ds(layers * n + 8 * h, 8), :] = x
        x_base.append(base)
    gather_x(xr_send, xr_recv, 3)

    def runs_y(ls):
        for l in ls:
            c, w, e, kept = reduce_matrix(
                [fy_v[l, n] for n in range(CELLS)], [wr_v[l, n] for n in range(CELLS)]
            )
            for k in kept:
                yi_v[l, k], yl_v[l, k], yr_v[l, k] = kept[k]
            node_w[at(l), :], node_c[at(l), :], node_e[at(l), :] = w, c, e

    looped(layers, 2, runs_y)

    is_a = core == 0

    def mine(pair):
        return jnp.where(is_a, pair[0], pair[1])

    def theirs(pair):
        return jnp.where(is_a, pair[1], pair[0])

    y_kept, y_values = [], []
    end_y = jnp.where(iy == ny - 1, 2.0, 1.0)
    for h in halves:
        values, kept = segment(h, inverse(end_y * hi_send[1, pl.ds(8 * h, 8), :]))
        y_values.append(values)
        y_kept.append(kept)
    for n, pair in enumerate(zip(*y_values)):
        pm_send[pl.ds(8 * n, 8), :] = theirs(pair)
    pm_copy = remote(pm_send, pm_recv, 4, mate)
    pm_copy.start()
    own = [mine(pair) for pair in zip(*y_values)]
    pm_copy.wait_recv()
    other = [pm_recv[pl.ds(8 * n, 8), :] for n in range(3)]
    c_a, c_b = mine((own[0], other[0])), theirs((own[0], other[0]))
    el_a, el_b = mine((own[1], other[1])), theirs((own[1], other[1]))
    er_a, er_b = mine((own[2], other[2])), theirs((own[2], other[2]))
    c, w_left, w_right, mid = take_out(c_a, c_b, er_a + el_b)
    for n, x in enumerate((c, el_a + w_left, er_b + w_right)):
        ym_send[pl.ds(8 * n, 8), :] = x
    gather_y(ym_send, ym_recv, 5)

    arrived(xm_recv, 2, nx - 1)
    zero = jnp.zeros((RUNS, 128), jnp.float32)

    def rows(ref, d, n, h):
        return ref[d, pl.ds(layers * n + 8 * h, 8), :]

    x_chain = []
    for h in halves:
        c = [rows(xm_recv, d, 0, h) for d in range(nx)]
        w = [rows(xm_recv, d, 2, h) + rows(xm_recv, d + 1, 1, h) for d in range(nx - 1)]
        x_chain.append(reduce_matrix(c, w + [zero])[3])

    arrived(xr_recv, 3, nx - 1)
    for h in halves:
        kept = x_chain[h]
        b = [rows(xr_recv, d, 1, h) + rows(xr_recv, d + 1, 0, h) for d in range(nx - 1)]
        base = reduce_rhs(b + [zero], lambda k: kept[k])[2]
        s = expand(
            nx, lambda k: base[k], lambda k: kept[k][1], lambda k: kept[k][2], zero, zero
        )
        for d in range(-1, nx):
            xs_v[d + 1, pl.ds(8 * h, 8), :] = s[d]

    def ends(s_left, s_right, h, base, kept):
        inv, tl, tr = kept[RUNS - 1]
        s_last = base[RUNS - 1] + tl * s_left + tr * s_right
        s = expand(
            RUNS, lambda k: base[k], lambda k: kept[k][1], lambda k: kept[k][2], s_left, s_last
        )
        for n in range(RUNS):
            put(node_w, n, h, s[n])
            put(node_c, n, h, s[n - 1])

    for h in halves:
        part = pl.ds(8 * h, 8)
        ends(xs_v[ix, part, :], xs_v[ix + 1, part, :], h, x_base[h], x_kept[h])

    def fill(l, base, tl, tr):
        s = expand(
            CELLS,
            lambda k: base[l, k],
            lambda k: tl[l, k],
            lambda k: tr[l, k],
            node_c[at(l), :],
            node_w[at(l), :],
        )
        return [s[n] for n in range(CELLS)]

    def fill_x(ls):
        lines = [turned(jnp.stack(fill(l, xi_v, xl_v, xr_v))) for l in ls]
        for u, l in enumerate(ls):
            q_v[l] = lines[u]
        for l in ls:
            sx = strided(q_v, l)
            b = [wr_v[l, n] * sx[n] - ly_v[l, n] for n in range(CELLS)]
            b, g, base = reduce_rhs(b, lambda k: (yi_v[l, k], yl_v[l, k], yr_v[l, k]))
            for k in base:
                yi_v[l, k] = base[k]
            node_b[at(l), :], node_g[at(l), :] = b, g

    looped(layers, 4, fill_x)

    y_base, y_values = [], []
    for h in halves:
        values, base = segment_rhs(h, y_kept[h])
        y_values.append(values)
        y_base.append(base)
    for n, pair in enumerate(zip(*y_values)):
        pr_send[pl.ds(8 * n, 8), :] = theirs(pair)
    pr_copy = remote(pr_send, pr_recv, 6, mate)
    pr_copy.start()
    own = [mine(pair) for pair in zip(*y_values)]

    arrived(ym_recv, 5, ny // 2 - 1)
    chips = ny // 2
    c = [ym_recv[d, pl.ds(0, 8), :] for d in range(chips)]
    w = [ym_recv[d, pl.ds(16, 8), :] + ym_recv[d + 1, pl.ds(8, 8), :] for d in range(chips - 1)]
    y_chain = reduce_matrix(c, w + [zero])[3]

    pr_copy.wait_recv()
    other = [pr_recv[pl.ds(8 * n, 8), :] for n in range(2)]
    gl_a, gl_b = mine((own[0], other[0])), theirs((own[0], other[0]))
    gr_a, gr_b = mine((own[1], other[1])), theirs((own[1], other[1]))
    b_mid = gr_a + gl_b
    inv_mid, tl_mid, tr_mid = mid
    yr_send[pl.ds(0, 8), :] = gl_a + b_mid * tl_mid
    yr_send[pl.ds(8, 8), :] = gr_b + b_mid * tr_mid
    gather_y(yr_send, yr_recv, 7)
    arrived(yr_recv, 7, chips - 1)
    b = [yr_recv[d, pl.ds(8, 8), :] + yr_recv[d + 1, pl.ds(0, 8), :] for d in range(chips - 1)]
    base = reduce_rhs(b + [zero], lambda k: y_chain[k])[2]
    s = expand(
        chips, lambda k: base[k], lambda k: y_chain[k][1], lambda k: y_chain[k][2], zero, zero
    )
    for d in range(-1, chips):
        ys_v[d + 1] = s[d]
    s_left, s_right = ys_v[chip], ys_v[chip + 1]
    s_mid = b_mid * inv_mid + tl_mid * s_left + tr_mid * s_right
    pb_send[pl.ds(0, 8), :] = theirs((s_left, s_mid))
    pb_send[pl.ds(8, 8), :] = theirs((s_mid, s_right))
    pb_copy = remote(pb_send, pb_recv, 8, mate)
    pb_copy.start()
    yl_end[at(core), :] = mine((s_left, s_mid))
    yr_end[at(core), :] = mine((s_mid, s_right))
    pb_copy.wait_recv()
    yl_end[at(1 - core), :] = pb_recv[pl.ds(0, 8), :]
    yr_end[at(1 - core), :] = pb_recv[pl.ds(8, 8), :]
    for h in halves:
        part = pl.ds(8 * h, 8)
        ends(yl_end[part, :], yr_end[part, :], h, y_base[h], y_kept[h])

    ez_v[...] = jnp.zeros_like(ez_v)

    def fill_y(ls):
        lines = [fill(l, yi_v, yl_v, yr_v) for l in ls]
        for u, l in enumerate(ls):
            for n in range(CELLS):
                b = wr_v[l, n] * lines[u][n] - lz_v[l, n] + ez_v[n]
                ez_v[n] = b * zt_v[l, n]
                zi_v[l, n] = b * zi_v[l, n]
            pltpu.make_async_copy(zi_v.at[l], zi_out.at[l], out_sem.at[1]).start()

    looped(layers, 2, fill_y)

    for halo in halos:
        halo.wait_send()
    for copy in (pm_copy, pr_copy, pb_copy):
        copy.wait_send()
    for ref, n, count in ((xm_recv, 2, nx), (xr_recv, 3, nx), (ym_recv, 5, chips), (yr_recv, 7, chips)):
        sent = ref.at[pl.ds(0, count - 1)]
        pltpu.make_async_copy(sent, sent, send_sem.at[n]).wait()
    zt_copy.wait()
    pltpu.make_async_copy(zi_v, zi_out, out_sem.at[1]).wait()


def layers_kernel(zi_in, zt_in, out, zi_v, zt_v, tmp_v, out_v, ez_v, in_sem, out_sem):
    layers = zi_in.shape[0]
    group = 4
    parts = list(range(layers - group, -1, -group))
    loads = []
    for n, l in enumerate(parts):
        part = pl.ds(l, group)
        loads.append(
            [
                pltpu.make_async_copy(zi_in.at[part], zi_v.at[part], in_sem.at[2 * n]),
                pltpu.make_async_copy(zt_in.at[part], zt_v.at[part], in_sem.at[2 * n + 1]),
            ]
        )
        for load in loads[-1]:
            load.start()
    ez_v[...] = jnp.zeros_like(ez_v)
    for n, l0 in enumerate(parts):
        for load in loads[n]:
            load.wait()
        for l in range(l0 + group - 1, l0 - 1, -1):
            for k in range(CELLS):
                s = zi_v[l, k] + zt_v[l, k] * ez_v[k]
                ez_v[k] = s
                tmp_v[l - l0, pl.ds(k, RUNS, stride=CELLS), :] = s
        for l in range(l0 + group - 1, l0 - 1, -1):
            out_v[l] = tmp_v[l - l0].T.reshape(CELLS, RUNS, 128)
        for q in range(RUNS):
            pltpu.make_async_copy(
                out_v.at[pl.ds(l0, group), :, q, :],
                out.at[pl.ds(l0, group), pl.ds(CELLS * q, CELLS), :],
                out_sem,
            ).start()
    pltpu.make_async_copy(out_v, out_v, out_sem).wait()


def body(*args):
    layers, cells_x, cells_y = args[0].shape
    nx, ny = lax.axis_size("gx"), lax.axis_size("gy")
    f32, i32 = jnp.float32, jnp.int32
    tile = pltpu.VMEM((layers, TILE, 128), f32)
    runs = pltpu.VMEM((layers, CELLS, RUNS, 128), f32)
    index = pltpu.VMEM((layers, CELLS, RUNS, 128), i32)
    layer = pltpu.VMEM((CELLS, RUNS, 128), f32)
    halo = pltpu.VMEM((2, layers, 128), f32)

    def rows(*shape):
        return pltpu.VMEM((*shape, 128), f32)

    hbm = pl.BlockSpec(memory_space=pltpu.HBM)
    smem = pl.BlockSpec(memory_space=pltpu.SMEM)
    shape = jax.ShapeDtypeStruct((layers, CELLS, RUNS, 128), f32)
    zi, zt = pl.pallas_call(
        runs_kernel,
        out_shape=(shape, shape),
        in_specs=[hbm, hbm, hbm, smem, smem, hbm, hbm, smem, hbm, smem],
        out_specs=(hbm, hbm),
        scratch_shapes=[
            runs,
            runs,
            index,
            index,
            pltpu.VMEM((CELLS, RUNS, 128), i32),
            index,
            runs,
            runs,
            runs,
            runs,
            tile,
            tile,
            tile,
            tile,
            runs,
            runs,
            runs,
            runs,
            runs,
            runs,
            runs,
            runs,
            runs,
            layer,
            layer,
            layer,
            layer,
            layer,
            halo,
            halo,
            halo,
            halo,
            *[rows(RUNS * layers)] * 5,
            rows(3 * layers),
            rows(nx, 3 * layers),
            rows(2 * layers),
            rows(nx, 2 * layers),
            rows(nx + 1, layers),
            rows(3 * layers // 2),
            rows(3 * layers // 2),
            rows(3 * layers // 2),
            rows(ny // 2, 3 * layers // 2),
            rows(layers),
            rows(layers),
            rows(layers),
            rows(ny // 2, layers),
            rows(ny // 2 + 1, layers // 2),
            rows(layers),
            rows(layers),
            rows(layers),
            rows(layers),
            pltpu.SemaphoreType.DMA((6,)),
            pltpu.SemaphoreType.DMA((2,)),
            pltpu.SemaphoreType.DMA((9,)),
            pltpu.SemaphoreType.DMA((9,)),
        ],
        compiler_params=pltpu.CompilerParams(
            collective_id=0, has_side_effects=True, vmem_limit_bytes=56 * 1024 * 1024
        ),
        cost_estimate=pl.CostEstimate(
            flops=100 * args[0].size, bytes_accessed=28 * args[0].size, transcendentals=0
        ),
        name="lines_xy",
    )(*args)
    return pl.pallas_call(
        layers_kernel,
        out_shape=jax.ShapeDtypeStruct(args[0].shape, f32),
        in_specs=[hbm, hbm],
        out_specs=hbm,
        scratch_shapes=[
            runs,
            runs,
            pltpu.VMEM((4, TILE, 128), f32),
            runs,
            layer,
            pltpu.SemaphoreType.DMA((8,)),
            pltpu.SemaphoreType.DMA,
        ],
        compiler_params=pltpu.CompilerParams(vmem_limit_bytes=62 * 1024 * 1024),
        cost_estimate=pl.CostEstimate(
            flops=2 * args[0].size, bytes_accessed=12 * args[0].size, transcendentals=0
        ),
        name="columns_z",
    )(zi, zt)


def solution(mesh):
    field = P(None, "gx", "gy")
    in_specs = (field, field, field, P(), P(), field, P("gx", "gy"), P(), field, P())
    return jax.shard_map(body, mesh=mesh, in_specs=in_specs, out_specs=field, check_vma=False)
```

```python
import jax
import jax.numpy as jnp
from jax import lax
from jax.experimental import pallas as pl
from jax.experimental.pallas import tpu as pltpu
from jax.sharding import PartitionSpec as P

MESH = pl.DeviceIdType.MESH
HELD = 2.0**100
CELLS = 16
RUNS = 8
TILE = CELLS * RUNS


def inverse(x):
    return pltpu.reciprocal(x, approx=True)


def order(count):
    steps = []
    stride = 1
    while stride < count:
        for node in range(stride - 1, count - 1, 2 * stride):
            steps.append((node, node - stride, node + stride))
        stride *= 2
    return steps


def plus(total, term):
    return term if total is None else total + term


def reduce_matrix(c, w):
    c, w, w_left, kept = list(c), list(w), None, {}
    for k, left, right in order(len(c)):
        inv = inverse(w[k] + (c[k] + c[right]))
        tl, tr = c[k] * inv, c[right] * inv
        c[right] = c[k] * tr
        if left < 0:
            w_left = plus(w_left, w[k] * tl)
        else:
            w[left] = w[left] + w[k] * tl
        w[right] = w[right] + w[k] * tr
        kept[k] = (inv, tl, tr)
    return c[-1], w[-1], w_left, kept


def reduce_rhs(b, kept):
    b, b_left, base = list(b), None, {}
    for k, left, right in order(len(b)):
        inv, tl, tr = kept(k)
        if left < 0:
            b_left = plus(b_left, b[k] * tl)
        else:
            b[left] = b[left] + b[k] * tl
        b[right] = b[right] + b[k] * tr
        base[k] = b[k] * inv
    return b[-1], b_left, base


def expand(count, base, tl, tr, s_left, s_last):
    s = {-1: s_left, count - 1: s_last}
    for k, left, right in reversed(order(count)):
        s[k] = base(k) + tl(k) * s[left] + tr(k) * s[right]
    return s


def take_out(c_left, c_right, w):
    inv = inverse(w + (c_left + c_right))
    tl, tr = c_left * inv, c_right * inv
    return c_left * tr, w * tl, w * tr, (inv, tl, tr)


def down(x):
    return pltpu.roll(x, 1, 0)


def up(x):
    return pltpu.roll(x, RUNS - 1, 0)


def looped(count, unroll, step):
    def body(i, _):
        step([i * unroll + u for u in range(unroll)])
        return 0

    lax.fori_loop(0, count // unroll, body, 0)


def runs_kernel(
    s_in,
    r_in,
    cls_in,
    k_tab,
    leak,
    well_in,
    rate_in,
    rate_tab,
    pit_in,
    level,
    zi_v,
    zt_v,
    s_v,
    w_v,
    cls_v,
    well_v,
    rate_v,
    pit_v,
    ra_v,
    xi_v,
    xl_v,
    xr_v,
    rat_v,
    st_v,
    wt_v,
    q_v,
    wr_v,
    ly_v,
    lz_v,
    fy_v,
    yi_v,
    yl_v,
    yr_v,
    pump_v,
    ez_v,
    flux_v,
    ra_c,
    s_c,
    lo_send,
    hi_send,
    lo_recv,
    hi_recv,
    node_w,
    node_c,
    node_e,
    node_b,
    node_g,
    xm_send,
    xm_recv,
    xr_send,
    xr_recv,
    xs_v,
    pm_send,
    pm_recv,
    ym_send,
    ym_recv,
    pr_send,
    pr_recv,
    yr_send,
    yr_recv,
    ys_v,
    pb_send,
    pb_recv,
    yl_end,
    yr_end,
    in_sem,
    send_sem,
    recv_sem,
):
    layers = s_in.shape[0]
    ix, iy = lax.axis_index("gx"), lax.axis_index("gy")
    nx, ny = lax.axis_size("gx"), lax.axis_size("gy")
    core, chip = lax.rem(iy, 2), iy // 2
    mate = {"gy": iy + 1 - 2 * core}
    halves = range(layers // 8)

    fields = [(cls_in, cls_v), (s_in, s_v), (r_in, w_v), (pit_in, pit_v), (well_in, well_v)]
    for n, (src, dst) in enumerate(fields):
        for q in range(RUNS):
            pltpu.make_async_copy(
                src.at[:, pl.ds(CELLS * q, CELLS), :], dst.at[:, :, q, :], in_sem.at[n]
            ).start()
    for q in range(RUNS):
        pltpu.make_async_copy(
            rate_in.at[pl.ds(CELLS * q, CELLS), :], rate_v.at[:, q, :], in_sem.at[5]
        ).start()

    def loaded(n):
        ref = fields[n][1] if n < 5 else rate_v
        pltpu.make_async_copy(ref, ref, in_sem.at[n]).wait()

    barrier = pltpu.get_barrier_semaphore()

    def greet(where):
        pl.semaphore_signal(barrier, inc=1, device_id=where, device_id_type=MESH)

    def greet_x(k, _):
        greet({"gx": lax.rem(ix + k, nx)})
        return 0

    def greet_y(k, _):
        greet({"gy": lax.rem(iy + 2 * k, ny)})
        return 0

    lax.fori_loop(1, nx, greet_x, 0)
    lax.fori_loop(1, ny // 2, greet_y, 0)
    greet({"gy": lax.rem(iy + 1, ny)})
    greet({"gy": lax.rem(iy + ny - 1, ny)})

    def remote(src, dst, n, where):
        return pltpu.make_async_remote_copy(
            src_ref=src,
            dst_ref=dst,
            send_sem=send_sem.at[n],
            recv_sem=recv_sem.at[n],
            device_id=where,
            device_id_type=MESH,
        )

    sub = lax.broadcasted_iota(jnp.int32, (RUNS, 128), 0)
    first, final = sub == 0, sub == RUNS - 1

    def at(l):
        return pl.ds(pl.multiple_of(l * RUNS, RUNS), RUNS)

    def turned(x):
        return x.reshape(TILE, 128).T

    def strided(ref, l):
        return [ref[l, pl.ds(n, RUNS, stride=CELLS), :] for n in range(CELLS)]

    ra_tab = [0.5 / jnp.full((RUNS, 128), k_tab[n], jnp.float32) for n in range(8)]
    ra_tab = [jnp.broadcast_to(t[:1], (TILE, 128)).reshape(CELLS, RUNS, 128) for t in ra_tab]
    loaded(0)
    loaded(1)

    def look(ls):
        ras = []
        for l in ls:
            cls = cls_v[l]
            odd, two, four = (cls & 1) != 0, (cls & 2) != 0, cls >= 4
            pairs = [jnp.where(odd, ra_tab[n + 1], ra_tab[n]) for n in (0, 2, 4, 6)]
            ras.append(
                jnp.where(
                    four,
                    jnp.where(two, pairs[3], pairs[2]),
                    jnp.where(two, pairs[1], pairs[0]),
                )
            )
        ss = [s_v[l] for l in ls]
        turned_ra = [turned(x) for x in ras]
        turned_s = [turned(x) for x in ss]
        for u, l in enumerate(ls):
            ra_v[l] = ras[u]
            rat_v[l] = turned_ra[u]
            st_v[l] = turned_s[u]

    looped(layers, 4, look)
    lo_send[0] = st_v[:, 0, :]
    lo_send[1] = rat_v[:, 0, :]
    hi_send[0] = st_v[:, TILE - 1, :]
    hi_send[1] = rat_v[:, TILE - 1, :]

    loaded(2)
    loaded(3)
    own_x = jnp.where(ix == 0, 1.0, 0.0)

    def weigh(ls):
        ws = []
        for l in ls:
            pit = pit_v[l] == 1
            w = jnp.where(pit, HELD, inverse(w_v[l]))
            ws.append(w)
            s_v[l] = w * jnp.where(pit, level[l], s_v[l])
        for u, l in enumerate(ls):
            ra, w = [ra_v[l, n] for n in range(CELLS)], [ws[u][n] for n in range(CELLS)]
            w_v[l] = ws[u]
            c = [inverse(ra[0] + jnp.where(first, own_x * ra[0], down(ra[15])))]
            c += [inverse(ra[n] + ra[n + 1]) for n in range(CELLS - 1)]
            c, w, e, kept = reduce_matrix(c, w)
            for k in kept:
                xi_v[l, k], xl_v[l, k], xr_v[l, k] = kept[k]
            node_w[at(l), :], node_c[at(l), :], node_e[at(l), :] = w, c, e

    looped(layers, 2, weigh)

    def nodes(ref, h):
        return [ref[pl.ds(n + 64 * h, 8, stride=RUNS), :] for n in range(RUNS)]

    def put(ref, n, h, x):
        ref[pl.ds(n + 64 * h, 8, stride=RUNS), :] = x

    def join(w, extra):
        return [w[n] + extra[n + 1] for n in range(RUNS - 1)] + [w[RUNS - 1]]

    def segment(h, c_end):
        extra = nodes(node_e, h)
        c, w, e, kept = reduce_matrix(nodes(node_c, h), join(nodes(node_w, h), extra))
        c, w_left, w_right, last = take_out(c, c_end, w)
        kept[RUNS - 1] = last
        return (c, extra[0] + e + w_left, w_right), kept

    def segment_rhs(h, kept):
        extra = nodes(node_g, h)
        b, g, base = reduce_rhs(join(nodes(node_b, h), extra), lambda k: kept[k])
        inv, tl, tr = kept[RUNS - 1]
        base[RUNS - 1] = b * inv
        return (extra[0] + g + b * tl, b * tr), base

    x_kept = []
    end_x = jnp.where(ix == nx - 1, 2.0, 1.0)
    for h in halves:
        values, kept = segment(h, inverse(end_x * ra_v[pl.ds(8 * h, 8), CELLS - 1, RUNS - 1, :]))
        for n, x in enumerate(values):
            xm_send[pl.ds(layers * n + 8 * h, 8), :] = x
        x_kept.append(kept)

    def gather_x(src, dst, n):
        def send(k, _):
            other = lax.rem(ix + k, nx)
            remote(src, dst.at[ix], n, {"gx": other}).start()
            return 0

        lax.fori_loop(1, nx, send, 0)
        dst[ix] = src[...]

    def gather_y(src, dst, n):
        def send(k, _):
            other = lax.rem(iy + 2 * k, ny)
            remote(src, dst.at[chip], n, {"gy": other}).start()
            return 0

        lax.fori_loop(1, ny // 2, send, 0)
        dst[chip] = src[...]

    def arrived(dst, n, count):
        ref = dst.at[pl.ds(0, count)]
        pltpu.make_async_copy(ref, ref, recv_sem.at[n]).wait()

    pl.semaphore_wait(barrier, nx + ny // 2)
    halos = [
        remote(lo_send, hi_recv, 0, {"gy": lax.rem(iy + ny - 1, ny)}),
        remote(hi_send, lo_recv, 1, {"gy": lax.rem(iy + 1, ny)}),
    ]
    for halo in halos:
        halo.start()
    gather_x(xm_send, xm_recv, 2)

    flux_v[...] = jnp.zeros_like(flux_v)
    own_y = jnp.where(iy == 0, 1.0, 0.0)
    for n in range(CELLS):
        ra_c[n] = rat_v[0, pl.ds(n, RUNS, stride=CELLS), :]
        s_c[n] = st_v[0, pl.ds(n, RUNS, stride=CELLS), :]

    def across(ls):
        ra = [ra_c[n] for n in range(CELLS)]
        s = [s_c[n] for n in range(CELLS)]
        for l in ls:
            above = jnp.minimum(l + 1, layers - 1)
            leak_l = jnp.where(l < layers - 1, leak[jnp.minimum(l, layers - 2)], 0.0)
            ra_up, s_up = strided(rat_v, above), strided(st_v, above)
            ra_before = down(ra[15])
            face = inverse(ra[0] + jnp.where(first, own_y * ra[0], ra_before))
            fy_v[l, 0] = face
            flux_left = jnp.where(first, 0.0, face * (s[0] - down(s[15])))
            flux = flux_left
            for n in range(CELLS):
                if n < CELLS - 1:
                    face = inverse(ra[n] + ra[n + 1])
                    fy_v[l, n + 1] = face
                    flux_next = face * (s[n + 1] - s[n])
                else:
                    flux_next = up(flux_left)
                ly = flux_next - flux
                flux = flux_next
                face_z = leak_l * inverse(ra[n] + ra_up[n])
                flux_z = face_z * (s_up[n] - s[n])
                lz = flux_z - flux_v[n]
                flux_v[n] = flux_z
                ly_v[l, n] = ly
                lz_v[l, n] = lz
                q_v[l, pl.ds(n, RUNS, stride=CELLS), :] = ly + lz
                zt_v[l, n] = face_z
            ra, s = ra_up, s_up
        for n in range(CELLS):
            ra_c[n], s_c[n] = ra[n], s[n]

    looped(layers, 2, across)

    loaded(4)
    loaded(5)
    rate = rate_v[...]
    pump = jnp.full(rate.shape, rate_tab[0], jnp.float32)
    for n in range(1, 16):
        pump = jnp.where(rate == n, rate_tab[n], pump)
    pump_v[...] = pump

    for halo in halos:
        halo.wait_recv()
    at_lo, at_hi = iy == 0, iy == ny - 1
    s_lo = jnp.where(at_lo, 0.0, lo_recv[0])
    ra_lo = jnp.where(at_lo, lo_send[1], lo_recv[1])
    s_hi = jnp.where(at_hi, 0.0, hi_recv[0])
    ra_hi = jnp.where(at_hi, hi_send[1], hi_recv[1])
    flux_lo = inverse(ra_lo + lo_send[1]) * (lo_send[0] - s_lo)
    flux_hi = inverse(ra_hi + hi_send[1]) * (s_hi - hi_send[0])
    q_v[:, 0, :] = q_v[:, 0, :] - flux_lo
    q_v[:, TILE - 1, :] = q_v[:, TILE - 1, :] + flux_hi
    ly_v[:, 0, 0, :] = ly_v[:, 0, 0, :] - flux_lo
    ly_v[:, CELLS - 1, RUNS - 1, :] = ly_v[:, CELLS - 1, RUNS - 1, :] + flux_hi

    def runs_x(ls):
        qs = [q_v[l].T.reshape(CELLS, RUNS, 128) for l in ls]
        bs = []
        for u, l in enumerate(ls):
            pumped = well_v[l].astype(jnp.float32) * pump_v[...]
            bs.append(s_v[l] + (qs[u] + pumped))
        for u, l in enumerate(ls):
            b, g, base = reduce_rhs(
                [bs[u][n] for n in range(CELLS)], lambda k: (xi_v[l, k], xl_v[l, k], xr_v[l, k])
            )
            for k in base:
                xi_v[l, k] = base[k]
            node_b[at(l), :], node_g[at(l), :] = b, g

    looped(layers, 4, runs_x)

    x_base = []
    for h in halves:
        values, base = segment_rhs(h, x_kept[h])
        for n, x in enumerate(values):
            xr_send[pl.ds(layers * n + 8 * h, 8), :] = x
        x_base.append(base)
    gather_x(xr_send, xr_recv, 3)

    ez_v[...] = jnp.zeros_like(ez_v)

    def runs_y(ls):
        wts = [turned(w_v[l]) for l in ls]
        for u, l in enumerate(ls):
            wt_v[l] = wts[u]
        for l in ls:
            wt = strided(wt_v, l)
            c, w, e, kept = reduce_matrix([fy_v[l, n] for n in range(CELLS)], wt)
            for k in kept:
                yi_v[l, k], yl_v[l, k], yr_v[l, k] = kept[k]
            node_w[at(l), :], node_c[at(l), :], node_e[at(l), :] = w, c, e
            for n in range(CELLS):
                wr_v[l, n] = wt[n]
                e = wt[n] + ez_v[n]
                inv = inverse(e + zt_v[l, n])
                t = zt_v[l, n] * inv
                zt_v[l, n] = t
                zi_v[l, n] = inv
                ez_v[n] = e * t

    looped(layers, 2, runs_y)

    is_a = core == 0

    def mine(pair):
        return jnp.where(is_a, pair[0], pair[1])

    def theirs(pair):
        return jnp.where(is_a, pair[1], pair[0])

    y_kept, y_values = [], []
    end_y = jnp.where(iy == ny - 1, 2.0, 1.0)
    for h in halves:
        values, kept = segment(h, inverse(end_y * hi_send[1, pl.ds(8 * h, 8), :]))
        y_values.append(values)
        y_kept.append(kept)
    for n, pair in enumerate(zip(*y_values)):
        pm_send[pl.ds(8 * n, 8), :] = theirs(pair)
    pm_copy = remote(pm_send, pm_recv, 4, mate)
    pm_copy.start()
    own = [mine(pair) for pair in zip(*y_values)]
    pm_copy.wait_recv()
    other = [pm_recv[pl.ds(8 * n, 8), :] for n in range(3)]
    c_a, c_b = mine((own[0], other[0])), theirs((own[0], other[0]))
    el_a, el_b = mine((own[1], other[1])), theirs((own[1], other[1]))
    er_a, er_b = mine((own[2], other[2])), theirs((own[2], other[2]))
    c, w_left, w_right, mid = take_out(c_a, c_b, er_a + el_b)
    for n, x in enumerate((c, el_a + w_left, er_b + w_right)):
        ym_send[pl.ds(8 * n, 8), :] = x
    gather_y(ym_send, ym_recv, 5)

    arrived(xm_recv, 2, nx - 1)
    zero = jnp.zeros((RUNS, 128), jnp.float32)

    def rows(ref, d, n, h):
        return ref[d, pl.ds(layers * n + 8 * h, 8), :]

    x_chain = []
    for h in halves:
        c = [rows(xm_recv, d, 0, h) for d in range(nx)]
        w = [rows(xm_recv, d, 2, h) + rows(xm_recv, d + 1, 1, h) for d in range(nx - 1)]
        x_chain.append(reduce_matrix(c, w + [zero])[3])

    arrived(xr_recv, 3, nx - 1)
    for h in halves:
        kept = x_chain[h]
        b = [rows(xr_recv, d, 1, h) + rows(xr_recv, d + 1, 0, h) for d in range(nx - 1)]
        base = reduce_rhs(b + [zero], lambda k: kept[k])[2]
        s = expand(
            nx, lambda k: base[k], lambda k: kept[k][1], lambda k: kept[k][2], zero, zero
        )
        for d in range(-1, nx):
            xs_v[d + 1, pl.ds(8 * h, 8), :] = s[d]

    def ends(s_left, s_right, h, base, kept):
        inv, tl, tr = kept[RUNS - 1]
        s_last = base[RUNS - 1] + tl * s_left + tr * s_right
        s = expand(
            RUNS, lambda k: base[k], lambda k: kept[k][1], lambda k: kept[k][2], s_left, s_last
        )
        for n in range(RUNS):
            put(node_w, n, h, s[n])
            put(node_c, n, h, s[n - 1])

    for h in halves:
        part = pl.ds(8 * h, 8)
        ends(xs_v[ix, part, :], xs_v[ix + 1, part, :], h, x_base[h], x_kept[h])

    def fill(l, base, tl, tr):
        s = expand(
            CELLS,
            lambda k: base[l, k],
            lambda k: tl[l, k],
            lambda k: tr[l, k],
            node_c[at(l), :],
            node_w[at(l), :],
        )
        return [s[n] for n in range(CELLS)]

    def fill_x(ls):
        lines = [turned(jnp.stack(fill(l, xi_v, xl_v, xr_v))) for l in ls]
        for u, l in enumerate(ls):
            q_v[l] = lines[u]
        for l in ls:
            sx = strided(q_v, l)
            b = [wr_v[l, n] * sx[n] - ly_v[l, n] for n in range(CELLS)]
            b, g, base = reduce_rhs(b, lambda k: (yi_v[l, k], yl_v[l, k], yr_v[l, k]))
            for k in base:
                yi_v[l, k] = base[k]
            node_b[at(l), :], node_g[at(l), :] = b, g

    looped(layers, 4, fill_x)

    y_base, y_values = [], []
    for h in halves:
        values, base = segment_rhs(h, y_kept[h])
        y_values.append(values)
        y_base.append(base)
    for n, pair in enumerate(zip(*y_values)):
        pr_send[pl.ds(8 * n, 8), :] = theirs(pair)
    pr_copy = remote(pr_send, pr_recv, 6, mate)
    pr_copy.start()
    own = [mine(pair) for pair in zip(*y_values)]

    arrived(ym_recv, 5, ny // 2 - 1)
    chips = ny // 2
    c = [ym_recv[d, pl.ds(0, 8), :] for d in range(chips)]
    w = [ym_recv[d, pl.ds(16, 8), :] + ym_recv[d + 1, pl.ds(8, 8), :] for d in range(chips - 1)]
    y_chain = reduce_matrix(c, w + [zero])[3]

    pr_copy.wait_recv()
    other = [pr_recv[pl.ds(8 * n, 8), :] for n in range(2)]
    gl_a, gl_b = mine((own[0], other[0])), theirs((own[0], other[0]))
    gr_a, gr_b = mine((own[1], other[1])), theirs((own[1], other[1]))
    b_mid = gr_a + gl_b
    inv_mid, tl_mid, tr_mid = mid
    yr_send[pl.ds(0, 8), :] = gl_a + b_mid * tl_mid
    yr_send[pl.ds(8, 8), :] = gr_b + b_mid * tr_mid
    gather_y(yr_send, yr_recv, 7)
    arrived(yr_recv, 7, chips - 1)
    b = [yr_recv[d, pl.ds(8, 8), :] + yr_recv[d + 1, pl.ds(0, 8), :] for d in range(chips - 1)]
    base = reduce_rhs(b + [zero], lambda k: y_chain[k])[2]
    s = expand(
        chips, lambda k: base[k], lambda k: y_chain[k][1], lambda k: y_chain[k][2], zero, zero
    )
    for d in range(-1, chips):
        ys_v[d + 1] = s[d]
    s_left, s_right = ys_v[chip], ys_v[chip + 1]
    s_mid = b_mid * inv_mid + tl_mid * s_left + tr_mid * s_right
    pb_send[pl.ds(0, 8), :] = theirs((s_left, s_mid))
    pb_send[pl.ds(8, 8), :] = theirs((s_mid, s_right))
    pb_copy = remote(pb_send, pb_recv, 8, mate)
    pb_copy.start()
    yl_end[at(core), :] = mine((s_left, s_mid))
    yr_end[at(core), :] = mine((s_mid, s_right))
    pb_copy.wait_recv()
    yl_end[at(1 - core), :] = pb_recv[pl.ds(0, 8), :]
    yr_end[at(1 - core), :] = pb_recv[pl.ds(8, 8), :]
    for h in halves:
        part = pl.ds(8 * h, 8)
        ends(yl_end[part, :], yr_end[part, :], h, y_base[h], y_kept[h])

    ez_v[...] = jnp.zeros_like(ez_v)

    def fill_y(ls):
        lines = [fill(l, yi_v, yl_v, yr_v) for l in ls]
        for u, l in enumerate(ls):
            for n in range(CELLS):
                b = wr_v[l, n] * lines[u][n] - lz_v[l, n] + ez_v[n]
                ez_v[n] = b * zt_v[l, n]
                zi_v[l, n] = b * zi_v[l, n]

    looped(layers, 2, fill_y)

    for halo in halos:
        halo.wait_send()
    for copy in (pm_copy, pr_copy, pb_copy):
        copy.wait_send()
    for ref, n, count in ((xm_recv, 2, nx), (xr_recv, 3, nx), (ym_recv, 5, chips), (yr_recv, 7, chips)):
        sent = ref.at[pl.ds(0, count - 1)]
        pltpu.make_async_copy(sent, sent, send_sem.at[n]).wait()


def layers_kernel(zi_v, zt_v, out, tmp_v, out_v, ez_v, out_sem):
    layers = zi_v.shape[0]
    group = 4
    ez_v[...] = jnp.zeros_like(ez_v)
    for l0 in range(layers - group, -1, -group):
        for l in range(l0 + group - 1, l0 - 1, -1):
            for k in range(CELLS):
                s = zi_v[l, k] + zt_v[l, k] * ez_v[k]
                ez_v[k] = s
                tmp_v[l - l0, pl.ds(k, RUNS, stride=CELLS), :] = s
        for l in range(l0 + group - 1, l0 - 1, -1):
            out_v[l] = tmp_v[l - l0].T.reshape(CELLS, RUNS, 128)
        for q in range(RUNS):
            pltpu.make_async_copy(
                out_v.at[pl.ds(l0, group), :, q, :],
                out.at[pl.ds(l0, group), pl.ds(CELLS * q, CELLS), :],
                out_sem,
            ).start()
    pltpu.make_async_copy(out_v, out_v, out_sem).wait()


def body(*args):
    layers, cells_x, cells_y = args[0].shape
    nx, ny = lax.axis_size("gx"), lax.axis_size("gy")
    f32, i32 = jnp.float32, jnp.int32
    tile = pltpu.VMEM((layers, TILE, 128), f32)
    runs = pltpu.VMEM((layers, CELLS, RUNS, 128), f32)
    index = pltpu.VMEM((layers, CELLS, RUNS, 128), i32)
    layer = pltpu.VMEM((CELLS, RUNS, 128), f32)
    halo = pltpu.VMEM((2, layers, 128), f32)

    def rows(*shape):
        return pltpu.VMEM((*shape, 128), f32)

    hbm = pl.BlockSpec(memory_space=pltpu.HBM)
    smem = pl.BlockSpec(memory_space=pltpu.SMEM)
    vmem = pl.BlockSpec(memory_space=pltpu.VMEM)
    shape = pltpu.VMEM((layers, CELLS, RUNS, 128), f32)
    zi, zt = pl.pallas_call(
        runs_kernel,
        out_shape=(shape, shape),
        in_specs=[hbm, hbm, hbm, smem, smem, hbm, hbm, smem, hbm, smem],
        out_specs=(vmem, vmem),
        scratch_shapes=[
            runs,
            runs,
            index,
            index,
            pltpu.VMEM((CELLS, RUNS, 128), i32),
            index,
            runs,
            runs,
            runs,
            runs,
            tile,
            tile,
            tile,
            tile,
            runs,
            runs,
            runs,
            runs,
            runs,
            runs,
            runs,
            layer,
            layer,
            layer,
            layer,
            layer,
            halo,
            halo,
            halo,
            halo,
            *[rows(RUNS * layers)] * 5,
            rows(3 * layers),
            rows(nx, 3 * layers),
            rows(2 * layers),
            rows(nx, 2 * layers),
            rows(nx + 1, layers),
            rows(3 * layers // 2),
            rows(3 * layers // 2),
            rows(3 * layers // 2),
            rows(ny // 2, 3 * layers // 2),
            rows(layers),
            rows(layers),
            rows(layers),
            rows(ny // 2, layers),
            rows(ny // 2 + 1, layers // 2),
            rows(layers),
            rows(layers),
            rows(layers),
            rows(layers),
            pltpu.SemaphoreType.DMA((6,)),
            pltpu.SemaphoreType.DMA((9,)),
            pltpu.SemaphoreType.DMA((9,)),
        ],
        compiler_params=pltpu.CompilerParams(
            collective_id=0, has_side_effects=True, vmem_limit_bytes=56 * 1024 * 1024
        ),
        cost_estimate=pl.CostEstimate(
            flops=100 * args[0].size, bytes_accessed=28 * args[0].size, transcendentals=0
        ),
        name="lines_xy",
    )(*args)
    return pl.pallas_call(
        layers_kernel,
        out_shape=jax.ShapeDtypeStruct(args[0].shape, f32),
        in_specs=[vmem, vmem],
        out_specs=hbm,
        scratch_shapes=[
            pltpu.VMEM((4, TILE, 128), f32),
            runs,
            layer,
            pltpu.SemaphoreType.DMA,
        ],
        compiler_params=pltpu.CompilerParams(vmem_limit_bytes=32 * 1024 * 1024),
        cost_estimate=pl.CostEstimate(
            flops=2 * args[0].size, bytes_accessed=12 * args[0].size, transcendentals=0
        ),
        name="columns_z",
    )(zi, zt)


def solution(mesh):
    field = P(None, "gx", "gy")
    in_specs = (field, field, field, P(), P(), field, P("gx", "gy"), P(), field, P())
    return jax.shard_map(body, mesh=mesh, in_specs=in_specs, out_specs=field, check_vma=False)
```

```python
import jax
import jax.numpy as jnp
from jax import lax
from jax.experimental import pallas as pl
from jax.experimental.pallas import tpu as pltpu
from jax.sharding import PartitionSpec as P

MESH = pl.DeviceIdType.MESH
HELD = 2.0**100
CELLS = 16
RUNS = 8
TILE = CELLS * RUNS
SIDE = 4


def far_first(steps, size):
    return sorted(steps, key=lambda step: -sum(min(d, n - d) for d, n in zip(step, size)))


def inverse(x):
    return pltpu.reciprocal(x, approx=True)


def order(count):
    steps = []
    stride = 1
    while stride < count:
        for node in range(stride - 1, count - 1, 2 * stride):
            steps.append((node, node - stride, node + stride))
        stride *= 2
    return steps


def plus(total, term):
    return term if total is None else total + term


def reduce_matrix(c, w):
    c, w, w_left, kept = list(c), list(w), None, {}
    for k, left, right in order(len(c)):
        inv = inverse(w[k] + (c[k] + c[right]))
        tl, tr = c[k] * inv, c[right] * inv
        c[right] = c[k] * tr
        if left < 0:
            w_left = plus(w_left, w[k] * tl)
        else:
            w[left] = w[left] + w[k] * tl
        w[right] = w[right] + w[k] * tr
        kept[k] = (inv, tl, tr)
    return c[-1], w[-1], w_left, kept


def reduce_rhs(b, kept):
    b, b_left, base = list(b), None, {}
    for k, left, right in order(len(b)):
        inv, tl, tr = kept(k)
        if left < 0:
            b_left = plus(b_left, b[k] * tl)
        else:
            b[left] = b[left] + b[k] * tl
        b[right] = b[right] + b[k] * tr
        base[k] = b[k] * inv
    return b[-1], b_left, base


def expand(count, base, tl, tr, s_left, s_last):
    s = {-1: s_left, count - 1: s_last}
    for k, left, right in reversed(order(count)):
        s[k] = base(k) + tl(k) * s[left] + tr(k) * s[right]
    return s


def take_out(c_left, c_right, w):
    inv = inverse(w + (c_left + c_right))
    tl, tr = c_left * inv, c_right * inv
    return c_left * tr, w * tl, w * tr, (inv, tl, tr)


def down(x):
    return pltpu.roll(x, 1, 0)


def up(x):
    return pltpu.roll(x, RUNS - 1, 0)


def looped(count, unroll, step, start=0):
    def body(i, _):
        step([start + i * unroll + u for u in range(unroll)])
        return 0

    lax.fori_loop(0, count // unroll, body, 0)


def runs_kernel(
    s_in,
    r_in,
    cls_in,
    k_tab,
    leak,
    well_in,
    rate_in,
    rate_tab,
    pit_in,
    level,
    zi_v,
    zt_v,
    s_v,
    w_v,
    cls_v,
    well_v,
    rate_v,
    pit_v,
    ra_v,
    xi_v,
    xl_v,
    xr_v,
    rat_v,
    st_v,
    wt_v,
    q_v,
    wr_v,
    ly_v,
    lz_v,
    fy_v,
    yi_v,
    yl_v,
    yr_v,
    pump_v,
    ez_v,
    flux_v,
    ra_c,
    s_c,
    lo_send,
    hi_send,
    lo_recv,
    hi_recv,
    node_w,
    node_c,
    node_e,
    node_b,
    node_g,
    xm_send,
    xm_recv,
    xr_send,
    xr_recv,
    xs_v,
    pm_send,
    pm_recv,
    ym_send,
    ym_recv,
    pr_send,
    pr_recv,
    yr_send,
    yr_recv,
    ys_v,
    in_sem,
    send_sem,
    recv_sem,
):
    layers = s_in.shape[0]
    ix, iy = lax.axis_index("gx"), lax.axis_index("gy")
    nx, ny = lax.axis_size("gx"), lax.axis_size("gy")
    core, chip = lax.rem(iy, 2), iy // 2
    mate = {"gy": iy + 1 - 2 * core}
    halves = range(layers // 8)

    sides = (nx // SIDE, SIDE)
    steps = [(p, q) for p in range(sides[0]) for q in range(sides[1])][1:]
    along_x = [
        lax.rem(ix // SIDE + p, sides[0]) * SIDE + lax.rem(lax.rem(ix, SIDE) + q, SIDE)
        for p, q in far_first(steps, sides)
    ]
    chips = ny // 2
    steps = [(p,) for p in range(1, chips)]
    along_y = [lax.rem(iy + 2 * p, ny) for (p,) in far_first(steps, (chips,))]
    before, after = lax.rem(iy + ny - 1, ny), lax.rem(iy + 1, ny)

    barrier = pltpu.get_barrier_semaphore()
    greeted = [{"gx": d} for d in along_x] + [{"gy": d} for d in along_y + [before, after]]
    for where in greeted:
        pl.semaphore_signal(barrier, inc=1, device_id=where, device_id_type=MESH)

    fields = [(cls_in, cls_v), (s_in, s_v), (r_in, w_v), (pit_in, pit_v), (well_in, well_v)]
    for n, (src, dst) in enumerate(fields):
        for q in range(RUNS):
            pltpu.make_async_copy(
                src.at[:, pl.ds(CELLS * q, CELLS), :], dst.at[:, :, q, :], in_sem.at[n]
            ).start()
    for q in range(RUNS):
        pltpu.make_async_copy(
            rate_in.at[pl.ds(CELLS * q, CELLS), :], rate_v.at[:, q, :], in_sem.at[5]
        ).start()

    def loaded(n):
        ref = fields[n][1] if n < 5 else rate_v
        pltpu.make_async_copy(ref, ref, in_sem.at[n]).wait()

    def remote(src, dst, n, where):
        return pltpu.make_async_remote_copy(
            src_ref=src,
            dst_ref=dst,
            send_sem=send_sem.at[n],
            recv_sem=recv_sem.at[n],
            device_id=where,
            device_id_type=MESH,
        )

    sub = lax.broadcasted_iota(jnp.int32, (RUNS, 128), 0)
    first, final = sub == 0, sub == RUNS - 1

    def at(l):
        return pl.ds(pl.multiple_of(l * RUNS, RUNS), RUNS)

    def turned(x):
        return x.reshape(TILE, 128).T

    def strided(ref, l):
        return [ref[l, pl.ds(n, RUNS, stride=CELLS), :] for n in range(CELLS)]

    ra_tab = [0.5 / jnp.full((RUNS, 128), k_tab[n], jnp.float32) for n in range(8)]
    ra_tab = [jnp.broadcast_to(t[:1], (TILE, 128)).reshape(CELLS, RUNS, 128) for t in ra_tab]
    loaded(0)
    loaded(1)

    def look(ls):
        ras = []
        for l in ls:
            cls = cls_v[l]
            odd, two, four = (cls & 1) != 0, (cls & 2) != 0, cls >= 4
            pairs = [jnp.where(odd, ra_tab[n + 1], ra_tab[n]) for n in (0, 2, 4, 6)]
            ras.append(
                jnp.where(
                    four,
                    jnp.where(two, pairs[3], pairs[2]),
                    jnp.where(two, pairs[1], pairs[0]),
                )
            )
        ss = [s_v[l] for l in ls]
        turned_ra = [turned(x) for x in ras]
        turned_s = [turned(x) for x in ss]
        for u, l in enumerate(ls):
            ra_v[l] = ras[u]
            rat_v[l] = turned_ra[u]
            st_v[l] = turned_s[u]

    looped(layers, 4, look)
    lo_send[0] = st_v[:, 0, :]
    lo_send[1] = rat_v[:, 0, :]
    hi_send[0] = st_v[:, TILE - 1, :]
    hi_send[1] = rat_v[:, TILE - 1, :]

    loaded(2)
    loaded(3)
    own_x = jnp.where(ix == 0, 1.0, 0.0)

    def weigh(ls):
        ws = []
        for l in ls:
            pit = pit_v[l] == 1
            w = jnp.where(pit, HELD, inverse(w_v[l]))
            ws.append(w)
            s_v[l] = w * jnp.where(pit, level[l], s_v[l])
        for u, l in enumerate(ls):
            ra, w = [ra_v[l, n] for n in range(CELLS)], [ws[u][n] for n in range(CELLS)]
            w_v[l] = ws[u]
            c = [inverse(ra[0] + jnp.where(first, own_x * ra[0], down(ra[15])))]
            c += [inverse(ra[n] + ra[n + 1]) for n in range(CELLS - 1)]
            c, w, e, kept = reduce_matrix(c, w)
            for k in kept:
                xi_v[l, k], xl_v[l, k], xr_v[l, k] = kept[k]
            node_w[at(l), :], node_c[at(l), :], node_e[at(l), :] = w, c, e

    looped(layers, 4, weigh)

    def nodes(ref, h):
        return [ref[pl.ds(n + 64 * h, 8, stride=RUNS), :] for n in range(RUNS)]

    def put(ref, n, h, x):
        ref[pl.ds(n + 64 * h, 8, stride=RUNS), :] = x

    def join(w, extra):
        return [w[n] + extra[n + 1] for n in range(RUNS - 1)] + [w[RUNS - 1]]

    def segment(h, c_end):
        extra = nodes(node_e, h)
        c, w, e, kept = reduce_matrix(nodes(node_c, h), join(nodes(node_w, h), extra))
        c, w_left, w_right, last = take_out(c, c_end, w)
        kept[RUNS - 1] = last
        return (c, extra[0] + e + w_left, w_right), kept

    def segment_rhs(h, kept):
        extra = nodes(node_g, h)
        b, g, base = reduce_rhs(join(nodes(node_b, h), extra), lambda k: kept[k])
        inv, tl, tr = kept[RUNS - 1]
        base[RUNS - 1] = b * inv
        return (extra[0] + g + b * tl, b * tr), base

    x_kept = []
    end_x = jnp.where(ix == nx - 1, 2.0, 1.0)
    for h in halves:
        values, kept = segment(h, inverse(end_x * ra_v[pl.ds(8 * h, 8), CELLS - 1, RUNS - 1, :]))
        for n, x in enumerate(values):
            xm_send[pl.ds(layers * n + 8 * h, 8), :] = x
        x_kept.append(kept)

    def gather_x(src, dst, n):
        for other in along_x:
            remote(src, dst.at[ix], n, {"gx": other}).start()
        dst[ix] = src[...]

    def gather_y(src, dst, n):
        for other in along_y:
            remote(src, dst.at[chip], n, {"gy": other}).start()
        dst[chip] = src[...]

    def arrived(dst, n, count):
        ref = dst.at[pl.ds(0, count)]
        pltpu.make_async_copy(ref, ref, recv_sem.at[n]).wait()

    pl.semaphore_wait(barrier, len(greeted))
    halos = [
        remote(lo_send, hi_recv, 0, {"gy": before}),
        remote(hi_send, lo_recv, 1, {"gy": after}),
    ]
    for halo in halos:
        halo.start()
    gather_x(xm_send, xm_recv, 2)

    flux_v[...] = jnp.zeros_like(flux_v)
    own_y = jnp.where(iy == 0, 1.0, 0.0)
    for n in range(CELLS):
        ra_c[n] = rat_v[0, pl.ds(n, RUNS, stride=CELLS), :]
        s_c[n] = st_v[0, pl.ds(n, RUNS, stride=CELLS), :]

    def across(ls):
        ra = [ra_c[n] for n in range(CELLS)]
        s = [s_c[n] for n in range(CELLS)]
        for l in ls:
            above = jnp.minimum(l + 1, layers - 1)
            leak_l = jnp.where(l < layers - 1, leak[jnp.minimum(l, layers - 2)], 0.0)
            ra_up, s_up = strided(rat_v, above), strided(st_v, above)
            ra_before = down(ra[15])
            face = inverse(ra[0] + jnp.where(first, own_y * ra[0], ra_before))
            fy_v[l, 0] = face
            flux_left = jnp.where(first, 0.0, face * (s[0] - down(s[15])))
            flux = flux_left
            for n in range(CELLS):
                if n < CELLS - 1:
                    face = inverse(ra[n] + ra[n + 1])
                    fy_v[l, n + 1] = face
                    flux_next = face * (s[n + 1] - s[n])
                else:
                    flux_next = up(flux_left)
                ly = flux_next - flux
                flux = flux_next
                face_z = leak_l * inverse(ra[n] + ra_up[n])
                flux_z = face_z * (s_up[n] - s[n])
                lz = flux_z - flux_v[n]
                flux_v[n] = flux_z
                ly_v[l, n] = ly
                lz_v[l, n] = lz
                q_v[l, pl.ds(n, RUNS, stride=CELLS), :] = ly + lz
                zt_v[l, n] = face_z
            ra, s = ra_up, s_up
        for n in range(CELLS):
            ra_c[n], s_c[n] = ra[n], s[n]

    looped(layers, 4, across)

    loaded(4)
    loaded(5)
    rate = rate_v[...]
    pump = jnp.full(rate.shape, rate_tab[0], jnp.float32)
    for n in range(1, 16):
        pump = jnp.where(rate == n, rate_tab[n], pump)
    pump_v[...] = pump

    for halo in halos:
        halo.wait_recv()
    at_lo, at_hi = iy == 0, iy == ny - 1
    s_lo = jnp.where(at_lo, 0.0, lo_recv[0])
    ra_lo = jnp.where(at_lo, lo_send[1], lo_recv[1])
    s_hi = jnp.where(at_hi, 0.0, hi_recv[0])
    ra_hi = jnp.where(at_hi, hi_send[1], hi_recv[1])
    flux_lo = inverse(ra_lo + lo_send[1]) * (lo_send[0] - s_lo)
    flux_hi = inverse(ra_hi + hi_send[1]) * (s_hi - hi_send[0])
    q_v[:, 0, :] = q_v[:, 0, :] - flux_lo
    q_v[:, TILE - 1, :] = q_v[:, TILE - 1, :] + flux_hi
    ly_v[:, 0, 0, :] = ly_v[:, 0, 0, :] - flux_lo
    ly_v[:, CELLS - 1, RUNS - 1, :] = ly_v[:, CELLS - 1, RUNS - 1, :] + flux_hi

    def runs_x(ls):
        qs = [q_v[l].T.reshape(CELLS, RUNS, 128) for l in ls]
        bs = []
        for u, l in enumerate(ls):
            pumped = well_v[l].astype(jnp.float32) * pump_v[...]
            bs.append(s_v[l] + (qs[u] + pumped))
        for u, l in enumerate(ls):
            b, g, base = reduce_rhs(
                [bs[u][n] for n in range(CELLS)], lambda k: (xi_v[l, k], xl_v[l, k], xr_v[l, k])
            )
            for k in base:
                xi_v[l, k] = base[k]
            node_b[at(l), :], node_g[at(l), :] = b, g

    x_base = []
    for h in halves:
        looped(8, 4, runs_x, 8 * h)
        values, base = segment_rhs(h, x_kept[h])
        for n, x in enumerate(values):
            xr_send[h, pl.ds(8 * n, 8), :] = x
        x_base.append(base)
        gather_x(xr_send.at[h], xr_recv.at[h], 3 + h)

    ez_v[...] = jnp.zeros_like(ez_v)

    def runs_y(ls):
        wts = [turned(w_v[l]) for l in ls]
        for u, l in enumerate(ls):
            wt_v[l] = wts[u]
        for l in ls:
            wt = strided(wt_v, l)
            c, w, e, kept = reduce_matrix([fy_v[l, n] for n in range(CELLS)], wt)
            for k in kept:
                yi_v[l, k], yl_v[l, k], yr_v[l, k] = kept[k]
            node_w[at(l), :], node_c[at(l), :], node_e[at(l), :] = w, c, e
            for n in range(CELLS):
                wr_v[l, n] = wt[n]
                e = wt[n] + ez_v[n]
                inv = inverse(e + zt_v[l, n])
                t = zt_v[l, n] * inv
                zt_v[l, n] = t
                zi_v[l, n] = inv
                ez_v[n] = e * t

    looped(layers, 4, runs_y)

    is_a = core == 0

    def mine(pair):
        return jnp.where(is_a, pair[0], pair[1])

    def theirs(pair):
        return jnp.where(is_a, pair[1], pair[0])

    y_kept, y_values = [], []
    end_y = jnp.where(iy == ny - 1, 2.0, 1.0)
    for h in halves:
        values, kept = segment(h, inverse(end_y * hi_send[1, pl.ds(8 * h, 8), :]))
        y_values.append(values)
        y_kept.append(kept)
    for h in halves:
        for n, x in enumerate(y_values[h]):
            pm_send[pl.ds(layers * n + 8 * h, 8), :] = x
    pm_copy = remote(pm_send, pm_recv, 5, mate)
    pm_copy.start()
    pm_copy.wait_recv()

    def sides_of(own, other):
        return mine((own, other)), theirs((own, other))

    mids = []
    for h in halves:
        other = [pm_recv[pl.ds(layers * n + 8 * h, 8), :] for n in range(3)]
        c, e, w = [sides_of(x, y) for x, y in zip(y_values[h], other)]
        joined, w_left, w_right, mid = take_out(c[0], c[1], w[0] + e[1])
        for n, x in enumerate((joined, e[0] + w_left, w[1] + w_right)):
            ym_send[pl.ds(layers * n + 8 * h, 8), :] = x
        mids.append(mid)
    gather_y(ym_send, ym_recv, 6)

    arrived(xm_recv, 2, nx - 1)
    zero = jnp.zeros((RUNS, 128), jnp.float32)

    def rows(ref, d, n, h):
        return ref[d, pl.ds(layers * n + 8 * h, 8), :]

    x_chain = []
    for h in halves:
        c = [rows(xm_recv, d, 0, h) for d in range(nx)]
        w = [rows(xm_recv, d, 2, h) + rows(xm_recv, d + 1, 1, h) for d in range(nx - 1)]
        x_chain.append(reduce_matrix(c, w + [zero])[3])

    def ends(s_left, s_right, h, base, kept):
        inv, tl, tr = kept[RUNS - 1]
        s_last = base[RUNS - 1] + tl * s_left + tr * s_right
        s = expand(
            RUNS, lambda k: base[k], lambda k: kept[k][1], lambda k: kept[k][2], s_left, s_last
        )
        for n in range(RUNS):
            put(node_w, n, h, s[n])
            put(node_c, n, h, s[n - 1])

    def fill(l, base, tl, tr):
        s = expand(
            CELLS,
            lambda k: base[l, k],
            lambda k: tl[l, k],
            lambda k: tr[l, k],
            node_c[at(l), :],
            node_w[at(l), :],
        )
        return [s[n] for n in range(CELLS)]

    def fill_x(ls):
        lines = [turned(jnp.stack(fill(l, xi_v, xl_v, xr_v))) for l in ls]
        for u, l in enumerate(ls):
            q_v[l] = lines[u]
        for l in ls:
            sx = strided(q_v, l)
            b = [wr_v[l, n] * sx[n] - ly_v[l, n] for n in range(CELLS)]
            b, g, base = reduce_rhs(b, lambda k: (yi_v[l, k], yl_v[l, k], yr_v[l, k]))
            for k in base:
                yi_v[l, k] = base[k]
            node_b[at(l), :], node_g[at(l), :] = b, g

    y_base, y_own, pr_copies = [], [], []
    for h in halves:
        arrived(xr_recv.at[h], 3 + h, nx - 1)
        got = xr_recv.at[h]
        kept = x_chain[h]
        b = [got[d, pl.ds(8, 8), :] + got[d + 1, pl.ds(0, 8), :] for d in range(nx - 1)]
        base = reduce_rhs(b + [zero], lambda k: kept[k])[2]
        s = expand(
            nx, lambda k: base[k], lambda k: kept[k][1], lambda k: kept[k][2], zero, zero
        )
        for d in range(-1, nx):
            xs_v[d + 1, pl.ds(8 * h, 8), :] = s[d]
        part = pl.ds(8 * h, 8)
        ends(xs_v[ix, part, :], xs_v[ix + 1, part, :], h, x_base[h], x_kept[h])
        looped(8, 4, fill_x, 8 * h)
        values, base = segment_rhs(h, y_kept[h])
        for n, x in enumerate(values):
            pr_send[h, pl.ds(8 * n, 8), :] = x
        y_own.append(values)
        y_base.append(base)
        pr_copies.append(remote(pr_send.at[h], pr_recv.at[h], 7 + h, mate))
        pr_copies[h].start()

    b_mids = []
    for h in halves:
        pr_copies[h].wait_recv()
        other = [pr_recv[h, pl.ds(8 * n, 8), :] for n in range(2)]
        (gl_a, gl_b), (gr_a, gr_b) = [sides_of(x, y) for x, y in zip(y_own[h], other)]
        b_mid = gr_a + gl_b
        inv, tl, tr = mids[h]
        yr_send[h, pl.ds(0, 8), :] = gl_a + b_mid * tl
        yr_send[h, pl.ds(8, 8), :] = gr_b + b_mid * tr
        b_mids.append(b_mid)
        gather_y(yr_send.at[h], yr_recv.at[h], 9 + h)
    arrived(ym_recv, 6, chips - 1)
    y_chain = []
    for h in halves:
        c = [rows(ym_recv, d, 0, h) for d in range(chips)]
        w = [rows(ym_recv, d, 2, h) + rows(ym_recv, d + 1, 1, h) for d in range(chips - 1)]
        y_chain.append(reduce_matrix(c, w + [zero])[3])

    def chip_faces(h):
        arrived(yr_recv.at[h], 9 + h, chips - 1)
        got = yr_recv.at[h]
        kept = y_chain[h]
        b = [got[d, pl.ds(8, 8), :] + got[d + 1, pl.ds(0, 8), :] for d in range(chips - 1)]
        base = reduce_rhs(b + [zero], lambda k: kept[k])[2]
        s = expand(
            chips, lambda k: base[k], lambda k: kept[k][1], lambda k: kept[k][2], zero, zero
        )
        for d in range(-1, chips):
            ys_v[d + 1, pl.ds(8 * h, 8), :] = s[d]
        s_left, s_right = ys_v[chip, pl.ds(8 * h, 8), :], ys_v[chip + 1, pl.ds(8 * h, 8), :]
        inv, tl, tr = mids[h]
        s_mid = b_mids[h] * inv + tl * s_left + tr * s_right
        ends(mine((s_left, s_mid)), mine((s_mid, s_right)), h, y_base[h], y_kept[h])

    ez_v[...] = jnp.zeros_like(ez_v)

    def fill_y(ls):
        lines = [fill(l, yi_v, yl_v, yr_v) for l in ls]
        for u, l in enumerate(ls):
            for n in range(CELLS):
                b = wr_v[l, n] * lines[u][n] - lz_v[l, n] + ez_v[n]
                ez_v[n] = b * zt_v[l, n]
                zi_v[l, n] = b * zi_v[l, n]

    for h in halves:
        chip_faces(h)
        looped(8, 2, fill_y, 8 * h)

    for halo in halos:
        halo.wait_send()
    for copy in [pm_copy] + pr_copies:
        copy.wait_send()
    sent = [(xm_recv, 2, nx), (ym_recv, 6, chips)]
    for h in halves:
        sent += [(xr_recv.at[h], 3 + h, nx), (yr_recv.at[h], 9 + h, chips)]
    for ref, n, count in sent:
        part = ref.at[pl.ds(0, count - 1)]
        pltpu.make_async_copy(part, part, send_sem.at[n]).wait()


def layers_kernel(zi_v, zt_v, out, tmp_v, out_v, ez_v, out_sem):
    layers = zi_v.shape[0]
    group = 4
    ez_v[...] = jnp.zeros_like(ez_v)
    for l0 in range(layers - group, -1, -group):
        for l in range(l0 + group - 1, l0 - 1, -1):
            for k in range(CELLS):
                s = zi_v[l, k] + zt_v[l, k] * ez_v[k]
                ez_v[k] = s
                tmp_v[l - l0, pl.ds(k, RUNS, stride=CELLS), :] = s
        for l in range(l0 + group - 1, l0 - 1, -1):
            out_v[l] = tmp_v[l - l0].T.reshape(CELLS, RUNS, 128)
        for q in range(RUNS):
            pltpu.make_async_copy(
                out_v.at[pl.ds(l0, group), :, q, :],
                out.at[pl.ds(l0, group), pl.ds(CELLS * q, CELLS), :],
                out_sem,
            ).start()
    pltpu.make_async_copy(out_v, out_v, out_sem).wait()


def body(*args):
    layers, cells_x, cells_y = args[0].shape
    nx, ny = lax.axis_size("gx"), lax.axis_size("gy")
    f32, i32 = jnp.float32, jnp.int32
    tile = pltpu.VMEM((layers, TILE, 128), f32)
    runs = pltpu.VMEM((layers, CELLS, RUNS, 128), f32)
    index = pltpu.VMEM((layers, CELLS, RUNS, 128), i32)
    layer = pltpu.VMEM((CELLS, RUNS, 128), f32)
    halo = pltpu.VMEM((2, layers, 128), f32)

    def rows(*shape):
        return pltpu.VMEM((*shape, 128), f32)

    hbm = pl.BlockSpec(memory_space=pltpu.HBM)
    smem = pl.BlockSpec(memory_space=pltpu.SMEM)
    vmem = pl.BlockSpec(memory_space=pltpu.VMEM)
    shape = pltpu.VMEM((layers, CELLS, RUNS, 128), f32)
    zi, zt = pl.pallas_call(
        runs_kernel,
        out_shape=(shape, shape),
        in_specs=[hbm, hbm, hbm, smem, smem, hbm, hbm, smem, hbm, smem],
        out_specs=(vmem, vmem),
        scratch_shapes=[
            runs,
            runs,
            index,
            index,
            pltpu.VMEM((CELLS, RUNS, 128), i32),
            index,
            runs,
            runs,
            runs,
            runs,
            tile,
            tile,
            tile,
            tile,
            runs,
            runs,
            runs,
            runs,
            runs,
            runs,
            runs,
            layer,
            layer,
            layer,
            layer,
            layer,
            halo,
            halo,
            halo,
            halo,
            *[rows(RUNS * layers)] * 5,
            rows(3 * layers),
            rows(nx, 3 * layers),
            rows(2, layers),
            rows(2, nx, layers),
            rows(nx + 1, layers),
            rows(3 * layers),
            rows(3 * layers),
            rows(3 * layers),
            rows(ny // 2, 3 * layers),
            rows(2, layers),
            rows(2, layers),
            rows(2, layers),
            rows(2, ny // 2, layers),
            rows(ny // 2 + 1, layers),
            pltpu.SemaphoreType.DMA((6,)),
            pltpu.SemaphoreType.DMA((11,)),
            pltpu.SemaphoreType.DMA((11,)),
        ],
        compiler_params=pltpu.CompilerParams(
            collective_id=0, has_side_effects=True, vmem_limit_bytes=56 * 1024 * 1024
        ),
        cost_estimate=pl.CostEstimate(
            flops=100 * args[0].size, bytes_accessed=28 * args[0].size, transcendentals=0
        ),
        name="lines_xy",
    )(*args)
    return pl.pallas_call(
        layers_kernel,
        out_shape=jax.ShapeDtypeStruct(args[0].shape, f32),
        in_specs=[vmem, vmem],
        out_specs=hbm,
        scratch_shapes=[
            pltpu.VMEM((4, TILE, 128), f32),
            runs,
            layer,
            pltpu.SemaphoreType.DMA,
        ],
        compiler_params=pltpu.CompilerParams(vmem_limit_bytes=32 * 1024 * 1024),
        cost_estimate=pl.CostEstimate(
            flops=2 * args[0].size, bytes_accessed=12 * args[0].size, transcendentals=0
        ),
        name="columns_z",
    )(zi, zt)


def solution(mesh):
    field = P(None, "gx", "gy")
    in_specs = (field, field, field, P(), P(), field, P("gx", "gy"), P(), field, P())
    return jax.shard_map(body, mesh=mesh, in_specs=in_specs, out_specs=field, check_vma=False)
```

```python
import jax
import jax.numpy as jnp
from jax import lax
from jax.experimental import pallas as pl
from jax.experimental.pallas import tpu as pltpu
from jax.sharding import PartitionSpec as P

MESH = pl.DeviceIdType.MESH
HELD = 2.0**100
CELLS = 16
RUNS = 8
TILE = CELLS * RUNS
SIDE = 4


def far_first(steps, size):
    return sorted(steps, key=lambda step: -sum(min(d, n - d) for d, n in zip(step, size)))


def inverse(x):
    return pltpu.reciprocal(x, approx=True)


def order(count):
    steps = []
    stride = 1
    while stride < count:
        for node in range(stride - 1, count - 1, 2 * stride):
            steps.append((node, node - stride, node + stride))
        stride *= 2
    return steps


def plus(total, term):
    return term if total is None else total + term


def reduce_matrix(c, w):
    c, w, w_left, kept = list(c), list(w), None, {}
    for k, left, right in order(len(c)):
        inv = inverse(w[k] + (c[k] + c[right]))
        tl, tr = c[k] * inv, c[right] * inv
        c[right] = c[k] * tr
        if left < 0:
            w_left = plus(w_left, w[k] * tl)
        else:
            w[left] = w[left] + w[k] * tl
        w[right] = w[right] + w[k] * tr
        kept[k] = (inv, tl, tr)
    return c[-1], w[-1], w_left, kept


def reduce_rhs(b, kept):
    b, b_left, base = list(b), None, {}
    for k, left, right in order(len(b)):
        inv, tl, tr = kept(k)
        if left < 0:
            b_left = plus(b_left, b[k] * tl)
        else:
            b[left] = b[left] + b[k] * tl
        b[right] = b[right] + b[k] * tr
        base[k] = b[k] * inv
    return b[-1], b_left, base


def expand(count, base, tl, tr, s_left, s_last):
    s = {-1: s_left, count - 1: s_last}
    for k, left, right in reversed(order(count)):
        s[k] = base(k) + tl(k) * s[left] + tr(k) * s[right]
    return s


def take_out(c_left, c_right, w):
    inv = inverse(w + (c_left + c_right))
    tl, tr = c_left * inv, c_right * inv
    return c_left * tr, w * tl, w * tr, (inv, tl, tr)


def down(x):
    return pltpu.roll(x, 1, 0)


def up(x):
    return pltpu.roll(x, RUNS - 1, 0)


def looped(count, unroll, step, start=0):
    def body(i, _):
        step([start + i * unroll + u for u in range(unroll)])
        return 0

    lax.fori_loop(0, count // unroll, body, 0)


def runs_kernel(
    s_in,
    r_in,
    cls_in,
    k_tab,
    leak,
    well_in,
    rate_in,
    rate_tab,
    pit_in,
    level,
    zi_v,
    zt_v,
    s_v,
    w_v,
    cls_v,
    well_v,
    rate_v,
    pit_v,
    ra_v,
    xi_v,
    xl_v,
    xr_v,
    rat_v,
    st_v,
    wt_v,
    q_v,
    wr_v,
    ly_v,
    lz_v,
    fy_v,
    yi_v,
    yl_v,
    yr_v,
    pump_v,
    ez_v,
    flux_v,
    ra_c,
    s_c,
    lo_send,
    hi_send,
    lo_recv,
    hi_recv,
    node_w,
    node_c,
    node_e,
    node_b,
    node_g,
    xm_send,
    xm_recv,
    xr_send,
    xr_recv,
    xs_v,
    pm_send,
    pm_recv,
    ym_send,
    ym_recv,
    pr_send,
    pr_recv,
    yr_send,
    yr_recv,
    ys_v,
    in_sem,
    send_sem,
    recv_sem,
):
    layers = s_in.shape[0]
    ix, iy = lax.axis_index("gx"), lax.axis_index("gy")
    nx, ny = lax.axis_size("gx"), lax.axis_size("gy")
    core, chip = lax.rem(iy, 2), iy // 2
    mate = {"gy": iy + 1 - 2 * core}
    halves = range(layers // 8)

    sides = (nx // SIDE, SIDE)
    steps = [(p, q) for p in range(sides[0]) for q in range(sides[1])][1:]
    along_x = [
        lax.rem(ix // SIDE + p, sides[0]) * SIDE + lax.rem(lax.rem(ix, SIDE) + q, SIDE)
        for p, q in far_first(steps, sides)
    ]
    chips = ny // 2
    steps = [(p,) for p in range(1, chips)]
    along_y = [lax.rem(iy + 2 * p, ny) for (p,) in far_first(steps, (chips,))]
    before, after = lax.rem(iy + ny - 1, ny), lax.rem(iy + 1, ny)

    barrier = pltpu.get_barrier_semaphore()
    greeted = [{"gx": d} for d in along_x] + [{"gy": d} for d in along_y + [before, after]]
    for where in greeted:
        pl.semaphore_signal(barrier, inc=1, device_id=where, device_id_type=MESH)

    fields = [(cls_in, cls_v), (s_in, s_v), (r_in, w_v), (pit_in, pit_v), (well_in, well_v)]
    for n, (src, dst) in enumerate(fields):
        for q in range(RUNS):
            pltpu.make_async_copy(
                src.at[:, pl.ds(CELLS * q, CELLS), :], dst.at[:, :, q, :], in_sem.at[n]
            ).start()
    for q in range(RUNS):
        pltpu.make_async_copy(
            rate_in.at[pl.ds(CELLS * q, CELLS), :], rate_v.at[:, q, :], in_sem.at[5]
        ).start()

    def loaded(n):
        ref = fields[n][1] if n < 5 else rate_v
        pltpu.make_async_copy(ref, ref, in_sem.at[n]).wait()

    def remote(src, dst, n, where):
        return pltpu.make_async_remote_copy(
            src_ref=src,
            dst_ref=dst,
            send_sem=send_sem.at[n],
            recv_sem=recv_sem.at[n],
            device_id=where,
            device_id_type=MESH,
        )

    sub = lax.broadcasted_iota(jnp.int32, (RUNS, 128), 0)
    first, final = sub == 0, sub == RUNS - 1

    def at(l):
        return pl.ds(pl.multiple_of(l * RUNS, RUNS), RUNS)

    def turned(x):
        return x.reshape(TILE, 128).T

    def strided(ref, l):
        return [ref[l, pl.ds(n, RUNS, stride=CELLS), :] for n in range(CELLS)]

    ra_tab = [0.5 / jnp.full((RUNS, 128), k_tab[n], jnp.float32) for n in range(8)]
    ra_tab = [jnp.broadcast_to(t[:1], (TILE, 128)).reshape(CELLS, RUNS, 128) for t in ra_tab]
    loaded(0)
    loaded(1)

    def look(ls):
        ras = []
        for l in ls:
            cls = cls_v[l]
            odd, two, four = (cls & 1) != 0, (cls & 2) != 0, cls >= 4
            pairs = [jnp.where(odd, ra_tab[n + 1], ra_tab[n]) for n in (0, 2, 4, 6)]
            ras.append(
                jnp.where(
                    four,
                    jnp.where(two, pairs[3], pairs[2]),
                    jnp.where(two, pairs[1], pairs[0]),
                )
            )
        ss = [s_v[l] for l in ls]
        turned_ra = [turned(x) for x in ras]
        turned_s = [turned(x) for x in ss]
        for u, l in enumerate(ls):
            ra_v[l] = ras[u]
            rat_v[l] = turned_ra[u]
            st_v[l] = turned_s[u]

    looped(layers, 4, look)
    lo_send[0] = st_v[:, 0, :]
    lo_send[1] = rat_v[:, 0, :]
    hi_send[0] = st_v[:, TILE - 1, :]
    hi_send[1] = rat_v[:, TILE - 1, :]

    loaded(2)
    loaded(3)
    own_x = jnp.where(ix == 0, 1.0, 0.0)

    def weigh(ls):
        ws = []
        for l in ls:
            pit = pit_v[l] == 1
            w = jnp.where(pit, HELD, inverse(w_v[l]))
            ws.append(w)
            s_v[l] = w * jnp.where(pit, level[l], s_v[l])
        for u, l in enumerate(ls):
            ra, w = [ra_v[l, n] for n in range(CELLS)], [ws[u][n] for n in range(CELLS)]
            w_v[l] = ws[u]
            c = [inverse(ra[0] + jnp.where(first, own_x * ra[0], down(ra[15])))]
            c += [inverse(ra[n] + ra[n + 1]) for n in range(CELLS - 1)]
            c, w, e, kept = reduce_matrix(c, w)
            for k in kept:
                xi_v[l, k], xl_v[l, k], xr_v[l, k] = kept[k]
            node_w[at(l), :], node_c[at(l), :], node_e[at(l), :] = w, c, e

    looped(layers, 4, weigh)

    def nodes(ref, h):
        return [ref[pl.ds(n + 64 * h, 8, stride=RUNS), :] for n in range(RUNS)]

    def put(ref, n, h, x):
        ref[pl.ds(n + 64 * h, 8, stride=RUNS), :] = x

    def join(w, extra):
        return [w[n] + extra[n + 1] for n in range(RUNS - 1)] + [w[RUNS - 1]]

    def segment(h, c_end):
        extra = nodes(node_e, h)
        c, w, e, kept = reduce_matrix(nodes(node_c, h), join(nodes(node_w, h), extra))
        c, w_left, w_right, last = take_out(c, c_end, w)
        kept[RUNS - 1] = last
        return (c, extra[0] + e + w_left, w_right), kept

    def segment_rhs(h, kept):
        extra = nodes(node_g, h)
        b, g, base = reduce_rhs(join(nodes(node_b, h), extra), lambda k: kept[k])
        inv, tl, tr = kept[RUNS - 1]
        base[RUNS - 1] = b * inv
        return (extra[0] + g + b * tl, b * tr), base

    x_kept = []
    end_x = jnp.where(ix == nx - 1, 2.0, 1.0)
    for h in halves:
        values, kept = segment(h, inverse(end_x * ra_v[pl.ds(8 * h, 8), CELLS - 1, RUNS - 1, :]))
        for n, x in enumerate(values):
            xm_send[pl.ds(layers * n + 8 * h, 8), :] = x
        x_kept.append(kept)

    def gather_x(src, dst, n):
        for other in along_x:
            remote(src, dst.at[ix], n, {"gx": other}).start()
        dst[ix] = src[...]

    def gather_y(src, dst, n):
        for other in along_y:
            remote(src, dst.at[chip], n, {"gy": other}).start()
        dst[chip] = src[...]

    def arrived(dst, n, count):
        ref = dst.at[pl.ds(0, count)]
        pltpu.make_async_copy(ref, ref, recv_sem.at[n]).wait()

    pl.semaphore_wait(barrier, len(greeted))
    halos = [
        remote(lo_send, hi_recv, 0, {"gy": before}),
        remote(hi_send, lo_recv, 1, {"gy": after}),
    ]
    for halo in halos:
        halo.start()
    gather_x(xm_send, xm_recv, 2)

    flux_v[...] = jnp.zeros_like(flux_v)
    own_y = jnp.where(iy == 0, 1.0, 0.0)
    for n in range(CELLS):
        ra_c[n] = rat_v[0, pl.ds(n, RUNS, stride=CELLS), :]
        s_c[n] = st_v[0, pl.ds(n, RUNS, stride=CELLS), :]

    def across(ls):
        ra = [ra_c[n] for n in range(CELLS)]
        s = [s_c[n] for n in range(CELLS)]
        for l in ls:
            above = jnp.minimum(l + 1, layers - 1)
            leak_l = jnp.where(l < layers - 1, leak[jnp.minimum(l, layers - 2)], 0.0)
            ra_up, s_up = strided(rat_v, above), strided(st_v, above)
            ra_before = down(ra[15])
            face = inverse(ra[0] + jnp.where(first, own_y * ra[0], ra_before))
            fy_v[l, 0] = face
            flux_left = jnp.where(first, 0.0, face * (s[0] - down(s[15])))
            flux = flux_left
            for n in range(CELLS):
                if n < CELLS - 1:
                    face = inverse(ra[n] + ra[n + 1])
                    fy_v[l, n + 1] = face
                    flux_next = face * (s[n + 1] - s[n])
                else:
                    flux_next = up(flux_left)
                ly = flux_next - flux
                flux = flux_next
                face_z = leak_l * inverse(ra[n] + ra_up[n])
                flux_z = face_z * (s_up[n] - s[n])
                lz = flux_z - flux_v[n]
                flux_v[n] = flux_z
                ly_v[l, n] = ly
                lz_v[l, n] = lz
                q_v[l, pl.ds(n, RUNS, stride=CELLS), :] = ly + lz
                zt_v[l, n] = face_z
            ra, s = ra_up, s_up
        for n in range(CELLS):
            ra_c[n], s_c[n] = ra[n], s[n]

    looped(layers, 4, across)

    loaded(4)
    loaded(5)
    rate = rate_v[...]
    pump = jnp.full(rate.shape, rate_tab[0], jnp.float32)
    for n in range(1, 16):
        pump = jnp.where(rate == n, rate_tab[n], pump)
    pump_v[...] = pump

    for halo in halos:
        halo.wait_recv()
    at_lo, at_hi = iy == 0, iy == ny - 1
    s_lo = jnp.where(at_lo, 0.0, lo_recv[0])
    ra_lo = jnp.where(at_lo, lo_send[1], lo_recv[1])
    s_hi = jnp.where(at_hi, 0.0, hi_recv[0])
    ra_hi = jnp.where(at_hi, hi_send[1], hi_recv[1])
    flux_lo = inverse(ra_lo + lo_send[1]) * (lo_send[0] - s_lo)
    flux_hi = inverse(ra_hi + hi_send[1]) * (s_hi - hi_send[0])
    q_v[:, 0, :] = q_v[:, 0, :] - flux_lo
    q_v[:, TILE - 1, :] = q_v[:, TILE - 1, :] + flux_hi
    ly_v[:, 0, 0, :] = ly_v[:, 0, 0, :] - flux_lo
    ly_v[:, CELLS - 1, RUNS - 1, :] = ly_v[:, CELLS - 1, RUNS - 1, :] + flux_hi

    def runs_x(ls):
        qs = [q_v[l].T.reshape(CELLS, RUNS, 128) for l in ls]
        bs = []
        for u, l in enumerate(ls):
            pumped = well_v[l].astype(jnp.float32) * pump_v[...]
            bs.append(s_v[l] + (qs[u] + pumped))
        for u, l in enumerate(ls):
            b, g, base = reduce_rhs(
                [bs[u][n] for n in range(CELLS)], lambda k: (xi_v[l, k], xl_v[l, k], xr_v[l, k])
            )
            for k in base:
                xi_v[l, k] = base[k]
            node_b[at(l), :], node_g[at(l), :] = b, g

    x_base = []
    for h in halves:
        looped(8, 4, runs_x, 8 * h)
        values, base = segment_rhs(h, x_kept[h])
        for n, x in enumerate(values):
            xr_send[h, pl.ds(8 * n, 8), :] = x
        x_base.append(base)
        gather_x(xr_send.at[h], xr_recv.at[h], 3 + h)

    ez_v[...] = jnp.zeros_like(ez_v)

    def runs_y(ls):
        wts = [turned(w_v[l]) for l in ls]
        for u, l in enumerate(ls):
            wt_v[l] = wts[u]
        for l in ls:
            wt = strided(wt_v, l)
            c, w, e, kept = reduce_matrix([fy_v[l, n] for n in range(CELLS)], wt)
            for k in kept:
                yi_v[l, k], yl_v[l, k], yr_v[l, k] = kept[k]
            node_w[at(l), :], node_c[at(l), :], node_e[at(l), :] = w, c, e
            for n in range(CELLS):
                wr_v[l, n] = wt[n]
                e = wt[n] + ez_v[n]
                inv = inverse(e + zt_v[l, n])
                t = zt_v[l, n] * inv
                zt_v[l, n] = t
                zi_v[l, n] = inv
                ez_v[n] = e * t

    looped(layers, 4, runs_y)

    is_a = core == 0

    def mine(pair):
        return jnp.where(is_a, pair[0], pair[1])

    def theirs(pair):
        return jnp.where(is_a, pair[1], pair[0])

    y_kept, y_values = [], []
    end_y = jnp.where(iy == ny - 1, 2.0, 1.0)
    for h in halves:
        values, kept = segment(h, inverse(end_y * hi_send[1, pl.ds(8 * h, 8), :]))
        y_values.append(values)
        y_kept.append(kept)
    for h in halves:
        for n, x in enumerate(y_values[h]):
            pm_send[pl.ds(layers * n + 8 * h, 8), :] = x
    pm_copy = remote(pm_send, pm_recv, 5, mate)
    pm_copy.start()
    pm_copy.wait_recv()

    def sides_of(own, other):
        return mine((own, other)), theirs((own, other))

    mids = []
    for h in halves:
        other = [pm_recv[pl.ds(layers * n + 8 * h, 8), :] for n in range(3)]
        c, e, w = [sides_of(x, y) for x, y in zip(y_values[h], other)]
        joined, w_left, w_right, mid = take_out(c[0], c[1], w[0] + e[1])
        for n, x in enumerate((joined, e[0] + w_left, w[1] + w_right)):
            ym_send[pl.ds(layers * n + 8 * h, 8), :] = x
        mids.append(mid)
    gather_y(ym_send, ym_recv, 6)

    arrived(xm_recv, 2, nx - 1)
    zero = jnp.zeros((RUNS, 128), jnp.float32)

    def rows(ref, d, n, h):
        return ref[d, pl.ds(layers * n + 8 * h, 8), :]

    x_chain = []
    for h in halves:
        c = [rows(xm_recv, d, 0, h) for d in range(nx)]
        w = [rows(xm_recv, d, 2, h) + rows(xm_recv, d + 1, 1, h) for d in range(nx - 1)]
        x_chain.append(reduce_matrix(c, w + [zero])[3])

    def ends(s_left, s_right, h, base, kept):
        inv, tl, tr = kept[RUNS - 1]
        s_last = base[RUNS - 1] + tl * s_left + tr * s_right
        s = expand(
            RUNS, lambda k: base[k], lambda k: kept[k][1], lambda k: kept[k][2], s_left, s_last
        )
        for n in range(RUNS):
            put(node_w, n, h, s[n])
            put(node_c, n, h, s[n - 1])

    def fill(l, base, tl, tr):
        s = expand(
            CELLS,
            lambda k: base[l, k],
            lambda k: tl[l, k],
            lambda k: tr[l, k],
            node_c[at(l), :],
            node_w[at(l), :],
        )
        return [s[n] for n in range(CELLS)]

    def fill_x(ls):
        lines = [turned(jnp.stack(fill(l, xi_v, xl_v, xr_v))) for l in ls]
        for u, l in enumerate(ls):
            q_v[l] = lines[u]
        for l in ls:
            sx = strided(q_v, l)
            b = [wr_v[l, n] * sx[n] - ly_v[l, n] for n in range(CELLS)]
            b, g, base = reduce_rhs(b, lambda k: (yi_v[l, k], yl_v[l, k], yr_v[l, k]))
            for k in base:
                yi_v[l, k] = base[k]
            node_b[at(l), :], node_g[at(l), :] = b, g

    y_base, y_own, pr_copies, b_mids = [], [], [], []

    def join_pair(h):
        pr_copies[h].wait_recv()
        other = [pr_recv[h, pl.ds(8 * n, 8), :] for n in range(2)]
        (gl_a, gl_b), (gr_a, gr_b) = [sides_of(x, y) for x, y in zip(y_own[h], other)]
        b_mid = gr_a + gl_b
        inv, tl, tr = mids[h]
        yr_send[h, pl.ds(0, 8), :] = gl_a + b_mid * tl
        yr_send[h, pl.ds(8, 8), :] = gr_b + b_mid * tr
        b_mids.append(b_mid)
        gather_y(yr_send.at[h], yr_recv.at[h], 9 + h)

    for h in halves:
        arrived(xr_recv.at[h], 3 + h, nx - 1)
        got = xr_recv.at[h]
        kept = x_chain[h]
        b = [got[d, pl.ds(8, 8), :] + got[d + 1, pl.ds(0, 8), :] for d in range(nx - 1)]
        base = reduce_rhs(b + [zero], lambda k: kept[k])[2]
        s = expand(
            nx, lambda k: base[k], lambda k: kept[k][1], lambda k: kept[k][2], zero, zero
        )
        for d in range(-1, nx):
            xs_v[d + 1, pl.ds(8 * h, 8), :] = s[d]
        part = pl.ds(8 * h, 8)
        ends(xs_v[ix, part, :], xs_v[ix + 1, part, :], h, x_base[h], x_kept[h])
        looped(4, 4, fill_x, 8 * h)
        if h:
            join_pair(0)
        looped(4, 4, fill_x, 8 * h + 4)
        values, base = segment_rhs(h, y_kept[h])
        for n, x in enumerate(values):
            pr_send[h, pl.ds(8 * n, 8), :] = x
        y_own.append(values)
        y_base.append(base)
        pr_copies.append(remote(pr_send.at[h], pr_recv.at[h], 7 + h, mate))
        pr_copies[h].start()

    join_pair(1)

    arrived(ym_recv, 6, chips - 1)
    y_chain = []
    for h in halves:
        c = [rows(ym_recv, d, 0, h) for d in range(chips)]
        w = [rows(ym_recv, d, 2, h) + rows(ym_recv, d + 1, 1, h) for d in range(chips - 1)]
        y_chain.append(reduce_matrix(c, w + [zero])[3])

    def chip_faces(h):
        arrived(yr_recv.at[h], 9 + h, chips - 1)
        got = yr_recv.at[h]
        kept = y_chain[h]
        b = [got[d, pl.ds(8, 8), :] + got[d + 1, pl.ds(0, 8), :] for d in range(chips - 1)]
        base = reduce_rhs(b + [zero], lambda k: kept[k])[2]
        s = expand(
            chips, lambda k: base[k], lambda k: kept[k][1], lambda k: kept[k][2], zero, zero
        )
        for d in range(-1, chips):
            ys_v[d + 1, pl.ds(8 * h, 8), :] = s[d]
        s_left, s_right = ys_v[chip, pl.ds(8 * h, 8), :], ys_v[chip + 1, pl.ds(8 * h, 8), :]
        inv, tl, tr = mids[h]
        s_mid = b_mids[h] * inv + tl * s_left + tr * s_right
        ends(mine((s_left, s_mid)), mine((s_mid, s_right)), h, y_base[h], y_kept[h])

    ez_v[...] = jnp.zeros_like(ez_v)

    def fill_y(ls):
        lines = [fill(l, yi_v, yl_v, yr_v) for l in ls]
        for u, l in enumerate(ls):
            for n in range(CELLS):
                b = wr_v[l, n] * lines[u][n] - lz_v[l, n] + ez_v[n]
                ez_v[n] = b * zt_v[l, n]
                zi_v[l, n] = b * zi_v[l, n]

    for h in halves:
        chip_faces(h)
        looped(8, 2, fill_y, 8 * h)

    for halo in halos:
        halo.wait_send()
    for copy in [pm_copy] + pr_copies:
        copy.wait_send()
    sent = [(xm_recv, 2, nx), (ym_recv, 6, chips)]
    for h in halves:
        sent += [(xr_recv.at[h], 3 + h, nx), (yr_recv.at[h], 9 + h, chips)]
    for ref, n, count in sent:
        part = ref.at[pl.ds(0, count - 1)]
        pltpu.make_async_copy(part, part, send_sem.at[n]).wait()


def layers_kernel(zi_v, zt_v, out, tmp_v, out_v, ez_v, out_sem):
    layers = zi_v.shape[0]
    group = 4
    ez_v[...] = jnp.zeros_like(ez_v)
    for l0 in range(layers - group, -1, -group):
        for l in range(l0 + group - 1, l0 - 1, -1):
            for k in range(CELLS):
                s = zi_v[l, k] + zt_v[l, k] * ez_v[k]
                ez_v[k] = s
                tmp_v[l - l0, pl.ds(k, RUNS, stride=CELLS), :] = s
        for l in range(l0 + group - 1, l0 - 1, -1):
            out_v[l] = tmp_v[l - l0].T.reshape(CELLS, RUNS, 128)
        for q in range(RUNS):
            pltpu.make_async_copy(
                out_v.at[pl.ds(l0, group), :, q, :],
                out.at[pl.ds(l0, group), pl.ds(CELLS * q, CELLS), :],
                out_sem,
            ).start()
    pltpu.make_async_copy(out_v, out_v, out_sem).wait()


def body(*args):
    layers, cells_x, cells_y = args[0].shape
    nx, ny = lax.axis_size("gx"), lax.axis_size("gy")
    f32, i32 = jnp.float32, jnp.int32
    tile = pltpu.VMEM((layers, TILE, 128), f32)
    runs = pltpu.VMEM((layers, CELLS, RUNS, 128), f32)
    index = pltpu.VMEM((layers, CELLS, RUNS, 128), i32)
    layer = pltpu.VMEM((CELLS, RUNS, 128), f32)
    halo = pltpu.VMEM((2, layers, 128), f32)

    def rows(*shape):
        return pltpu.VMEM((*shape, 128), f32)

    hbm = pl.BlockSpec(memory_space=pltpu.HBM)
    smem = pl.BlockSpec(memory_space=pltpu.SMEM)
    vmem = pl.BlockSpec(memory_space=pltpu.VMEM)
    shape = pltpu.VMEM((layers, CELLS, RUNS, 128), f32)
    zi, zt = pl.pallas_call(
        runs_kernel,
        out_shape=(shape, shape),
        in_specs=[hbm, hbm, hbm, smem, smem, hbm, hbm, smem, hbm, smem],
        out_specs=(vmem, vmem),
        scratch_shapes=[
            runs,
            runs,
            index,
            index,
            pltpu.VMEM((CELLS, RUNS, 128), i32),
            index,
            runs,
            runs,
            runs,
            runs,
            tile,
            tile,
            tile,
            tile,
            runs,
            runs,
            runs,
            runs,
            runs,
            runs,
            runs,
            layer,
            layer,
            layer,
            layer,
            layer,
            halo,
            halo,
            halo,
            halo,
            *[rows(RUNS * layers)] * 5,
            rows(3 * layers),
            rows(nx, 3 * layers),
            rows(2, layers),
            rows(2, nx, layers),
            rows(nx + 1, layers),
            rows(3 * layers),
            rows(3 * layers),
            rows(3 * layers),
            rows(ny // 2, 3 * layers),
            rows(2, layers),
            rows(2, layers),
            rows(2, layers),
            rows(2, ny // 2, layers),
            rows(ny // 2 + 1, layers),
            pltpu.SemaphoreType.DMA((6,)),
            pltpu.SemaphoreType.DMA((11,)),
            pltpu.SemaphoreType.DMA((11,)),
        ],
        compiler_params=pltpu.CompilerParams(
            collective_id=0, has_side_effects=True, vmem_limit_bytes=56 * 1024 * 1024
        ),
        cost_estimate=pl.CostEstimate(
            flops=100 * args[0].size, bytes_accessed=28 * args[0].size, transcendentals=0
        ),
        name="lines_xy",
    )(*args)
    return pl.pallas_call(
        layers_kernel,
        out_shape=jax.ShapeDtypeStruct(args[0].shape, f32),
        in_specs=[vmem, vmem],
        out_specs=hbm,
        scratch_shapes=[
            pltpu.VMEM((4, TILE, 128), f32),
            runs,
            layer,
            pltpu.SemaphoreType.DMA,
        ],
        compiler_params=pltpu.CompilerParams(vmem_limit_bytes=32 * 1024 * 1024),
        cost_estimate=pl.CostEstimate(
            flops=2 * args[0].size, bytes_accessed=12 * args[0].size, transcendentals=0
        ),
        name="columns_z",
    )(zi, zt)


def solution(mesh):
    field = P(None, "gx", "gy")
    in_specs = (field, field, field, P(), P(), field, P("gx", "gy"), P(), field, P())
    return jax.shard_map(body, mesh=mesh, in_specs=in_specs, out_specs=field, check_vma=False)
```

```python
import jax
import jax.numpy as jnp
from jax import lax
from jax.experimental import pallas as pl
from jax.experimental.pallas import tpu as pltpu
from jax.sharding import PartitionSpec as P

MESH = pl.DeviceIdType.MESH
HELD = 2.0**100
CELLS = 16
RUNS = 8
TILE = CELLS * RUNS
SIDE = 4


def far_first(steps, size):
    return sorted(steps, key=lambda step: -sum(min(d, n - d) for d, n in zip(step, size)))


def inverse(x):
    return pltpu.reciprocal(x, approx=True)


def order(count):
    steps = []
    stride = 1
    while stride < count:
        for node in range(stride - 1, count - 1, 2 * stride):
            steps.append((node, node - stride, node + stride))
        stride *= 2
    return steps


def plus(total, term):
    return term if total is None else total + term


def reduce_matrix(c, w):
    c, w, w_left, kept = list(c), list(w), None, {}
    for k, left, right in order(len(c)):
        inv = inverse(w[k] + (c[k] + c[right]))
        tl, tr = c[k] * inv, c[right] * inv
        c[right] = c[k] * tr
        if left < 0:
            w_left = plus(w_left, w[k] * tl)
        else:
            w[left] = w[left] + w[k] * tl
        w[right] = w[right] + w[k] * tr
        kept[k] = (inv, tl, tr)
    return c[-1], w[-1], w_left, kept


def reduce_rhs(b, kept):
    b, b_left, base = list(b), None, {}
    for k, left, right in order(len(b)):
        inv, tl, tr = kept(k)
        if left < 0:
            b_left = plus(b_left, b[k] * tl)
        else:
            b[left] = b[left] + b[k] * tl
        b[right] = b[right] + b[k] * tr
        base[k] = b[k] * inv
    return b[-1], b_left, base


def expand(count, base, tl, tr, s_left, s_last):
    s = {-1: s_left, count - 1: s_last}
    for k, left, right in reversed(order(count)):
        s[k] = base(k) + tl(k) * s[left] + tr(k) * s[right]
    return s


def take_out(c_left, c_right, w):
    inv = inverse(w + (c_left + c_right))
    tl, tr = c_left * inv, c_right * inv
    return c_left * tr, w * tl, w * tr, (inv, tl, tr)


def down(x):
    return pltpu.roll(x, 1, 0)


def up(x):
    return pltpu.roll(x, RUNS - 1, 0)


def looped(count, unroll, step, start=0):
    def body(i, _):
        step([start + i * unroll + u for u in range(unroll)])
        return 0

    lax.fori_loop(0, count // unroll, body, 0)


def runs_kernel(
    s_in,
    r_in,
    cls_in,
    k_tab,
    leak,
    well_in,
    rate_in,
    rate_tab,
    pit_in,
    level,
    zi_v,
    zt_v,
    s_v,
    w_v,
    cls_v,
    well_v,
    rate_v,
    pit_v,
    ra_v,
    xi_v,
    xl_v,
    xr_v,
    rat_v,
    st_v,
    wt_v,
    q_v,
    wr_v,
    ly_v,
    lz_v,
    fy_v,
    yi_v,
    yl_v,
    yr_v,
    pump_v,
    ez_v,
    flux_v,
    ra_c,
    s_c,
    lo_send,
    hi_send,
    lo_recv,
    hi_recv,
    node_w,
    node_c,
    node_e,
    node_b,
    node_g,
    xm_send,
    xm_recv,
    xr_send,
    xr_recv,
    xs_v,
    pm_send,
    pm_recv,
    ym_send,
    ym_recv,
    pr_send,
    pr_recv,
    yr_send,
    yr_recv,
    ys_v,
    in_sem,
    send_sem,
    recv_sem,
):
    layers = s_in.shape[0]
    ix, iy = lax.axis_index("gx"), lax.axis_index("gy")
    nx, ny = lax.axis_size("gx"), lax.axis_size("gy")
    core, chip = lax.rem(iy, 2), iy // 2
    mate = {"gy": iy + 1 - 2 * core}
    halves = range(layers // 8)

    sides = (nx // SIDE, SIDE)
    steps = [(p, q) for p in range(sides[0]) for q in range(sides[1])][1:]
    along_x = [
        lax.rem(ix // SIDE + p, sides[0]) * SIDE + lax.rem(lax.rem(ix, SIDE) + q, SIDE)
        for p, q in far_first(steps, sides)
    ]
    chips = ny // 2
    steps = [(p,) for p in range(1, chips)]
    along_y = [lax.rem(iy + 2 * p, ny) for (p,) in far_first(steps, (chips,))]
    before, after = lax.rem(iy + ny - 1, ny), lax.rem(iy + 1, ny)

    barrier = pltpu.get_barrier_semaphore()
    greeted = [{"gx": d} for d in along_x] + [{"gy": d} for d in along_y + [before, after]]
    for where in greeted:
        pl.semaphore_signal(barrier, inc=1, device_id=where, device_id_type=MESH)

    fields = [(cls_in, cls_v), (s_in, s_v), (r_in, w_v), (pit_in, pit_v), (well_in, well_v)]
    for n, (src, dst) in enumerate(fields):
        for q in range(RUNS):
            pltpu.make_async_copy(
                src.at[:, pl.ds(CELLS * q, CELLS), :], dst.at[:, :, q, :], in_sem.at[n]
            ).start()
    for q in range(RUNS):
        pltpu.make_async_copy(
            rate_in.at[pl.ds(CELLS * q, CELLS), :], rate_v.at[:, q, :], in_sem.at[5]
        ).start()

    def loaded(n):
        ref = fields[n][1] if n < 5 else rate_v
        pltpu.make_async_copy(ref, ref, in_sem.at[n]).wait()

    def remote(src, dst, n, where):
        return pltpu.make_async_remote_copy(
            src_ref=src,
            dst_ref=dst,
            send_sem=send_sem.at[n],
            recv_sem=recv_sem.at[n],
            device_id=where,
            device_id_type=MESH,
        )

    sub = lax.broadcasted_iota(jnp.int32, (RUNS, 128), 0)
    first, final = sub == 0, sub == RUNS - 1

    def at(l):
        return pl.ds(pl.multiple_of(l * RUNS, RUNS), RUNS)

    def turned(x):
        return x.reshape(TILE, 128).T

    def strided(ref, l):
        return [ref[l, pl.ds(n, RUNS, stride=CELLS), :] for n in range(CELLS)]

    ra_tab = [0.5 / jnp.full((RUNS, 128), k_tab[n], jnp.float32) for n in range(8)]
    ra_tab = [jnp.broadcast_to(t[:1], (TILE, 128)).reshape(CELLS, RUNS, 128) for t in ra_tab]
    loaded(0)
    loaded(1)

    def look(ls):
        ras = []
        for l in ls:
            cls = cls_v[l]
            odd, two, four = (cls & 1) != 0, (cls & 2) != 0, cls >= 4
            pairs = [jnp.where(odd, ra_tab[n + 1], ra_tab[n]) for n in (0, 2, 4, 6)]
            ras.append(
                jnp.where(
                    four,
                    jnp.where(two, pairs[3], pairs[2]),
                    jnp.where(two, pairs[1], pairs[0]),
                )
            )
        ss = [s_v[l] for l in ls]
        turned_ra = [turned(x) for x in ras]
        turned_s = [turned(x) for x in ss]
        for u, l in enumerate(ls):
            ra_v[l] = ras[u]
            rat_v[l] = turned_ra[u]
            st_v[l] = turned_s[u]

    looped(layers, 4, look)
    lo_send[0] = st_v[:, 0, :]
    lo_send[1] = rat_v[:, 0, :]
    hi_send[0] = st_v[:, TILE - 1, :]
    hi_send[1] = rat_v[:, TILE - 1, :]

    loaded(2)
    loaded(3)
    own_x = jnp.where(ix == 0, 1.0, 0.0)

    def weigh(ls):
        ws = []
        for l in ls:
            pit = pit_v[l] == 1
            w = jnp.where(pit, HELD, inverse(w_v[l]))
            ws.append(w)
            s_v[l] = w * jnp.where(pit, level[l], s_v[l])
        for u, l in enumerate(ls):
            ra, w = [ra_v[l, n] for n in range(CELLS)], [ws[u][n] for n in range(CELLS)]
            w_v[l] = ws[u]
            c = [inverse(ra[0] + jnp.where(first, own_x * ra[0], down(ra[15])))]
            c += [inverse(ra[n] + ra[n + 1]) for n in range(CELLS - 1)]
            c, w, e, kept = reduce_matrix(c, w)
            for k in kept:
                xi_v[l, k], xl_v[l, k], xr_v[l, k] = kept[k]
            node_w[at(l), :], node_c[at(l), :], node_e[at(l), :] = w, c, e

    looped(layers, 4, weigh)

    def nodes(ref, h):
        return [ref[pl.ds(n + 64 * h, 8, stride=RUNS), :] for n in range(RUNS)]

    def put(ref, n, h, x):
        ref[pl.ds(n + 64 * h, 8, stride=RUNS), :] = x

    def join(w, extra):
        return [w[n] + extra[n + 1] for n in range(RUNS - 1)] + [w[RUNS - 1]]

    def segment(h, c_end):
        extra = nodes(node_e, h)
        c, w, e, kept = reduce_matrix(nodes(node_c, h), join(nodes(node_w, h), extra))
        c, w_left, w_right, last = take_out(c, c_end, w)
        kept[RUNS - 1] = last
        return (c, extra[0] + e + w_left, w_right), kept

    def segment_rhs(h, kept):
        extra = nodes(node_g, h)
        b, g, base = reduce_rhs(join(nodes(node_b, h), extra), lambda k: kept[k])
        inv, tl, tr = kept[RUNS - 1]
        base[RUNS - 1] = b * inv
        return (extra[0] + g + b * tl, b * tr), base

    x_kept = []
    end_x = jnp.where(ix == nx - 1, 2.0, 1.0)
    for h in halves:
        values, kept = segment(h, inverse(end_x * ra_v[pl.ds(8 * h, 8), CELLS - 1, RUNS - 1, :]))
        for n, x in enumerate(values):
            xm_send[pl.ds(layers * n + 8 * h, 8), :] = x
        x_kept.append(kept)

    def gather_x(src, dst, n):
        for other in along_x:
            remote(src, dst.at[ix], n, {"gx": other}).start()
        dst[ix] = src[...]

    def gather_y(src, dst, n):
        for other in along_y:
            remote(src, dst.at[chip], n, {"gy": other}).start()
        dst[chip] = src[...]

    def arrived(dst, n, count):
        ref = dst.at[pl.ds(0, count)]
        pltpu.make_async_copy(ref, ref, recv_sem.at[n]).wait()

    pl.semaphore_wait(barrier, len(greeted))
    halos = [
        remote(lo_send, hi_recv, 0, {"gy": before}),
        remote(hi_send, lo_recv, 1, {"gy": after}),
    ]
    for halo in halos:
        halo.start()
    gather_x(xm_send, xm_recv, 2)

    flux_v[...] = jnp.zeros_like(flux_v)
    own_y = jnp.where(iy == 0, 1.0, 0.0)
    for n in range(CELLS):
        ra_c[n] = rat_v[0, pl.ds(n, RUNS, stride=CELLS), :]
        s_c[n] = st_v[0, pl.ds(n, RUNS, stride=CELLS), :]

    def across(ls):
        ra = [ra_c[n] for n in range(CELLS)]
        s = [s_c[n] for n in range(CELLS)]
        for l in ls:
            above = jnp.minimum(l + 1, layers - 1)
            leak_l = jnp.where(l < layers - 1, leak[jnp.minimum(l, layers - 2)], 0.0)
            ra_up, s_up = strided(rat_v, above), strided(st_v, above)
            ra_before = down(ra[15])
            face = inverse(ra[0] + jnp.where(first, own_y * ra[0], ra_before))
            fy_v[l, 0] = face
            flux_left = jnp.where(first, 0.0, face * (s[0] - down(s[15])))
            flux = flux_left
            for n in range(CELLS):
                if n < CELLS - 1:
                    face = inverse(ra[n] + ra[n + 1])
                    fy_v[l, n + 1] = face
                    flux_next = face * (s[n + 1] - s[n])
                else:
                    flux_next = up(flux_left)
                ly = flux_next - flux
                flux = flux_next
                face_z = leak_l * inverse(ra[n] + ra_up[n])
                flux_z = face_z * (s_up[n] - s[n])
                lz = flux_z - flux_v[n]
                flux_v[n] = flux_z
                ly_v[l, n] = ly
                lz_v[l, n] = lz
                q_v[l, pl.ds(n, RUNS, stride=CELLS), :] = ly + lz
                zt_v[l, n] = face_z
            ra, s = ra_up, s_up
        for n in range(CELLS):
            ra_c[n], s_c[n] = ra[n], s[n]

    looped(layers, 4, across)

    loaded(4)
    loaded(5)
    rate = rate_v[...]
    pump = jnp.full(rate.shape, rate_tab[0], jnp.float32)
    for n in range(1, 16):
        pump = jnp.where(rate == n, rate_tab[n], pump)
    pump_v[...] = pump

    for halo in halos:
        halo.wait_recv()
    at_lo, at_hi = iy == 0, iy == ny - 1
    s_lo = jnp.where(at_lo, 0.0, lo_recv[0])
    ra_lo = jnp.where(at_lo, lo_send[1], lo_recv[1])
    s_hi = jnp.where(at_hi, 0.0, hi_recv[0])
    ra_hi = jnp.where(at_hi, hi_send[1], hi_recv[1])
    flux_lo = inverse(ra_lo + lo_send[1]) * (lo_send[0] - s_lo)
    flux_hi = inverse(ra_hi + hi_send[1]) * (s_hi - hi_send[0])
    q_v[:, 0, :] = q_v[:, 0, :] - flux_lo
    q_v[:, TILE - 1, :] = q_v[:, TILE - 1, :] + flux_hi
    ly_v[:, 0, 0, :] = ly_v[:, 0, 0, :] - flux_lo
    ly_v[:, CELLS - 1, RUNS - 1, :] = ly_v[:, CELLS - 1, RUNS - 1, :] + flux_hi

    def runs_x(ls):
        qs = [q_v[l].T.reshape(CELLS, RUNS, 128) for l in ls]
        bs = []
        for u, l in enumerate(ls):
            pumped = well_v[l].astype(jnp.float32) * pump_v[...]
            bs.append(s_v[l] + (qs[u] + pumped))
        for u, l in enumerate(ls):
            b, g, base = reduce_rhs(
                [bs[u][n] for n in range(CELLS)], lambda k: (xi_v[l, k], xl_v[l, k], xr_v[l, k])
            )
            for k in base:
                xi_v[l, k] = base[k]
            node_b[at(l), :], node_g[at(l), :] = b, g

    x_base = []
    for h in halves:
        looped(8, 4, runs_x, 8 * h)
        values, base = segment_rhs(h, x_kept[h])
        for n, x in enumerate(values):
            xr_send[h, pl.ds(8 * n, 8), :] = x
        x_base.append(base)
        gather_x(xr_send.at[h], xr_recv.at[h], 3 + h)

    ez_v[...] = jnp.zeros_like(ez_v)

    def runs_y(ls):
        wts = [turned(w_v[l]) for l in ls]
        for u, l in enumerate(ls):
            wt_v[l] = wts[u]
        for l in ls:
            wt = strided(wt_v, l)
            c, w, e, kept = reduce_matrix([fy_v[l, n] for n in range(CELLS)], wt)
            for k in kept:
                yi_v[l, k], yl_v[l, k], yr_v[l, k] = kept[k]
            node_w[at(l), :], node_c[at(l), :], node_e[at(l), :] = w, c, e
            for n in range(CELLS):
                wr_v[l, n] = wt[n]
                e = wt[n] + ez_v[n]
                inv = inverse(e + zt_v[l, n])
                t = zt_v[l, n] * inv
                zt_v[l, n] = t
                zi_v[l, n] = inv
                ez_v[n] = e * t

    looped(layers, 4, runs_y)

    is_a = core == 0

    def mine(pair):
        return jnp.where(is_a, pair[0], pair[1])

    def theirs(pair):
        return jnp.where(is_a, pair[1], pair[0])

    y_kept, y_values = [], []
    end_y = jnp.where(iy == ny - 1, 2.0, 1.0)
    for h in halves:
        values, kept = segment(h, inverse(end_y * hi_send[1, pl.ds(8 * h, 8), :]))
        y_values.append(values)
        y_kept.append(kept)
    for h in halves:
        for n, x in enumerate(y_values[h]):
            pm_send[pl.ds(layers * n + 8 * h, 8), :] = x
    pm_copy = remote(pm_send, pm_recv, 5, mate)
    pm_copy.start()
    pm_copy.wait_recv()

    def sides_of(own, other):
        return mine((own, other)), theirs((own, other))

    mids = []
    for h in halves:
        other = [pm_recv[pl.ds(layers * n + 8 * h, 8), :] for n in range(3)]
        c, e, w = [sides_of(x, y) for x, y in zip(y_values[h], other)]
        joined, w_left, w_right, mid = take_out(c[0], c[1], w[0] + e[1])
        for n, x in enumerate((joined, e[0] + w_left, w[1] + w_right)):
            ym_send[pl.ds(layers * n + 8 * h, 8), :] = x
        mids.append(mid)
    gather_y(ym_send, ym_recv, 6)

    arrived(xm_recv, 2, nx - 1)
    zero = jnp.zeros((RUNS, 128), jnp.float32)

    def rows(ref, d, n, h):
        return ref[d, pl.ds(layers * n + 8 * h, 8), :]

    x_chain = []
    for h in halves:
        c = [rows(xm_recv, d, 0, h) for d in range(nx)]
        w = [rows(xm_recv, d, 2, h) + rows(xm_recv, d + 1, 1, h) for d in range(nx - 1)]
        x_chain.append(reduce_matrix(c, w + [zero])[3])

    def ends(s_left, s_right, h, base, kept):
        inv, tl, tr = kept[RUNS - 1]
        s_last = base[RUNS - 1] + tl * s_left + tr * s_right
        s = expand(
            RUNS, lambda k: base[k], lambda k: kept[k][1], lambda k: kept[k][2], s_left, s_last
        )
        for n in range(RUNS):
            put(node_w, n, h, s[n])
            put(node_c, n, h, s[n - 1])

    def fill(l, base, tl, tr):
        s = expand(
            CELLS,
            lambda k: base[l, k],
            lambda k: tl[l, k],
            lambda k: tr[l, k],
            node_c[at(l), :],
            node_w[at(l), :],
        )
        return [s[n] for n in range(CELLS)]

    def fill_x(ls):
        lines = [turned(jnp.stack(fill(l, xi_v, xl_v, xr_v))) for l in ls]
        for u, l in enumerate(ls):
            q_v[l] = lines[u]
        for l in ls:
            sx = strided(q_v, l)
            b = [wr_v[l, n] * sx[n] - ly_v[l, n] for n in range(CELLS)]
            b, g, base = reduce_rhs(b, lambda k: (yi_v[l, k], yl_v[l, k], yr_v[l, k]))
            for k in base:
                yi_v[l, k] = base[k]
            node_b[at(l), :], node_g[at(l), :] = b, g

    y_base, y_own, pr_copies, b_mids = [], [], [], []

    def join_pair(h):
        pr_copies[h].wait_recv()
        other = [pr_recv[h, pl.ds(8 * n, 8), :] for n in range(2)]
        (gl_a, gl_b), (gr_a, gr_b) = [sides_of(x, y) for x, y in zip(y_own[h], other)]
        b_mid = gr_a + gl_b
        inv, tl, tr = mids[h]
        yr_send[h, pl.ds(0, 8), :] = gl_a + b_mid * tl
        yr_send[h, pl.ds(8, 8), :] = gr_b + b_mid * tr
        b_mids.append(b_mid)
        gather_y(yr_send.at[h], yr_recv.at[h], 9 + h)

    for h in halves:
        arrived(xr_recv.at[h], 3 + h, nx - 1)
        got = xr_recv.at[h]
        kept = x_chain[h]
        b = [got[d, pl.ds(8, 8), :] + got[d + 1, pl.ds(0, 8), :] for d in range(nx - 1)]
        base = reduce_rhs(b + [zero], lambda k: kept[k])[2]
        s = expand(
            nx, lambda k: base[k], lambda k: kept[k][1], lambda k: kept[k][2], zero, zero
        )
        for d in range(-1, nx):
            xs_v[d + 1, pl.ds(8 * h, 8), :] = s[d]
        part = pl.ds(8 * h, 8)
        ends(xs_v[ix, part, :], xs_v[ix + 1, part, :], h, x_base[h], x_kept[h])
        looped(4, 4, fill_x, 8 * h)
        if h:
            join_pair(0)
        looped(4, 4, fill_x, 8 * h + 4)
        values, base = segment_rhs(h, y_kept[h])
        for n, x in enumerate(values):
            pr_send[h, pl.ds(8 * n, 8), :] = x
        y_own.append(values)
        y_base.append(base)
        pr_copies.append(remote(pr_send.at[h], pr_recv.at[h], 7 + h, mate))
        pr_copies[h].start()

    join_pair(1)

    arrived(ym_recv, 6, chips - 1)
    y_chain = []
    for h in halves:
        c = [rows(ym_recv, d, 0, h) for d in range(chips)]
        w = [rows(ym_recv, d, 2, h) + rows(ym_recv, d + 1, 1, h) for d in range(chips - 1)]
        y_chain.append(reduce_matrix(c, w + [zero])[3])

    def chip_faces(h):
        arrived(yr_recv.at[h], 9 + h, chips - 1)
        got = yr_recv.at[h]
        kept = y_chain[h]
        b = [got[d, pl.ds(8, 8), :] + got[d + 1, pl.ds(0, 8), :] for d in range(chips - 1)]
        base = reduce_rhs(b + [zero], lambda k: kept[k])[2]
        s = expand(
            chips, lambda k: base[k], lambda k: kept[k][1], lambda k: kept[k][2], zero, zero
        )
        for d in range(-1, chips):
            ys_v[d + 1, pl.ds(8 * h, 8), :] = s[d]
        s_left, s_right = ys_v[chip, pl.ds(8 * h, 8), :], ys_v[chip + 1, pl.ds(8 * h, 8), :]
        inv, tl, tr = mids[h]
        s_mid = b_mids[h] * inv + tl * s_left + tr * s_right
        ends(mine((s_left, s_mid)), mine((s_mid, s_right)), h, y_base[h], y_kept[h])

    ez_v[...] = jnp.zeros_like(ez_v)

    def fill_y(ls):
        lines = [fill(l, yi_v, yl_v, yr_v) for l in ls]
        for u, l in enumerate(ls):
            for n in range(CELLS):
                b = wr_v[l, n] * lines[u][n] - lz_v[l, n] + ez_v[n]
                ez_v[n] = b * zt_v[l, n]
                zi_v[l, n] = b * zi_v[l, n]

    for h in halves:
        chip_faces(h)
        looped(8, 2, fill_y, 8 * h)

    for halo in halos:
        halo.wait_send()
    for copy in [pm_copy] + pr_copies:
        copy.wait_send()
    sent = [(xm_recv, 2, nx), (ym_recv, 6, chips)]
    for h in halves:
        sent += [(xr_recv.at[h], 3 + h, nx), (yr_recv.at[h], 9 + h, chips)]
    for ref, n, count in sent:
        part = ref.at[pl.ds(0, count - 1)]
        pltpu.make_async_copy(part, part, send_sem.at[n]).wait()


def layers_kernel(zi_v, zt_v, out, tmp_v, out_v, ez_v, out_sem):
    layers = zi_v.shape[0]
    group = 8
    ez_v[...] = jnp.zeros_like(ez_v)
    for l0 in range(layers - group, -1, -group):
        for l in range(l0 + group - 1, l0 - 1, -1):
            for k in range(CELLS):
                s = zi_v[l, k] + zt_v[l, k] * ez_v[k]
                ez_v[k] = s
                tmp_v[l - l0, pl.ds(k, RUNS, stride=CELLS), :] = s
        for l in range(l0 + group - 1, l0 - 1, -1):
            out_v[l] = tmp_v[l - l0].T.reshape(CELLS, RUNS, 128)
        for q in range(RUNS):
            pltpu.make_async_copy(
                out_v.at[pl.ds(l0, group), :, q, :],
                out.at[pl.ds(l0, group), pl.ds(CELLS * q, CELLS), :],
                out_sem,
            ).start()
    pltpu.make_async_copy(out_v, out_v, out_sem).wait()


def body(*args):
    layers, cells_x, cells_y = args[0].shape
    nx, ny = lax.axis_size("gx"), lax.axis_size("gy")
    f32, i32 = jnp.float32, jnp.int32
    tile = pltpu.VMEM((layers, TILE, 128), f32)
    runs = pltpu.VMEM((layers, CELLS, RUNS, 128), f32)
    index = pltpu.VMEM((layers, CELLS, RUNS, 128), i32)
    layer = pltpu.VMEM((CELLS, RUNS, 128), f32)
    halo = pltpu.VMEM((2, layers, 128), f32)

    def rows(*shape):
        return pltpu.VMEM((*shape, 128), f32)

    hbm = pl.BlockSpec(memory_space=pltpu.HBM)
    smem = pl.BlockSpec(memory_space=pltpu.SMEM)
    vmem = pl.BlockSpec(memory_space=pltpu.VMEM)
    shape = pltpu.VMEM((layers, CELLS, RUNS, 128), f32)
    zi, zt = pl.pallas_call(
        runs_kernel,
        out_shape=(shape, shape),
        in_specs=[hbm, hbm, hbm, smem, smem, hbm, hbm, smem, hbm, smem],
        out_specs=(vmem, vmem),
        scratch_shapes=[
            runs,
            runs,
            index,
            index,
            pltpu.VMEM((CELLS, RUNS, 128), i32),
            index,
            runs,
            runs,
            runs,
            runs,
            tile,
            tile,
            tile,
            tile,
            runs,
            runs,
            runs,
            runs,
            runs,
            runs,
            runs,
            layer,
            layer,
            layer,
            layer,
            layer,
            halo,
            halo,
            halo,
            halo,
            *[rows(RUNS * layers)] * 5,
            rows(3 * layers),
            rows(nx, 3 * layers),
            rows(2, layers),
            rows(2, nx, layers),
            rows(nx + 1, layers),
            rows(3 * layers),
            rows(3 * layers),
            rows(3 * layers),
            rows(ny // 2, 3 * layers),
            rows(2, layers),
            rows(2, layers),
            rows(2, layers),
            rows(2, ny // 2, layers),
            rows(ny // 2 + 1, layers),
            pltpu.SemaphoreType.DMA((6,)),
            pltpu.SemaphoreType.DMA((11,)),
            pltpu.SemaphoreType.DMA((11,)),
        ],
        compiler_params=pltpu.CompilerParams(
            collective_id=0, has_side_effects=True, vmem_limit_bytes=56 * 1024 * 1024
        ),
        cost_estimate=pl.CostEstimate(
            flops=100 * args[0].size, bytes_accessed=28 * args[0].size, transcendentals=0
        ),
        name="lines_xy",
    )(*args)
    return pl.pallas_call(
        layers_kernel,
        out_shape=jax.ShapeDtypeStruct(args[0].shape, f32),
        in_specs=[vmem, vmem],
        out_specs=hbm,
        scratch_shapes=[
            pltpu.VMEM((8, TILE, 128), f32),
            runs,
            layer,
            pltpu.SemaphoreType.DMA,
        ],
        compiler_params=pltpu.CompilerParams(vmem_limit_bytes=32 * 1024 * 1024),
        cost_estimate=pl.CostEstimate(
            flops=2 * args[0].size, bytes_accessed=12 * args[0].size, transcendentals=0
        ),
        name="columns_z",
    )(zi, zt)


def solution(mesh):
    field = P(None, "gx", "gy")
    in_specs = (field, field, field, P(), P(), field, P("gx", "gy"), P(), field, P())
    return jax.shard_map(body, mesh=mesh, in_specs=in_specs, out_specs=field, check_vma=False)
```

```python
import jax
import jax.numpy as jnp
from jax import lax
from jax.experimental import pallas as pl
from jax.experimental.pallas import tpu as pltpu
from jax.sharding import PartitionSpec as P

MESH = pl.DeviceIdType.MESH
HELD = 2.0**100
CELLS = 16
RUNS = 8
TILE = CELLS * RUNS
SIDE = 4


def far_first(steps, size):
    return sorted(steps, key=lambda step: -sum(min(d, n - d) for d, n in zip(step, size)))


def inverse(x):
    return pltpu.reciprocal(x, approx=True)


def order(count):
    steps = []
    stride = 1
    while stride < count:
        for node in range(stride - 1, count - 1, 2 * stride):
            steps.append((node, node - stride, node + stride))
        stride *= 2
    return steps


def plus(total, term):
    return term if total is None else total + term


def reduce_matrix(c, w):
    c, w, w_left, kept = list(c), list(w), None, {}
    for k, left, right in order(len(c)):
        inv = inverse(w[k] + (c[k] + c[right]))
        tl, tr = c[k] * inv, c[right] * inv
        c[right] = c[k] * tr
        if left < 0:
            w_left = plus(w_left, w[k] * tl)
        else:
            w[left] = w[left] + w[k] * tl
        w[right] = w[right] + w[k] * tr
        kept[k] = (inv, tl, tr)
    return c[-1], w[-1], w_left, kept


def reduce_rhs(b, kept):
    b, b_left, base = list(b), None, {}
    for k, left, right in order(len(b)):
        inv, tl, tr = kept(k)
        if left < 0:
            b_left = plus(b_left, b[k] * tl)
        else:
            b[left] = b[left] + b[k] * tl
        b[right] = b[right] + b[k] * tr
        base[k] = b[k] * inv
    return b[-1], b_left, base


def expand(count, base, tl, tr, s_left, s_last):
    s = {-1: s_left, count - 1: s_last}
    for k, left, right in reversed(order(count)):
        s[k] = base(k) + tl(k) * s[left] + tr(k) * s[right]
    return s


def take_out(c_left, c_right, w):
    inv = inverse(w + (c_left + c_right))
    tl, tr = c_left * inv, c_right * inv
    return c_left * tr, w * tl, w * tr, (inv, tl, tr)


def down(x):
    return pltpu.roll(x, 1, 0)


def up(x):
    return pltpu.roll(x, RUNS - 1, 0)


def looped(count, unroll, step, start=0):
    def body(i, _):
        step([start + i * unroll + u for u in range(unroll)])
        return 0

    lax.fori_loop(0, count // unroll, body, 0)


def runs_kernel(
    s_in,
    r_in,
    cls_in,
    k_tab,
    leak,
    well_in,
    rate_in,
    rate_tab,
    pit_in,
    level,
    zi_v,
    zt_v,
    s_v,
    w_v,
    cls_v,
    well_v,
    rate_v,
    pit_v,
    ra_v,
    xi_v,
    xl_v,
    xr_v,
    rat_v,
    st_v,
    wt_v,
    q_v,
    wr_v,
    ly_v,
    lz_v,
    fy_v,
    yi_v,
    yl_v,
    yr_v,
    pump_v,
    ez_v,
    flux_v,
    ra_c,
    s_c,
    lo_send,
    hi_send,
    lo_recv,
    hi_recv,
    node_w,
    node_c,
    node_e,
    node_b,
    node_g,
    xm_send,
    xm_recv,
    xr_send,
    xr_recv,
    xs_v,
    pm_send,
    pm_recv,
    ym_send,
    ym_recv,
    pr_send,
    pr_recv,
    yr_send,
    yr_recv,
    ys_v,
    in_sem,
    send_sem,
    recv_sem,
):
    layers = s_in.shape[0]
    ix, iy = lax.axis_index("gx"), lax.axis_index("gy")
    nx, ny = lax.axis_size("gx"), lax.axis_size("gy")
    core, chip = lax.rem(iy, 2), iy // 2
    mate = {"gy": iy + 1 - 2 * core}
    halves = range(layers // 8)

    sides = (nx // SIDE, SIDE)
    steps = [(p, q) for p in range(sides[0]) for q in range(sides[1])][1:]
    along_x = [
        lax.rem(ix // SIDE + p, sides[0]) * SIDE + lax.rem(lax.rem(ix, SIDE) + q, SIDE)
        for p, q in far_first(steps, sides)
    ]
    chips = ny // 2
    steps = [(p,) for p in range(1, chips)]
    along_y = [lax.rem(iy + 2 * p, ny) for (p,) in far_first(steps, (chips,))]
    before, after = lax.rem(iy + ny - 1, ny), lax.rem(iy + 1, ny)

    barrier = pltpu.get_barrier_semaphore()
    greeted = [{"gx": d} for d in along_x] + [{"gy": d} for d in along_y + [before, after]]
    for where in greeted:
        pl.semaphore_signal(barrier, inc=1, device_id=where, device_id_type=MESH)

    fields = [(cls_in, cls_v), (s_in, s_v), (r_in, w_v), (pit_in, pit_v), (well_in, well_v)]
    for n, (src, dst) in enumerate(fields):
        for q in range(RUNS):
            pltpu.make_async_copy(
                src.at[:, pl.ds(CELLS * q, CELLS), :], dst.at[:, :, q, :], in_sem.at[n]
            ).start()
    for q in range(RUNS):
        pltpu.make_async_copy(
            rate_in.at[pl.ds(CELLS * q, CELLS), :], rate_v.at[:, q, :], in_sem.at[5]
        ).start()

    def loaded(n):
        ref = fields[n][1] if n < 5 else rate_v
        pltpu.make_async_copy(ref, ref, in_sem.at[n]).wait()

    def remote(src, dst, n, where):
        return pltpu.make_async_remote_copy(
            src_ref=src,
            dst_ref=dst,
            send_sem=send_sem.at[n],
            recv_sem=recv_sem.at[n],
            device_id=where,
            device_id_type=MESH,
        )

    sub = lax.broadcasted_iota(jnp.int32, (RUNS, 128), 0)
    first, final = sub == 0, sub == RUNS - 1

    def at(l):
        return pl.ds(pl.multiple_of(l * RUNS, RUNS), RUNS)

    def turned(x):
        return x.reshape(TILE, 128).T

    def strided(ref, l):
        return [ref[l, pl.ds(n, RUNS, stride=CELLS), :] for n in range(CELLS)]

    ra_tab = [0.5 / jnp.full((RUNS, 128), k_tab[n], jnp.float32) for n in range(8)]
    ra_tab = [jnp.broadcast_to(t[:1], (TILE, 128)).reshape(CELLS, RUNS, 128) for t in ra_tab]
    loaded(0)
    loaded(1)

    def look(ls):
        ras = []
        for l in ls:
            cls = cls_v[l]
            odd, two, four = (cls & 1) != 0, (cls & 2) != 0, cls >= 4
            pairs = [jnp.where(odd, ra_tab[n + 1], ra_tab[n]) for n in (0, 2, 4, 6)]
            ras.append(
                jnp.where(
                    four,
                    jnp.where(two, pairs[3], pairs[2]),
                    jnp.where(two, pairs[1], pairs[0]),
                )
            )
        ss = [s_v[l] for l in ls]
        turned_ra = [turned(x) for x in ras]
        turned_s = [turned(x) for x in ss]
        for u, l in enumerate(ls):
            ra_v[l] = ras[u]
            rat_v[l] = turned_ra[u]
            st_v[l] = turned_s[u]

    looped(layers, 4, look)
    lo_send[0] = st_v[:, 0, :]
    lo_send[1] = rat_v[:, 0, :]
    hi_send[0] = st_v[:, TILE - 1, :]
    hi_send[1] = rat_v[:, TILE - 1, :]

    loaded(2)
    loaded(3)
    own_x = jnp.where(ix == 0, 1.0, 0.0)

    def weigh(ls):
        ws = []
        for l in ls:
            pit = pit_v[l] == 1
            w = jnp.where(pit, HELD, inverse(w_v[l]))
            ws.append(w)
            s_v[l] = w * jnp.where(pit, level[l], s_v[l])
        for u, l in enumerate(ls):
            ra, w = [ra_v[l, n] for n in range(CELLS)], [ws[u][n] for n in range(CELLS)]
            w_v[l] = ws[u]
            c = [inverse(ra[0] + jnp.where(first, own_x * ra[0], down(ra[15])))]
            c += [inverse(ra[n] + ra[n + 1]) for n in range(CELLS - 1)]
            c, w, e, kept = reduce_matrix(c, w)
            for k in kept:
                xi_v[l, k], xl_v[l, k], xr_v[l, k] = kept[k]
            node_w[at(l), :], node_c[at(l), :], node_e[at(l), :] = w, c, e

    looped(layers, 4, weigh)

    def nodes(ref, h):
        return [ref[pl.ds(n + 64 * h, 8, stride=RUNS), :] for n in range(RUNS)]

    def put(ref, n, h, x):
        ref[pl.ds(n + 64 * h, 8, stride=RUNS), :] = x

    def join(w, extra):
        return [w[n] + extra[n + 1] for n in range(RUNS - 1)] + [w[RUNS - 1]]

    def segment(h, c_end):
        extra = nodes(node_e, h)
        c, w, e, kept = reduce_matrix(nodes(node_c, h), join(nodes(node_w, h), extra))
        c, w_left, w_right, last = take_out(c, c_end, w)
        kept[RUNS - 1] = last
        return (c, extra[0] + e + w_left, w_right), kept

    def segment_rhs(h, kept):
        extra = nodes(node_g, h)
        b, g, base = reduce_rhs(join(nodes(node_b, h), extra), lambda k: kept[k])
        inv, tl, tr = kept[RUNS - 1]
        base[RUNS - 1] = b * inv
        return (extra[0] + g + b * tl, b * tr), base

    pl.semaphore_wait(barrier, len(greeted))
    halos = [
        remote(lo_send, hi_recv, 0, {"gy": before}),
        remote(hi_send, lo_recv, 1, {"gy": after}),
    ]
    for halo in halos:
        halo.start()

    x_kept = []
    end_x = jnp.where(ix == nx - 1, 2.0, 1.0)
    for h in halves:
        values, kept = segment(h, inverse(end_x * ra_v[pl.ds(8 * h, 8), CELLS - 1, RUNS - 1, :]))
        for n, x in enumerate(values):
            xm_send[pl.ds(layers * n + 8 * h, 8), :] = x
        x_kept.append(kept)

    def gather_x(src, dst, n):
        for other in along_x:
            remote(src, dst.at[ix], n, {"gx": other}).start()
        dst[ix] = src[...]

    def gather_y(src, dst, n):
        for other in along_y:
            remote(src, dst.at[chip], n, {"gy": other}).start()
        dst[chip] = src[...]

    def arrived(dst, n, count):
        ref = dst.at[pl.ds(0, count)]
        pltpu.make_async_copy(ref, ref, recv_sem.at[n]).wait()

    gather_x(xm_send, xm_recv, 2)

    flux_v[...] = jnp.zeros_like(flux_v)
    own_y = jnp.where(iy == 0, 1.0, 0.0)
    for n in range(CELLS):
        ra_c[n] = rat_v[0, pl.ds(n, RUNS, stride=CELLS), :]
        s_c[n] = st_v[0, pl.ds(n, RUNS, stride=CELLS), :]

    def across(ls):
        ra = [ra_c[n] for n in range(CELLS)]
        s = [s_c[n] for n in range(CELLS)]
        for l in ls:
            above = jnp.minimum(l + 1, layers - 1)
            leak_l = jnp.where(l < layers - 1, leak[jnp.minimum(l, layers - 2)], 0.0)
            ra_up, s_up = strided(rat_v, above), strided(st_v, above)
            ra_before = down(ra[15])
            face = inverse(ra[0] + jnp.where(first, own_y * ra[0], ra_before))
            fy_v[l, 0] = face
            flux_left = jnp.where(first, 0.0, face * (s[0] - down(s[15])))
            flux = flux_left
            for n in range(CELLS):
                if n < CELLS - 1:
                    face = inverse(ra[n] + ra[n + 1])
                    fy_v[l, n + 1] = face
                    flux_next = face * (s[n + 1] - s[n])
                else:
                    flux_next = up(flux_left)
                ly = flux_next - flux
                flux = flux_next
                face_z = leak_l * inverse(ra[n] + ra_up[n])
                flux_z = face_z * (s_up[n] - s[n])
                lz = flux_z - flux_v[n]
                flux_v[n] = flux_z
                ly_v[l, n] = ly
                lz_v[l, n] = lz
                q_v[l, pl.ds(n, RUNS, stride=CELLS), :] = ly + lz
                zt_v[l, n] = face_z
            ra, s = ra_up, s_up
        for n in range(CELLS):
            ra_c[n], s_c[n] = ra[n], s[n]

    looped(layers, 4, across)

    loaded(4)
    loaded(5)
    rate = rate_v[...]
    pump = jnp.full(rate.shape, rate_tab[0], jnp.float32)
    for n in range(1, 16):
        pump = jnp.where(rate == n, rate_tab[n], pump)
    pump_v[...] = pump

    for halo in halos:
        halo.wait_recv()
    at_lo, at_hi = iy == 0, iy == ny - 1
    s_lo = jnp.where(at_lo, 0.0, lo_recv[0])
    ra_lo = jnp.where(at_lo, lo_send[1], lo_recv[1])
    s_hi = jnp.where(at_hi, 0.0, hi_recv[0])
    ra_hi = jnp.where(at_hi, hi_send[1], hi_recv[1])
    flux_lo = inverse(ra_lo + lo_send[1]) * (lo_send[0] - s_lo)
    flux_hi = inverse(ra_hi + hi_send[1]) * (s_hi - hi_send[0])
    q_v[:, 0, :] = q_v[:, 0, :] - flux_lo
    q_v[:, TILE - 1, :] = q_v[:, TILE - 1, :] + flux_hi
    ly_v[:, 0, 0, :] = ly_v[:, 0, 0, :] - flux_lo
    ly_v[:, CELLS - 1, RUNS - 1, :] = ly_v[:, CELLS - 1, RUNS - 1, :] + flux_hi

    def runs_x(ls):
        qs = [q_v[l].T.reshape(CELLS, RUNS, 128) for l in ls]
        bs = []
        for u, l in enumerate(ls):
            pumped = well_v[l].astype(jnp.float32) * pump_v[...]
            bs.append(s_v[l] + (qs[u] + pumped))
        for u, l in enumerate(ls):
            b, g, base = reduce_rhs(
                [bs[u][n] for n in range(CELLS)], lambda k: (xi_v[l, k], xl_v[l, k], xr_v[l, k])
            )
            for k in base:
                xi_v[l, k] = base[k]
            node_b[at(l), :], node_g[at(l), :] = b, g

    x_base = []
    for h in halves:
        looped(8, 4, runs_x, 8 * h)
        values, base = segment_rhs(h, x_kept[h])
        for n, x in enumerate(values):
            xr_send[h, pl.ds(8 * n, 8), :] = x
        x_base.append(base)
        gather_x(xr_send.at[h], xr_recv.at[h], 3 + h)

    ez_v[...] = jnp.zeros_like(ez_v)

    def runs_y(ls):
        wts = [turned(w_v[l]) for l in ls]
        for u, l in enumerate(ls):
            wt_v[l] = wts[u]
        for l in ls:
            wt = strided(wt_v, l)
            c, w, e, kept = reduce_matrix([fy_v[l, n] for n in range(CELLS)], wt)
            for k in kept:
                yi_v[l, k], yl_v[l, k], yr_v[l, k] = kept[k]
            node_w[at(l), :], node_c[at(l), :], node_e[at(l), :] = w, c, e
            for n in range(CELLS):
                wr_v[l, n] = wt[n]
                e = wt[n] + ez_v[n]
                inv = inverse(e + zt_v[l, n])
                t = zt_v[l, n] * inv
                zt_v[l, n] = t
                zi_v[l, n] = inv
                ez_v[n] = e * t

    looped(layers, 4, runs_y)

    is_a = core == 0

    def mine(pair):
        return jnp.where(is_a, pair[0], pair[1])

    def theirs(pair):
        return jnp.where(is_a, pair[1], pair[0])

    y_kept, y_values = [], []
    end_y = jnp.where(iy == ny - 1, 2.0, 1.0)
    for h in halves:
        values, kept = segment(h, inverse(end_y * hi_send[1, pl.ds(8 * h, 8), :]))
        y_values.append(values)
        y_kept.append(kept)
    for h in halves:
        for n, x in enumerate(y_values[h]):
            pm_send[pl.ds(layers * n + 8 * h, 8), :] = x
    pm_copy = remote(pm_send, pm_recv, 5, mate)
    pm_copy.start()
    pm_copy.wait_recv()

    def sides_of(own, other):
        return mine((own, other)), theirs((own, other))

    mids = []
    for h in halves:
        other = [pm_recv[pl.ds(layers * n + 8 * h, 8), :] for n in range(3)]
        c, e, w = [sides_of(x, y) for x, y in zip(y_values[h], other)]
        joined, w_left, w_right, mid = take_out(c[0], c[1], w[0] + e[1])
        for n, x in enumerate((joined, e[0] + w_left, w[1] + w_right)):
            ym_send[pl.ds(layers * n + 8 * h, 8), :] = x
        mids.append(mid)
    gather_y(ym_send, ym_recv, 6)

    arrived(xm_recv, 2, nx - 1)
    zero = jnp.zeros((RUNS, 128), jnp.float32)

    def rows(ref, d, n, h):
        return ref[d, pl.ds(layers * n + 8 * h, 8), :]

    x_chain = []
    for h in halves:
        c = [rows(xm_recv, d, 0, h) for d in range(nx)]
        w = [rows(xm_recv, d, 2, h) + rows(xm_recv, d + 1, 1, h) for d in range(nx - 1)]
        x_chain.append(reduce_matrix(c, w + [zero])[3])

    def ends(s_left, s_right, h, base, kept):
        inv, tl, tr = kept[RUNS - 1]
        s_last = base[RUNS - 1] + tl * s_left + tr * s_right
        s = expand(
            RUNS, lambda k: base[k], lambda k: kept[k][1], lambda k: kept[k][2], s_left, s_last
        )
        for n in range(RUNS):
            put(node_w, n, h, s[n])
            put(node_c, n, h, s[n - 1])

    def fill(l, base, tl, tr):
        s = expand(
            CELLS,
            lambda k: base[l, k],
            lambda k: tl[l, k],
            lambda k: tr[l, k],
            node_c[at(l), :],
            node_w[at(l), :],
        )
        return [s[n] for n in range(CELLS)]

    def fill_x(ls):
        lines = [turned(jnp.stack(fill(l, xi_v, xl_v, xr_v))) for l in ls]
        for u, l in enumerate(ls):
            q_v[l] = lines[u]
        for l in ls:
            sx = strided(q_v, l)
            b = [wr_v[l, n] * sx[n] - ly_v[l, n] for n in range(CELLS)]
            b, g, base = reduce_rhs(b, lambda k: (yi_v[l, k], yl_v[l, k], yr_v[l, k]))
            for k in base:
                yi_v[l, k] = base[k]
            node_b[at(l), :], node_g[at(l), :] = b, g

    y_base, y_own, pr_copies, b_mids = [], [], [], []

    def join_pair(h):
        pr_copies[h].wait_recv()
        other = [pr_recv[h, pl.ds(8 * n, 8), :] for n in range(2)]
        (gl_a, gl_b), (gr_a, gr_b) = [sides_of(x, y) for x, y in zip(y_own[h], other)]
        b_mid = gr_a + gl_b
        inv, tl, tr = mids[h]
        yr_send[h, pl.ds(0, 8), :] = gl_a + b_mid * tl
        yr_send[h, pl.ds(8, 8), :] = gr_b + b_mid * tr
        b_mids.append(b_mid)
        gather_y(yr_send.at[h], yr_recv.at[h], 9 + h)

    for h in halves:
        arrived(xr_recv.at[h], 3 + h, nx - 1)
        got = xr_recv.at[h]
        kept = x_chain[h]
        b = [got[d, pl.ds(8, 8), :] + got[d + 1, pl.ds(0, 8), :] for d in range(nx - 1)]
        base = reduce_rhs(b + [zero], lambda k: kept[k])[2]
        s = expand(
            nx, lambda k: base[k], lambda k: kept[k][1], lambda k: kept[k][2], zero, zero
        )
        for d in range(-1, nx):
            xs_v[d + 1, pl.ds(8 * h, 8), :] = s[d]
        part = pl.ds(8 * h, 8)
        ends(xs_v[ix, part, :], xs_v[ix + 1, part, :], h, x_base[h], x_kept[h])
        looped(4, 4, fill_x, 8 * h)
        if h:
            join_pair(0)
        looped(4, 4, fill_x, 8 * h + 4)
        values, base = segment_rhs(h, y_kept[h])
        for n, x in enumerate(values):
            pr_send[h, pl.ds(8 * n, 8), :] = x
        y_own.append(values)
        y_base.append(base)
        pr_copies.append(remote(pr_send.at[h], pr_recv.at[h], 7 + h, mate))
        pr_copies[h].start()

    join_pair(1)

    arrived(ym_recv, 6, chips - 1)
    y_chain = []
    for h in halves:
        c = [rows(ym_recv, d, 0, h) for d in range(chips)]
        w = [rows(ym_recv, d, 2, h) + rows(ym_recv, d + 1, 1, h) for d in range(chips - 1)]
        y_chain.append(reduce_matrix(c, w + [zero])[3])

    def chip_faces(h):
        arrived(yr_recv.at[h], 9 + h, chips - 1)
        got = yr_recv.at[h]
        kept = y_chain[h]
        b = [got[d, pl.ds(8, 8), :] + got[d + 1, pl.ds(0, 8), :] for d in range(chips - 1)]
        base = reduce_rhs(b + [zero], lambda k: kept[k])[2]
        s = expand(
            chips, lambda k: base[k], lambda k: kept[k][1], lambda k: kept[k][2], zero, zero
        )
        for d in range(-1, chips):
            ys_v[d + 1, pl.ds(8 * h, 8), :] = s[d]
        s_left, s_right = ys_v[chip, pl.ds(8 * h, 8), :], ys_v[chip + 1, pl.ds(8 * h, 8), :]
        inv, tl, tr = mids[h]
        s_mid = b_mids[h] * inv + tl * s_left + tr * s_right
        ends(mine((s_left, s_mid)), mine((s_mid, s_right)), h, y_base[h], y_kept[h])

    ez_v[...] = jnp.zeros_like(ez_v)

    def fill_y(ls):
        lines = [fill(l, yi_v, yl_v, yr_v) for l in ls]
        for u, l in enumerate(ls):
            for n in range(CELLS):
                b = wr_v[l, n] * lines[u][n] - lz_v[l, n] + ez_v[n]
                ez_v[n] = b * zt_v[l, n]
                zi_v[l, n] = b * zi_v[l, n]

    for h in halves:
        chip_faces(h)
        looped(8, 2, fill_y, 8 * h)

    for halo in halos:
        halo.wait_send()
    for copy in [pm_copy] + pr_copies:
        copy.wait_send()
    sent = [(xm_recv, 2, nx), (ym_recv, 6, chips)]
    for h in halves:
        sent += [(xr_recv.at[h], 3 + h, nx), (yr_recv.at[h], 9 + h, chips)]
    for ref, n, count in sent:
        part = ref.at[pl.ds(0, count - 1)]
        pltpu.make_async_copy(part, part, send_sem.at[n]).wait()


def layers_kernel(zi_v, zt_v, out, tmp_v, out_v, ez_v, out_sem):
    layers = zi_v.shape[0]
    group = 8
    ez_v[...] = jnp.zeros_like(ez_v)
    for l0 in range(layers - group, -1, -group):
        for l in range(l0 + group - 1, l0 - 1, -1):
            for k in range(CELLS):
                s = zi_v[l, k] + zt_v[l, k] * ez_v[k]
                ez_v[k] = s
                tmp_v[l - l0, pl.ds(k, RUNS, stride=CELLS), :] = s
        for l in range(l0 + group - 1, l0 - 1, -1):
            out_v[l] = tmp_v[l - l0].T.reshape(CELLS, RUNS, 128)
        for q in range(RUNS):
            pltpu.make_async_copy(
                out_v.at[pl.ds(l0, group), :, q, :],
                out.at[pl.ds(l0, group), pl.ds(CELLS * q, CELLS), :],
                out_sem,
            ).start()
    pltpu.make_async_copy(out_v, out_v, out_sem).wait()


def body(*args):
    layers, cells_x, cells_y = args[0].shape
    nx, ny = lax.axis_size("gx"), lax.axis_size("gy")
    f32, i32 = jnp.float32, jnp.int32
    tile = pltpu.VMEM((layers, TILE, 128), f32)
    runs = pltpu.VMEM((layers, CELLS, RUNS, 128), f32)
    index = pltpu.VMEM((layers, CELLS, RUNS, 128), i32)
    layer = pltpu.VMEM((CELLS, RUNS, 128), f32)
    halo = pltpu.VMEM((2, layers, 128), f32)

    def rows(*shape):
        return pltpu.VMEM((*shape, 128), f32)

    hbm = pl.BlockSpec(memory_space=pltpu.HBM)
    smem = pl.BlockSpec(memory_space=pltpu.SMEM)
    vmem = pl.BlockSpec(memory_space=pltpu.VMEM)
    shape = pltpu.VMEM((layers, CELLS, RUNS, 128), f32)
    zi, zt = pl.pallas_call(
        runs_kernel,
        out_shape=(shape, shape),
        in_specs=[hbm, hbm, hbm, smem, smem, hbm, hbm, smem, hbm, smem],
        out_specs=(vmem, vmem),
        scratch_shapes=[
            runs,
            runs,
            index,
            index,
            pltpu.VMEM((CELLS, RUNS, 128), i32),
            index,
            runs,
            runs,
            runs,
            runs,
            tile,
            tile,
            tile,
            tile,
            runs,
            runs,
            runs,
            runs,
            runs,
            runs,
            runs,
            layer,
            layer,
            layer,
            layer,
            layer,
            halo,
            halo,
            halo,
            halo,
            *[rows(RUNS * layers)] * 5,
            rows(3 * layers),
            rows(nx, 3 * layers),
            rows(2, layers),
            rows(2, nx, layers),
            rows(nx + 1, layers),
            rows(3 * layers),
            rows(3 * layers),
            rows(3 * layers),
            rows(ny // 2, 3 * layers),
            rows(2, layers),
            rows(2, layers),
            rows(2, layers),
            rows(2, ny // 2, layers),
            rows(ny // 2 + 1, layers),
            pltpu.SemaphoreType.DMA((6,)),
            pltpu.SemaphoreType.DMA((11,)),
            pltpu.SemaphoreType.DMA((11,)),
        ],
        compiler_params=pltpu.CompilerParams(
            collective_id=0, has_side_effects=True, vmem_limit_bytes=56 * 1024 * 1024
        ),
        cost_estimate=pl.CostEstimate(
            flops=100 * args[0].size, bytes_accessed=28 * args[0].size, transcendentals=0
        ),
        name="lines_xy",
    )(*args)
    return pl.pallas_call(
        layers_kernel,
        out_shape=jax.ShapeDtypeStruct(args[0].shape, f32),
        in_specs=[vmem, vmem],
        out_specs=hbm,
        scratch_shapes=[
            pltpu.VMEM((8, TILE, 128), f32),
            runs,
            layer,
            pltpu.SemaphoreType.DMA,
        ],
        compiler_params=pltpu.CompilerParams(vmem_limit_bytes=32 * 1024 * 1024),
        cost_estimate=pl.CostEstimate(
            flops=2 * args[0].size, bytes_accessed=12 * args[0].size, transcendentals=0
        ),
        name="columns_z",
    )(zi, zt)


def solution(mesh):
    field = P(None, "gx", "gy")
    in_specs = (field, field, field, P(), P(), field, P("gx", "gy"), P(), field, P())
    return jax.shard_map(body, mesh=mesh, in_specs=in_specs, out_specs=field, check_vma=False)
```

```python
import jax
import jax.numpy as jnp
from jax import lax
from jax.experimental import pallas as pl
from jax.experimental.pallas import tpu as pltpu
from jax.sharding import PartitionSpec as P

MESH = pl.DeviceIdType.MESH
HELD = 2.0**100
CELLS = 16
RUNS = 8
TILE = CELLS * RUNS
SIDE = 4


def far_first(steps, size):
    return sorted(steps, key=lambda step: -sum(min(d, n - d) for d, n in zip(step, size)))


def inverse(x):
    return pltpu.reciprocal(x, approx=True)


def order(count):
    steps = []
    stride = 1
    while stride < count:
        for node in range(stride - 1, count - 1, 2 * stride):
            steps.append((node, node - stride, node + stride))
        stride *= 2
    return steps


def plus(total, term):
    return term if total is None else total + term


def reduce_matrix(c, w):
    c, w, w_left, kept = list(c), list(w), None, {}
    for k, left, right in order(len(c)):
        inv = inverse(w[k] + (c[k] + c[right]))
        tl, tr = c[k] * inv, c[right] * inv
        c[right] = c[k] * tr
        if left < 0:
            w_left = plus(w_left, w[k] * tl)
        else:
            w[left] = w[left] + w[k] * tl
        w[right] = w[right] + w[k] * tr
        kept[k] = (inv, tl, tr)
    return c[-1], w[-1], w_left, kept


def reduce_rhs(b, kept):
    b, b_left, base = list(b), None, {}
    for k, left, right in order(len(b)):
        inv, tl, tr = kept(k)
        if left < 0:
            b_left = plus(b_left, b[k] * tl)
        else:
            b[left] = b[left] + b[k] * tl
        b[right] = b[right] + b[k] * tr
        base[k] = b[k] * inv
    return b[-1], b_left, base


def expand(count, base, tl, tr, s_left, s_last):
    s = {-1: s_left, count - 1: s_last}
    for k, left, right in reversed(order(count)):
        s[k] = base(k) + tl(k) * s[left] + tr(k) * s[right]
    return s


def take_out(c_left, c_right, w):
    inv = inverse(w + (c_left + c_right))
    tl, tr = c_left * inv, c_right * inv
    return c_left * tr, w * tl, w * tr, (inv, tl, tr)


def down(x):
    return pltpu.roll(x, 1, 0)


def up(x):
    return pltpu.roll(x, RUNS - 1, 0)


def looped(count, unroll, step, start=0):
    def body(i, _):
        step([start + i * unroll + u for u in range(unroll)])
        return 0

    lax.fori_loop(0, count // unroll, body, 0)


def runs_kernel(
    s_in,
    r_in,
    cls_in,
    k_tab,
    leak,
    well_in,
    rate_in,
    rate_tab,
    pit_in,
    level,
    zi_v,
    zt_v,
    s_v,
    w_v,
    cls_v,
    well_v,
    rate_v,
    pit_v,
    ra_v,
    xi_v,
    xl_v,
    xr_v,
    rat_v,
    st_v,
    wt_v,
    q_v,
    wr_v,
    ly_v,
    lz_v,
    fy_v,
    yi_v,
    yl_v,
    yr_v,
    pump_v,
    ez_v,
    flux_v,
    ra_c,
    s_c,
    lo_send,
    hi_send,
    lo_recv,
    hi_recv,
    node_w,
    node_c,
    node_e,
    node_b,
    node_g,
    xm_send,
    xm_recv,
    xr_send,
    xr_recv,
    xs_v,
    pm_send,
    pm_recv,
    ym_send,
    ym_recv,
    pr_send,
    pr_recv,
    yr_send,
    yr_recv,
    ys_v,
    in_sem,
    send_sem,
    recv_sem,
):
    layers = s_in.shape[0]
    ix, iy = lax.axis_index("gx"), lax.axis_index("gy")
    nx, ny = lax.axis_size("gx"), lax.axis_size("gy")
    core, chip = lax.rem(iy, 2), iy // 2
    mate = {"gy": iy + 1 - 2 * core}
    halves = range(layers // 8)

    sides = (nx // SIDE, SIDE)
    steps = [(p, q) for p in range(sides[0]) for q in range(sides[1])][1:]
    along_x = [
        lax.rem(ix // SIDE + p, sides[0]) * SIDE + lax.rem(lax.rem(ix, SIDE) + q, SIDE)
        for p, q in far_first(steps, sides)
    ]
    chips = ny // 2
    steps = [(p,) for p in range(1, chips)]
    along_y = [lax.rem(iy + 2 * p, ny) for (p,) in far_first(steps, (chips,))]
    before, after = lax.rem(iy + ny - 1, ny), lax.rem(iy + 1, ny)

    barrier = pltpu.get_barrier_semaphore()
    greeted = [{"gx": d} for d in along_x] + [{"gy": d} for d in along_y + [before, after]]
    for where in greeted:
        pl.semaphore_signal(barrier, inc=1, device_id=where, device_id_type=MESH)

    fields = [(cls_in, cls_v), (s_in, s_v), (r_in, w_v), (pit_in, pit_v), (well_in, well_v)]
    for n, (src, dst) in enumerate(fields):
        for q in range(RUNS):
            pltpu.make_async_copy(
                src.at[:, pl.ds(CELLS * q, CELLS), :], dst.at[:, :, q, :], in_sem.at[n]
            ).start()
    for q in range(RUNS):
        pltpu.make_async_copy(
            rate_in.at[pl.ds(CELLS * q, CELLS), :], rate_v.at[:, q, :], in_sem.at[5]
        ).start()

    def loaded(n):
        ref = fields[n][1] if n < 5 else rate_v
        pltpu.make_async_copy(ref, ref, in_sem.at[n]).wait()

    def remote(src, dst, n, where):
        return pltpu.make_async_remote_copy(
            src_ref=src,
            dst_ref=dst,
            send_sem=send_sem.at[n],
            recv_sem=recv_sem.at[n],
            device_id=where,
            device_id_type=MESH,
        )

    sub = lax.broadcasted_iota(jnp.int32, (RUNS, 128), 0)
    first, final = sub == 0, sub == RUNS - 1

    def at(l):
        return pl.ds(pl.multiple_of(l * RUNS, RUNS), RUNS)

    def turned(x):
        return x.reshape(TILE, 128).T

    def strided(ref, l):
        return [ref[l, pl.ds(n, RUNS, stride=CELLS), :] for n in range(CELLS)]

    ra_tab = [0.5 / jnp.full((RUNS, 128), k_tab[n], jnp.float32) for n in range(8)]
    ra_tab = [jnp.broadcast_to(t[:1], (TILE, 128)).reshape(CELLS, RUNS, 128) for t in ra_tab]
    loaded(0)
    loaded(1)

    def look(ls):
        ras = []
        for l in ls:
            cls = cls_v[l]
            odd, two, four = (cls & 1) != 0, (cls & 2) != 0, cls >= 4
            pairs = [jnp.where(odd, ra_tab[n + 1], ra_tab[n]) for n in (0, 2, 4, 6)]
            ras.append(
                jnp.where(
                    four,
                    jnp.where(two, pairs[3], pairs[2]),
                    jnp.where(two, pairs[1], pairs[0]),
                )
            )
        ss = [s_v[l] for l in ls]
        turned_ra = [turned(x) for x in ras]
        turned_s = [turned(x) for x in ss]
        for u, l in enumerate(ls):
            ra_v[l] = ras[u]
            rat_v[l] = turned_ra[u]
            st_v[l] = turned_s[u]

    looped(layers, 4, look)
    lo_send[0] = st_v[:, 0, :]
    lo_send[1] = rat_v[:, 0, :]
    hi_send[0] = st_v[:, TILE - 1, :]
    hi_send[1] = rat_v[:, TILE - 1, :]

    loaded(2)
    loaded(3)
    own_x = jnp.where(ix == 0, 1.0, 0.0)

    def weigh(ls):
        ws = []
        for l in ls:
            pit = pit_v[l] == 1
            w = jnp.where(pit, HELD, inverse(w_v[l]))
            ws.append(w)
            s_v[l] = w * jnp.where(pit, level[l], s_v[l])
        for u, l in enumerate(ls):
            ra, w = [ra_v[l, n] for n in range(CELLS)], [ws[u][n] for n in range(CELLS)]
            w_v[l] = ws[u]
            c = [inverse(ra[0] + jnp.where(first, own_x * ra[0], down(ra[15])))]
            c += [inverse(ra[n] + ra[n + 1]) for n in range(CELLS - 1)]
            c, w, e, kept = reduce_matrix(c, w)
            for k in kept:
                xi_v[l, k], xl_v[l, k], xr_v[l, k] = kept[k]
            node_w[at(l), :], node_c[at(l), :], node_e[at(l), :] = w, c, e

    looped(layers, 4, weigh)

    def nodes(ref, h):
        return [ref[pl.ds(n + 64 * h, 8, stride=RUNS), :] for n in range(RUNS)]

    def put(ref, n, h, x):
        ref[pl.ds(n + 64 * h, 8, stride=RUNS), :] = x

    def join(w, extra):
        return [w[n] + extra[n + 1] for n in range(RUNS - 1)] + [w[RUNS - 1]]

    def segment(h, c_end):
        extra = nodes(node_e, h)
        c, w, e, kept = reduce_matrix(nodes(node_c, h), join(nodes(node_w, h), extra))
        c, w_left, w_right, last = take_out(c, c_end, w)
        kept[RUNS - 1] = last
        return (c, extra[0] + e + w_left, w_right), kept

    def segment_rhs(h, kept):
        extra = nodes(node_g, h)
        b, g, base = reduce_rhs(join(nodes(node_b, h), extra), lambda k: kept[k])
        inv, tl, tr = kept[RUNS - 1]
        base[RUNS - 1] = b * inv
        return (extra[0] + g + b * tl, b * tr), base

    x_kept = []
    end_x = jnp.where(ix == nx - 1, 2.0, 1.0)
    for h in halves:
        values, kept = segment(h, inverse(end_x * ra_v[pl.ds(8 * h, 8), CELLS - 1, RUNS - 1, :]))
        for n, x in enumerate(values):
            xm_send[pl.ds(layers * n + 8 * h, 8), :] = x
        x_kept.append(kept)

    def gather_x(src, dst, n):
        for other in along_x:
            remote(src, dst.at[ix], n, {"gx": other}).start()
        dst[ix] = src[...]

    def gather_y(src, dst, n):
        for other in along_y:
            remote(src, dst.at[chip], n, {"gy": other}).start()
        dst[chip] = src[...]

    def arrived(dst, n, count):
        ref = dst.at[pl.ds(0, count)]
        pltpu.make_async_copy(ref, ref, recv_sem.at[n]).wait()

    pl.semaphore_wait(barrier, len(greeted))
    halos = [
        remote(lo_send, hi_recv, 0, {"gy": before}),
        remote(hi_send, lo_recv, 1, {"gy": after}),
    ]
    for halo in halos:
        halo.start()
    gather_x(xm_send, xm_recv, 2)

    flux_v[...] = jnp.zeros_like(flux_v)
    own_y = jnp.where(iy == 0, 1.0, 0.0)
    for n in range(CELLS):
        ra_c[n] = rat_v[0, pl.ds(n, RUNS, stride=CELLS), :]
        s_c[n] = st_v[0, pl.ds(n, RUNS, stride=CELLS), :]

    def across(ls):
        ra = [ra_c[n] for n in range(CELLS)]
        s = [s_c[n] for n in range(CELLS)]
        for l in ls:
            above = jnp.minimum(l + 1, layers - 1)
            leak_l = jnp.where(l < layers - 1, leak[jnp.minimum(l, layers - 2)], 0.0)
            ra_up, s_up = strided(rat_v, above), strided(st_v, above)
            ra_before = down(ra[15])
            face = inverse(ra[0] + jnp.where(first, own_y * ra[0], ra_before))
            fy_v[l, 0] = face
            flux_left = jnp.where(first, 0.0, face * (s[0] - down(s[15])))
            flux = flux_left
            for n in range(CELLS):
                if n < CELLS - 1:
                    face = inverse(ra[n] + ra[n + 1])
                    fy_v[l, n + 1] = face
                    flux_next = face * (s[n + 1] - s[n])
                else:
                    flux_next = up(flux_left)
                ly = flux_next - flux
                flux = flux_next
                face_z = leak_l * inverse(ra[n] + ra_up[n])
                flux_z = face_z * (s_up[n] - s[n])
                lz = flux_z - flux_v[n]
                flux_v[n] = flux_z
                ly_v[l, n] = ly
                lz_v[l, n] = lz
                q_v[l, pl.ds(n, RUNS, stride=CELLS), :] = ly + lz
                zt_v[l, n] = face_z
            ra, s = ra_up, s_up
        for n in range(CELLS):
            ra_c[n], s_c[n] = ra[n], s[n]

    looped(layers, 4, across)

    loaded(4)
    loaded(5)
    rate = rate_v[...]
    pump = jnp.full(rate.shape, rate_tab[0], jnp.float32)
    for n in range(1, 16):
        pump = jnp.where(rate == n, rate_tab[n], pump)
    pump_v[...] = pump

    for halo in halos:
        halo.wait_recv()
    at_lo, at_hi = iy == 0, iy == ny - 1
    s_lo = jnp.where(at_lo, 0.0, lo_recv[0])
    ra_lo = jnp.where(at_lo, lo_send[1], lo_recv[1])
    s_hi = jnp.where(at_hi, 0.0, hi_recv[0])
    ra_hi = jnp.where(at_hi, hi_send[1], hi_recv[1])
    flux_lo = inverse(ra_lo + lo_send[1]) * (lo_send[0] - s_lo)
    flux_hi = inverse(ra_hi + hi_send[1]) * (s_hi - hi_send[0])
    q_v[:, 0, :] = q_v[:, 0, :] - flux_lo
    q_v[:, TILE - 1, :] = q_v[:, TILE - 1, :] + flux_hi
    ly_v[:, 0, 0, :] = ly_v[:, 0, 0, :] - flux_lo
    ly_v[:, CELLS - 1, RUNS - 1, :] = ly_v[:, CELLS - 1, RUNS - 1, :] + flux_hi

    def runs_x(ls):
        qs = [q_v[l].T.reshape(CELLS, RUNS, 128) for l in ls]
        bs = []
        for u, l in enumerate(ls):
            pumped = well_v[l].astype(jnp.float32) * pump_v[...]
            bs.append(s_v[l] + (qs[u] + pumped))
        for u, l in enumerate(ls):
            b, g, base = reduce_rhs(
                [bs[u][n] for n in range(CELLS)], lambda k: (xi_v[l, k], xl_v[l, k], xr_v[l, k])
            )
            for k in base:
                xi_v[l, k] = base[k]
            node_b[at(l), :], node_g[at(l), :] = b, g

    x_base = []
    for h in halves:
        looped(8, 4, runs_x, 8 * h)
        values, base = segment_rhs(h, x_kept[h])
        for n, x in enumerate(values):
            xr_send[h, pl.ds(8 * n, 8), :] = x
        x_base.append(base)
        gather_x(xr_send.at[h], xr_recv.at[h], 3 + h)

    ez_v[...] = jnp.zeros_like(ez_v)

    def runs_y(ls):
        wts = [turned(w_v[l]) for l in ls]
        for u, l in enumerate(ls):
            wt_v[l] = wts[u]
        for l in ls:
            wt = strided(wt_v, l)
            c, w, e, kept = reduce_matrix([fy_v[l, n] for n in range(CELLS)], wt)
            for k in kept:
                yi_v[l, k], yl_v[l, k], yr_v[l, k] = kept[k]
            node_w[at(l), :], node_c[at(l), :], node_e[at(l), :] = w, c, e
            for n in range(CELLS):
                wr_v[l, n] = wt[n]
                e = wt[n] + ez_v[n]
                inv = inverse(e + zt_v[l, n])
                t = zt_v[l, n] * inv
                zt_v[l, n] = t
                zi_v[l, n] = inv
                ez_v[n] = e * t

    looped(layers, 4, runs_y)

    is_a = core == 0

    def mine(pair):
        return jnp.where(is_a, pair[0], pair[1])

    def theirs(pair):
        return jnp.where(is_a, pair[1], pair[0])

    y_kept, y_values = [], []
    end_y = jnp.where(iy == ny - 1, 2.0, 1.0)
    for h in halves:
        values, kept = segment(h, inverse(end_y * hi_send[1, pl.ds(8 * h, 8), :]))
        y_values.append(values)
        y_kept.append(kept)
    for h in halves:
        for n, x in enumerate(y_values[h]):
            pm_send[pl.ds(layers * n + 8 * h, 8), :] = x
    pm_copy = remote(pm_send, pm_recv, 5, mate)
    pm_copy.start()
    pm_copy.wait_recv()

    def sides_of(own, other):
        return mine((own, other)), theirs((own, other))

    mids = []
    for h in halves:
        other = [pm_recv[pl.ds(layers * n + 8 * h, 8), :] for n in range(3)]
        c, e, w = [sides_of(x, y) for x, y in zip(y_values[h], other)]
        joined, w_left, w_right, mid = take_out(c[0], c[1], w[0] + e[1])
        for n, x in enumerate((joined, e[0] + w_left, w[1] + w_right)):
            ym_send[pl.ds(layers * n + 8 * h, 8), :] = x
        mids.append(mid)
    gather_y(ym_send, ym_recv, 6)

    arrived(xm_recv, 2, nx - 1)
    zero = jnp.zeros((RUNS, 128), jnp.float32)

    def rows(ref, d, n, h):
        return ref[d, pl.ds(layers * n + 8 * h, 8), :]

    x_chain = []
    for h in halves:
        c = [rows(xm_recv, d, 0, h) for d in range(nx)]
        w = [rows(xm_recv, d, 2, h) + rows(xm_recv, d + 1, 1, h) for d in range(nx - 1)]
        x_chain.append(reduce_matrix(c, w + [zero])[3])

    def ends(s_left, s_right, h, base, kept):
        inv, tl, tr = kept[RUNS - 1]
        s_last = base[RUNS - 1] + tl * s_left + tr * s_right
        s = expand(
            RUNS, lambda k: base[k], lambda k: kept[k][1], lambda k: kept[k][2], s_left, s_last
        )
        for n in range(RUNS):
            put(node_w, n, h, s[n])
            put(node_c, n, h, s[n - 1])

    def fill(l, base, tl, tr):
        s = expand(
            CELLS,
            lambda k: base[l, k],
            lambda k: tl[l, k],
            lambda k: tr[l, k],
            node_c[at(l), :],
            node_w[at(l), :],
        )
        return [s[n] for n in range(CELLS)]

    def fill_x(ls):
        lines = [turned(jnp.stack(fill(l, xi_v, xl_v, xr_v))) for l in ls]
        for u, l in enumerate(ls):
            q_v[l] = lines[u]
        for l in ls:
            sx = strided(q_v, l)
            b = [wr_v[l, n] * sx[n] - ly_v[l, n] for n in range(CELLS)]
            b, g, base = reduce_rhs(b, lambda k: (yi_v[l, k], yl_v[l, k], yr_v[l, k]))
            for k in base:
                yi_v[l, k] = base[k]
            node_b[at(l), :], node_g[at(l), :] = b, g

    y_base, y_own, pr_copies, b_mids = [], [], [], []

    def join_pair(h):
        pr_copies[h].wait_recv()
        other = [pr_recv[h, pl.ds(8 * n, 8), :] for n in range(2)]
        (gl_a, gl_b), (gr_a, gr_b) = [sides_of(x, y) for x, y in zip(y_own[h], other)]
        b_mid = gr_a + gl_b
        inv, tl, tr = mids[h]
        yr_send[h, pl.ds(0, 8), :] = gl_a + b_mid * tl
        yr_send[h, pl.ds(8, 8), :] = gr_b + b_mid * tr
        b_mids.append(b_mid)
        gather_y(yr_send.at[h], yr_recv.at[h], 9 + h)

    for h in halves:
        arrived(xr_recv.at[h], 3 + h, nx - 1)
        got = xr_recv.at[h]
        kept = x_chain[h]
        b = [got[d, pl.ds(8, 8), :] + got[d + 1, pl.ds(0, 8), :] for d in range(nx - 1)]
        base = reduce_rhs(b + [zero], lambda k: kept[k])[2]
        s = expand(
            nx, lambda k: base[k], lambda k: kept[k][1], lambda k: kept[k][2], zero, zero
        )
        for d in range(-1, nx):
            xs_v[d + 1, pl.ds(8 * h, 8), :] = s[d]
        part = pl.ds(8 * h, 8)
        ends(xs_v[ix, part, :], xs_v[ix + 1, part, :], h, x_base[h], x_kept[h])
        looped(4, 4, fill_x, 8 * h)
        if h:
            join_pair(0)
        looped(4, 4, fill_x, 8 * h + 4)
        values, base = segment_rhs(h, y_kept[h])
        for n, x in enumerate(values):
            pr_send[h, pl.ds(8 * n, 8), :] = x
        y_own.append(values)
        y_base.append(base)
        pr_copies.append(remote(pr_send.at[h], pr_recv.at[h], 7 + h, mate))
        pr_copies[h].start()

    join_pair(1)

    arrived(ym_recv, 6, chips - 1)
    y_chain = []
    for h in halves:
        c = [rows(ym_recv, d, 0, h) for d in range(chips)]
        w = [rows(ym_recv, d, 2, h) + rows(ym_recv, d + 1, 1, h) for d in range(chips - 1)]
        y_chain.append(reduce_matrix(c, w + [zero])[3])

    def chip_faces(h):
        arrived(yr_recv.at[h], 9 + h, chips - 1)
        got = yr_recv.at[h]
        kept = y_chain[h]
        b = [got[d, pl.ds(8, 8), :] + got[d + 1, pl.ds(0, 8), :] for d in range(chips - 1)]
        base = reduce_rhs(b + [zero], lambda k: kept[k])[2]
        s = expand(
            chips, lambda k: base[k], lambda k: kept[k][1], lambda k: kept[k][2], zero, zero
        )
        for d in range(-1, chips):
            ys_v[d + 1, pl.ds(8 * h, 8), :] = s[d]
        s_left, s_right = ys_v[chip, pl.ds(8 * h, 8), :], ys_v[chip + 1, pl.ds(8 * h, 8), :]
        inv, tl, tr = mids[h]
        s_mid = b_mids[h] * inv + tl * s_left + tr * s_right
        ends(mine((s_left, s_mid)), mine((s_mid, s_right)), h, y_base[h], y_kept[h])

    ez_v[...] = jnp.zeros_like(ez_v)

    def fill_y(ls):
        lines = [fill(l, yi_v, yl_v, yr_v) for l in ls]
        for u, l in enumerate(ls):
            for n in range(CELLS):
                b = wr_v[l, n] * lines[u][n] - lz_v[l, n] + ez_v[n]
                ez_v[n] = b * zt_v[l, n]
                zi_v[l, n] = b * zi_v[l, n]

    for h in halves:
        chip_faces(h)
        looped(8, 2, fill_y, 8 * h)

    for halo in halos:
        halo.wait_send()
    for copy in [pm_copy] + pr_copies:
        copy.wait_send()
    sent = [(xm_recv, 2, nx), (ym_recv, 6, chips)]
    for h in halves:
        sent += [(xr_recv.at[h], 3 + h, nx), (yr_recv.at[h], 9 + h, chips)]
    for ref, n, count in sent:
        part = ref.at[pl.ds(0, count - 1)]
        pltpu.make_async_copy(part, part, send_sem.at[n]).wait()


def layers_kernel(zi_v, zt_v, out, tmp_v, out_v, ez_v, out_sem):
    layers = zi_v.shape[0]
    group = 4
    ez_v[...] = jnp.zeros_like(ez_v)
    for l0 in range(layers - group, -1, -group):
        for l in range(l0 + group - 1, l0 - 1, -1):
            for k in range(CELLS):
                s = zi_v[l, k] + zt_v[l, k] * ez_v[k]
                ez_v[k] = s
                tmp_v[l - l0, pl.ds(k, RUNS, stride=CELLS), :] = s
        for l in range(l0 + group - 1, l0 - 1, -1):
            rows = tmp_v[l - l0].T.reshape(CELLS, RUNS, 128)
            for n in range(CELLS):
                out_v[l, pl.ds(n, RUNS, stride=CELLS), :] = rows[n]
        part = pl.ds(l0, group)
        pltpu.make_async_copy(out_v.at[part], out.at[part], out_sem).start()
    pltpu.make_async_copy(out_v, out_v, out_sem).wait()


def body(*args):
    layers, cells_x, cells_y = args[0].shape
    nx, ny = lax.axis_size("gx"), lax.axis_size("gy")
    f32, i32 = jnp.float32, jnp.int32
    tile = pltpu.VMEM((layers, TILE, 128), f32)
    runs = pltpu.VMEM((layers, CELLS, RUNS, 128), f32)
    index = pltpu.VMEM((layers, CELLS, RUNS, 128), i32)
    layer = pltpu.VMEM((CELLS, RUNS, 128), f32)
    halo = pltpu.VMEM((2, layers, 128), f32)

    def rows(*shape):
        return pltpu.VMEM((*shape, 128), f32)

    hbm = pl.BlockSpec(memory_space=pltpu.HBM)
    smem = pl.BlockSpec(memory_space=pltpu.SMEM)
    vmem = pl.BlockSpec(memory_space=pltpu.VMEM)
    shape = pltpu.VMEM((layers, CELLS, RUNS, 128), f32)
    zi, zt = pl.pallas_call(
        runs_kernel,
        out_shape=(shape, shape),
        in_specs=[hbm, hbm, hbm, smem, smem, hbm, hbm, smem, hbm, smem],
        out_specs=(vmem, vmem),
        scratch_shapes=[
            runs,
            runs,
            index,
            index,
            pltpu.VMEM((CELLS, RUNS, 128), i32),
            index,
            runs,
            runs,
            runs,
            runs,
            tile,
            tile,
            tile,
            tile,
            runs,
            runs,
            runs,
            runs,
            runs,
            runs,
            runs,
            layer,
            layer,
            layer,
            layer,
            layer,
            halo,
            halo,
            halo,
            halo,
            *[rows(RUNS * layers)] * 5,
            rows(3 * layers),
            rows(nx, 3 * layers),
            rows(2, layers),
            rows(2, nx, layers),
            rows(nx + 1, layers),
            rows(3 * layers),
            rows(3 * layers),
            rows(3 * layers),
            rows(ny // 2, 3 * layers),
            rows(2, layers),
            rows(2, layers),
            rows(2, layers),
            rows(2, ny // 2, layers),
            rows(ny // 2 + 1, layers),
            pltpu.SemaphoreType.DMA((6,)),
            pltpu.SemaphoreType.DMA((11,)),
            pltpu.SemaphoreType.DMA((11,)),
        ],
        compiler_params=pltpu.CompilerParams(
            collective_id=0, has_side_effects=True, vmem_limit_bytes=56 * 1024 * 1024
        ),
        cost_estimate=pl.CostEstimate(
            flops=100 * args[0].size, bytes_accessed=28 * args[0].size, transcendentals=0
        ),
        name="lines_xy",
    )(*args)
    return pl.pallas_call(
        layers_kernel,
        out_shape=jax.ShapeDtypeStruct(args[0].shape, f32),
        in_specs=[vmem, vmem],
        out_specs=hbm,
        scratch_shapes=[
            pltpu.VMEM((4, TILE, 128), f32),
            tile,
            layer,
            pltpu.SemaphoreType.DMA,
        ],
        compiler_params=pltpu.CompilerParams(vmem_limit_bytes=32 * 1024 * 1024),
        cost_estimate=pl.CostEstimate(
            flops=2 * args[0].size, bytes_accessed=12 * args[0].size, transcendentals=0
        ),
        name="columns_z",
    )(zi, zt)


def solution(mesh):
    field = P(None, "gx", "gy")
    in_specs = (field, field, field, P(), P(), field, P("gx", "gy"), P(), field, P())
    return jax.shard_map(body, mesh=mesh, in_specs=in_specs, out_specs=field, check_vma=False)
```
